512 devices in a mesh: chips: 32 (over z, y_lo, core), samples: 16 (over y_hi, x).
Axes of the slice: x: 4, y: 8 (y_hi: 4, y_lo: 2; y = y_hi * 2 + y_lo), z: 8, core: 2. Of those that a mesh axis runs over, the one named last changes fastest.
Arguments:
- telemetry: bfloat16 [73728, 16384], P('chips', 'samples'), may hold values from 0 to 100, as said below
- chip_factors: float32 [64, 73728], P(None, ('chips', 'samples')), may hold values from 0.03 to 0.3
- sample_factors: float32 [64, 16384], P(None, ('samples', 'chips')), may hold values from 0.03 to 0.3
Outputs:
- chip_updated: float32 [64, 73728], P(None, ('chips', 'samples'))
- sample_updated: float32 [64, 16384], P(None, ('samples', 'chips'))
- relative_error: float32 [], replicated
The draws below stay inside these ranges and needn't reach their ends.
Inputs may be any that keep to these rules, and one draw needn't show every extreme that they name: `telemetry`: nonnegative readings.
All inputs are finite; a program needn't handle non-finite values.
Results may differ from the reference program's by a relative error of at most 0.00035.
Values may be sent and summed in bfloat16 or wider, within the bound.
No kernel may reach another device: no remote copies, remote signals or barrier semaphores. Data moves between devices by JAX's collectives and lax.ppermute only.
A program may use at most 64 MiB of HBM per device.

```python
import math
import jax
import jax.numpy as jnp
from jax import lax

K = 64
RC = 2304
ITERS = 2
ROWS = 73728
COLS = 16384
N_CHIPS = 32


def draw_telemetry(key, part):
    key = jax.random.fold_in(key, 11)
    key_rows, key_cols, key_base = jax.random.split(key, 3)
    row_pos = jnp.arange(ROWS, dtype=jnp.float32) / ROWS
    col_pos = jnp.arange(COLS, dtype=jnp.float32) / COLS
    row_scale = jnp.exp(jax.random.uniform(key_rows, (ROWS,), jnp.float32, -1.15, 1.15)) * 3.0 ** (row_pos - 0.5)
    col_scale = jnp.exp(jax.random.uniform(key_cols, (COLS,), jnp.float32, -1.15, 1.15)) * 3.0 ** (col_pos - 0.5)
    uniform_base = jax.random.uniform(key_base, (ROWS, COLS), jnp.float32)
    spread = 0.5 * (row_pos[:, None] + col_pos[None, :])
    level = 0.1 * 10.0 ** spread
    base = 1.0 + level * (2.0 * uniform_base - 1.0)
    return (row_scale[:, None] * col_scale[None, :] * base).astype(jnp.bfloat16)


def shard_levels(own_key, shape, cuts, least, top_value):
    def one(dim, shards_of):
        heights = jax.random.uniform(jax.random.fold_in(jax.random.fold_in(own_key, 6), dim), (shards_of,), jnp.float32, least / len(cuts), top_value / len(cuts))
        return jnp.repeat(jnp.exp(heights), shape[dim] // shards_of).reshape((-1,) + (1,) * (len(shape) - dim - 1))

    factor_of = one(*cuts[0])
    for cut in cuts[1:]:
        factor_of = factor_of * one(*cut)
    return factor_of


def setup_inputs(seed: int = 0) -> dict:
    seeds = jax.random.split(jax.random.key(seed), 4)
    telemetry = draw_telemetry(jax.random.fold_in(seeds[3], 71), 0)
    chip_factors = jnp.clip(jnp.exp(math.log(0.3) - 2.3025852 * jax.random.uniform(seeds[1], (K, ROWS), jnp.float32) ** shard_levels(seeds[1], (K, ROWS), ((1, 512),), -0.2, 0.2)), 0.03, 0.3)
    sample_factors = jnp.clip(jnp.exp(math.log(0.3) - 2.3025852 * jax.random.uniform(seeds[2], (K, COLS), jnp.float32) ** shard_levels(seeds[2], (K, COLS), ((1, 512),), -0.2, 0.2)), 0.03, 0.3)
    return dict(telemetry=telemetry, chip_factors=chip_factors, sample_factors=sample_factors)


epsilon = 1e-09

def reference(telemetry, chip_factors, sample_factors):
    highest = lax.Precision.HIGHEST
    chips_now = chip_factors
    samples_now = sample_factors
    for sweep in range(ITERS):
        chips_bf = chips_now.astype(jnp.bfloat16)
        numer_h = jnp.dot(chips_bf, telemetry, preferred_element_type=jnp.float32)
        gram_chip = jnp.dot(chips_now, chips_now.T, precision=highest)
        samples_now = samples_now * numer_h / (jnp.dot(gram_chip, samples_now, precision=highest) + epsilon)
        samples_bf = samples_now.astype(jnp.bfloat16)
        numer_w = lax.dot_general(samples_bf, telemetry, (((1,), (1,)), ((), ())), preferred_element_type=jnp.float32)
        gram_sample = jnp.dot(samples_now, samples_now.T, precision=highest)
        chips_now = chips_now * numer_w / (jnp.dot(gram_sample, chips_now, precision=highest) + epsilon)
    chips_bf = chips_now.astype(jnp.bfloat16)
    samples_bf = samples_now.astype(jnp.bfloat16)
    blocks = N_CHIPS
    chip_blocks = jnp.moveaxis(chips_bf.reshape(K, blocks, RC), 1, 0)
    tel_blocks = telemetry.reshape(blocks, RC, COLS)

    def block_error(pair):
        factor_blk, rows_blk = pair
        rebuilt = lax.dot_general(factor_blk, samples_bf, (((0,), (0,)), ((), ())), preferred_element_type=jnp.float32)
        values = rows_blk.astype(jnp.float32)
        difference = values - rebuilt
        return (jnp.sum(difference * difference), jnp.sum(values * values))
    errors, energies = lax.map(block_error, (chip_blocks, tel_blocks))
    relative_error = jnp.sqrt(jnp.sum(errors) / jnp.sum(energies))
    return (chips_now, samples_now, relative_error)
```

```python
import jax
import jax.numpy as jnp
from jax import lax
from jax.experimental import pallas as pl
from jax.experimental.pallas import tpu as pltpu
from jax.sharding import PartitionSpec as P

ITERS = 2

epsilon = 1e-09

F32 = jnp.float32
BF16 = jnp.bfloat16
HIGHEST = lax.Precision.HIGHEST

K = 64
CHIPS = 32
SAMPLES = 16
ROWS = 2304
COLS = 1024
W_OWN = ROWS // SAMPLES
H_OWN = COLS // CHIPS
GRAM = 32
W_HALF = 80
W_MSG = W_HALF + GRAM
H_RED = H_OWN + GRAM
W_RED = W_OWN + GRAM


def split(x):
    high = x.astype(BF16).astype(F32)
    return jnp.concatenate([high, x - high], axis=1).astype(BF16)


def join(x):
    return x[:, :K] + x[:, K:]


def squares():
    row = lax.broadcasted_iota(jnp.int32, (32, 32), 0)
    col = lax.broadcasted_iota(jnp.int32, (32, 32), 1)
    return row, col


def pack_parts(upper, block, lower_diag, row, col):
    high = upper.astype(BF16).astype(F32)
    low = upper - high
    block_high = block.astype(BF16).astype(F32)
    own = row == col
    return jnp.concatenate(
        [jnp.where(own, upper, high), block_high, jnp.where(own, lower_diag, low), block - block_high],
        axis=1,
    ).astype(BF16)


def pack_gram(gram):
    row, col = squares()
    first, block, last = gram[:32, :32], gram[:32, 32:], gram[32:, 32:]
    return pack_parts(jnp.where(row <= col, first, last), block, last, row, col)


def repack_gram(total):
    row, col = squares()
    own = row == col
    first, third = total[:, :32], total[:, 64:96]
    upper = jnp.where(own, first, first + third)
    return pack_parts(upper, total[:, 32:64] + total[:, 96:], third, row, col)


def unpack_gram(total):
    row, col = squares()
    first, third = total[:, :32], total[:, 64:96]
    mixed = first + third
    block = total[:, 32:64] + total[:, 96:]
    eye = (row == col).astype(F32)
    turned = lax.dot_general(
        eye,
        jnp.concatenate([mixed, block], axis=0),
        (((1,), (1,)), ((), ())),
        precision=HIGHEST,
        preferred_element_type=F32,
    )
    mixed_t, block_t = turned[:, :32], turned[:, 32:]
    one = jnp.where(row < col, mixed, jnp.where(row > col, mixed_t, first))
    two = jnp.where(row > col, mixed, jnp.where(row < col, mixed_t, third))
    return jnp.concatenate(
        [jnp.concatenate([one, block], axis=1), jnp.concatenate([block_t, two], axis=1)], axis=0
    )


def gram_of(halves):
    four = lax.dot_general(
        halves, halves, (((0,), (0,)), ((), ())), preferred_element_type=F32
    )
    two = four[:K] + four[K:]
    return two[:, :K] + two[:, K:]


def fill_w(w, out):
    tail = jnp.concatenate([w[W_HALF:], jnp.zeros((2 * W_HALF - W_OWN, K), F32)], axis=0)
    rows = jnp.concatenate([w[:W_HALF], tail], axis=1).astype(BF16)
    gram = pack_gram(gram_of(split(w)))
    for i in range(SAMPLES):
        out[i, :W_HALF, :] = rows
        out[i, W_HALF:, :] = gram


def own_rows(ref, i):
    both = ref[i, :W_HALF, :].astype(F32)
    return jnp.concatenate([both[:, :K], both[: W_OWN - W_HALF, K:]], axis=0)


def start_kernel(w, out):
    fill_w(w[...], out)


def h_numer_kernel(got, tel, out, w_all, w_turned):
    total = jnp.zeros((GRAM, 128), F32)
    for i in range(SAMPLES):
        w_all[i * W_OWN : (i + 1) * W_OWN, :] = own_rows(got, i)
        total += got[i, W_HALF:, :].astype(F32)
    gram = repack_gram(total)
    for j in range(ROWS // 128):
        w_turned[:, j * 128 : (j + 1) * 128] = w_all[j * 128 : (j + 1) * 128, :].T.astype(BF16)
    width = 256
    per = width // H_OWN

    def step(n, carry):
        cols = pl.ds(pl.multiple_of(n * width, width), width)
        part = jnp.dot(w_turned[...], tel[:, cols], preferred_element_type=F32).T
        for q in range(per):
            out[n * per + q, :H_OWN, :] = split(part[q * H_OWN : (q + 1) * H_OWN])
            out[n * per + q, H_OWN:, :] = gram
        return carry

    lax.fori_loop(0, COLS // width, step, 0)


def h_update_kernel(got, h, h_out, out):
    total = jnp.zeros((H_RED, 128), F32)
    for i in range(CHIPS):
        total += got[i].astype(F32)
    gram = unpack_gram(total[H_OWN:])
    old = h[...]
    below = jnp.dot(old, gram, precision=HIGHEST, preferred_element_type=F32) + epsilon
    new = old * join(total[:H_OWN]) / below
    h_out[...] = new
    halves = split(new)
    for i in range(CHIPS):
        out[i] = halves


def w_numer_kernel(got, tel, out):
    halves = got[...].reshape(COLS, 128)
    gram = pack_gram(gram_of(halves))
    high = halves[:, :K]
    per = 4
    block = per * W_OWN

    def step(b, carry):
        rows = pl.ds(pl.multiple_of(b * block, block), block)
        part = jnp.dot(tel[rows, :], high, preferred_element_type=F32)
        for q in range(per):
            out[b * per + q, :W_OWN, :] = split(part[q * W_OWN : (q + 1) * W_OWN])
            out[b * per + q, W_OWN:, :] = gram
        return carry

    lax.fori_loop(0, ROWS // block, step, 0)


def w_update_kernel(got, w, w_out, out):
    total = jnp.zeros((W_RED, 128), F32)
    for i in range(SAMPLES):
        total += got[i].astype(F32)
    gram = unpack_gram(total[W_OWN:])
    old = w[...]
    below = jnp.dot(old, gram, precision=HIGHEST, preferred_element_type=F32) + epsilon
    new = old * join(total[:W_OWN]) / below
    w_out[...] = new
    fill_w(new, out)


def error_kernel(got_w, got_h, tel, out):
    high = got_h[...].reshape(COLS, 128)[:, :K]

    def step(i, carry):
        error, energy = carry
        rows = pl.ds(pl.multiple_of(i * W_OWN, W_OWN), W_OWN)
        rebuilt = lax.dot_general(
            own_rows(got_w, i).astype(BF16),
            high,
            (((1,), (1,)), ((), ())),
            preferred_element_type=F32,
        )
        values = tel[rows, :].astype(F32)
        difference = values - rebuilt
        error += jnp.sum((difference * difference).reshape(W_OWN // 8, 8, COLS), axis=0)
        energy += jnp.sum((values * values).reshape(W_OWN // 8, 8, COLS), axis=0)
        return error, energy

    zero = jnp.zeros((8, COLS), F32)
    error, energy = lax.fori_loop(0, SAMPLES, step, (zero, zero))
    lane = lax.broadcasted_iota(jnp.int32, (8, 128), 1)
    pair = jnp.where(lane < K, jnp.sum(error), jnp.sum(energy))
    for i in range(SAMPLES):
        out[i] = pair


VMEM = pl.BlockSpec(memory_space=pltpu.VMEM)


def call(kernel, inputs, outs, scratch=(), cost=(0, 0)):
    return pl.pallas_call(
        kernel,
        out_shape=[jax.ShapeDtypeStruct(shape, dtype) for shape, dtype in outs],
        in_specs=[VMEM] * len(inputs),
        out_specs=[VMEM] * len(outs),
        scratch_shapes=list(scratch),
        compiler_params=pltpu.CompilerParams(vmem_limit_bytes=32 * 1024 * 1024),
        cost_estimate=pl.CostEstimate(flops=cost[0], bytes_accessed=cost[1], transcendentals=0),
    )(*inputs)


def exchange(x, axis):
    return lax.all_to_all(x, axis, 0, 0, tiled=True)


def body(telemetry, chip_factors, sample_factors):
    w, h = chip_factors.T, sample_factors.T
    product = (2 * K * ROWS * COLS, ROWS * COLS * 2)
    (sent,) = call(start_kernel, (w,), [((SAMPLES, W_MSG, 128), BF16)])
    got_w = exchange(sent, "samples")
    for sweep in range(ITERS):
        (sent,) = call(
            h_numer_kernel,
            (got_w, telemetry),
            [((CHIPS, H_RED, 128), BF16)],
            (pltpu.VMEM((ROWS, K), F32), pltpu.VMEM((K, ROWS), BF16)),
            product,
        )
        got = exchange(sent, "chips")
        h, sent = call(
            h_update_kernel, (got, h), [((H_OWN, K), F32), ((CHIPS, H_OWN, 128), BF16)]
        )
        got_h = exchange(sent, "chips")
        (sent,) = call(
            w_numer_kernel, (got_h, telemetry), [((SAMPLES, W_RED, 128), BF16)], (), product
        )
        got = exchange(sent, "samples")
        w, sent = call(
            w_update_kernel, (got, w), [((W_OWN, K), F32), ((SAMPLES, W_MSG, 128), BF16)]
        )
        got_w = exchange(sent, "samples")
    (pair,) = call(
        error_kernel, (got_w, got_h, telemetry), [((SAMPLES, 8, 128), F32)], (), product
    )
    pair = jnp.sum(exchange(pair, "samples"), axis=0)
    pair = exchange(jnp.broadcast_to(pair[None], (CHIPS, 8, 128)), "chips")
    pair = jnp.sum(pair, axis=0)
    return w.T, h.T, jnp.sqrt(pair[0, 0] / pair[0, K])


def solution(mesh):
    return jax.shard_map(
        body,
        mesh=mesh,
        in_specs=(
            P("chips", "samples"),
            P(None, ("chips", "samples")),
            P(None, ("samples", "chips")),
        ),
        out_specs=(P(None, ("chips", "samples")), P(None, ("samples", "chips")), P()),
        check_vma=False,
    )
```

```python
import jax
import jax.numpy as jnp
from jax import lax
from jax.experimental import pallas as pl
from jax.experimental.pallas import tpu as pltpu
from jax.sharding import Mesh
from jax.sharding import PartitionSpec as P

ITERS = 2

epsilon = 1e-09

F32 = jnp.float32
BF16 = jnp.bfloat16
HIGHEST = lax.Precision.HIGHEST

K = 64
CHIPS = 32
PAIRS = CHIPS // 2
SAMPLES = 16
ROWS = 2304
COLS = 1024
W_OWN = ROWS // SAMPLES
H_OWN = COLS // CHIPS
H_WIDTH = 256
GRAM = 32
W_HALF = 80
W_MSG = W_HALF + GRAM
H_RED = H_OWN + GRAM
W_RED = W_OWN + GRAM


def split(x):
    high = x.astype(BF16).astype(F32)
    return jnp.concatenate([high, x - high], axis=1).astype(BF16)


def join(x):
    return x[:, :K] + x[:, K:]


def squares():
    row = lax.broadcasted_iota(jnp.int32, (32, 32), 0)
    col = lax.broadcasted_iota(jnp.int32, (32, 32), 1)
    return row, col


def pack_parts(upper, block, lower_diag, row, col):
    high = upper.astype(BF16).astype(F32)
    low = upper - high
    block_high = block.astype(BF16).astype(F32)
    own = row == col
    return jnp.concatenate(
        [jnp.where(own, upper, high), block_high, jnp.where(own, lower_diag, low), block - block_high],
        axis=1,
    ).astype(BF16)


def pack_gram(gram):
    row, col = squares()
    first, block, last = gram[:32, :32], gram[:32, 32:], gram[32:, 32:]
    return pack_parts(jnp.where(row <= col, first, last), block, last, row, col)


def repack_gram(total):
    row, col = squares()
    own = row == col
    first, third = total[:, :32], total[:, 64:96]
    upper = jnp.where(own, first, first + third)
    return pack_parts(upper, total[:, 32:64] + total[:, 96:], third, row, col)


def unpack_gram(total):
    row, col = squares()
    first, third = total[:, :32], total[:, 64:96]
    mixed = first + third
    block = total[:, 32:64] + total[:, 96:]
    eye = (row == col).astype(F32)
    turned = lax.dot_general(
        eye,
        jnp.concatenate([mixed, block], axis=0),
        (((1,), (1,)), ((), ())),
        precision=HIGHEST,
        preferred_element_type=F32,
    )
    mixed_t, block_t = turned[:, :32], turned[:, 32:]
    one = jnp.where(row < col, mixed, jnp.where(row > col, mixed_t, first))
    two = jnp.where(row > col, mixed, jnp.where(row < col, mixed_t, third))
    return jnp.concatenate(
        [jnp.concatenate([one, block], axis=1), jnp.concatenate([block_t, two], axis=1)], axis=0
    )


def gram_of(halves):
    four = lax.dot_general(
        halves, halves, (((0,), (0,)), ((), ())), preferred_element_type=F32
    )
    two = four[:K] + four[K:]
    return two[:, :K] + two[:, K:]


def fill_w(w, out):
    tail = jnp.concatenate([w[W_HALF:], jnp.zeros((2 * W_HALF - W_OWN, K), F32)], axis=0)
    rows = jnp.concatenate([w[:W_HALF], tail], axis=1).astype(BF16)
    for i in range(SAMPLES):
        out[i, :W_HALF, :] = rows
    if out.shape[1] > W_HALF:
        gram = pack_gram(gram_of(split(w)))
        for i in range(SAMPLES):
            out[i, W_HALF:, :] = gram


def own_rows(ref, i):
    both = ref[i, :W_HALF, :].astype(F32)
    return jnp.concatenate([both[:, :K], both[: W_OWN - W_HALF, K:]], axis=0)


def start_kernel(w, out):
    fill_w(w[...], out)


def h_numer_kernel(core, got, tel, keep, give, w_turned, w_all, gram):
    step = pl.program_id(0)

    @pl.when(step == 0)
    def _():
        total = jnp.zeros((GRAM, 128), F32)
        for i in range(SAMPLES):
            w_all[i * W_OWN : (i + 1) * W_OWN, :] = own_rows(got, i)
            total += got[i, W_HALF:, :].astype(F32)
        gram[...] = repack_gram(total)
        for j in range(ROWS // 128):
            w_turned[:, j * 128 : (j + 1) * 128] = w_all[j * 128 : (j + 1) * 128, :].T.astype(BF16)

    part = jnp.dot(w_turned[...], tel[...], preferred_element_type=F32).T
    first = core[0] == 0
    for q in range(H_WIDTH // (2 * H_OWN)):
        even = part[2 * q * H_OWN : (2 * q + 1) * H_OWN]
        odd = part[(2 * q + 1) * H_OWN : (2 * q + 2) * H_OWN]
        keep[q, :H_OWN, :] = split(jnp.where(first, even, odd))
        give[q, :H_OWN, :] = split(jnp.where(first, odd, even))
        keep[q, H_OWN:, :] = gram[...]
        give[q, H_OWN:, :] = gram[...]


def pair_kernel(keep, got, out):
    gram = repack_gram(keep[0, H_OWN:, :].astype(F32) + got[0, H_OWN:, :].astype(F32))
    for i in range(PAIRS):
        total = keep[i, :H_OWN, :].astype(F32) + got[i, :H_OWN, :].astype(F32)
        out[i, :H_OWN, :] = split(join(total))
        out[i, H_OWN:, :] = gram


def h_update_kernel(got, h, h_out, out):
    total = jnp.zeros((H_RED, 128), F32)
    for i in range(PAIRS):
        total += got[i].astype(F32)
    gram = unpack_gram(total[H_OWN:])
    old = h[...]
    below = jnp.dot(old, gram, precision=HIGHEST, preferred_element_type=F32) + epsilon
    new = old * join(total[:H_OWN]) / below
    h_out[...] = new
    halves = split(new)
    for i in range(CHIPS):
        out[i] = halves


def w_numer_kernel(got, tel, out):
    halves = got[...].reshape(COLS, 128)
    gram = pack_gram(gram_of(halves))
    high = halves[:, :K]
    per = 4
    block = per * W_OWN

    def step(b, carry):
        rows = pl.ds(pl.multiple_of(b * block, block), block)
        part = jnp.dot(tel[rows, :], high, preferred_element_type=F32)
        for q in range(per):
            out[b * per + q, :W_OWN, :] = split(part[q * W_OWN : (q + 1) * W_OWN])
            out[b * per + q, W_OWN:, :] = gram
        return carry

    lax.fori_loop(0, ROWS // block, step, 0)


def w_update_kernel(got, w, w_out, out):
    total = jnp.zeros((W_RED, 128), F32)
    for i in range(SAMPLES):
        total += got[i].astype(F32)
    gram = unpack_gram(total[W_OWN:])
    old = w[...]
    below = jnp.dot(old, gram, precision=HIGHEST, preferred_element_type=F32) + epsilon
    new = old * join(total[:W_OWN]) / below
    w_out[...] = new
    fill_w(new, out)


def error_kernel(got_w, got_h, tel, out):
    high = got_h[...].reshape(COLS, 128)[:, :K]

    def step(i, carry):
        error, energy = carry
        rows = pl.ds(pl.multiple_of(i * W_OWN, W_OWN), W_OWN)
        rebuilt = lax.dot_general(
            own_rows(got_w, i).astype(BF16),
            high,
            (((1,), (1,)), ((), ())),
            preferred_element_type=F32,
        )
        values = tel[rows, :].astype(F32)
        difference = values - rebuilt
        error += jnp.sum((difference * difference).reshape(W_OWN // 8, 8, COLS), axis=0)
        energy += jnp.sum((values * values).reshape(W_OWN // 8, 8, COLS), axis=0)
        return error, energy

    zero = jnp.zeros((8, COLS), F32)
    error, energy = lax.fori_loop(0, SAMPLES, step, (zero, zero))
    lane = lax.broadcasted_iota(jnp.int32, (8, 128), 1)
    pair = jnp.where(lane < K, jnp.sum(error), jnp.sum(energy))
    for i in range(SAMPLES):
        out[i] = pair


VMEM = pl.BlockSpec(memory_space=pltpu.VMEM)
LIMIT = pltpu.CompilerParams(vmem_limit_bytes=32 * 1024 * 1024)
PRODUCT = pl.CostEstimate(
    flops=2 * K * ROWS * COLS, bytes_accessed=2 * ROWS * COLS, transcendentals=0
)


def call(kernel, inputs, outs, cost=None):
    return pl.pallas_call(
        kernel,
        out_shape=[jax.ShapeDtypeStruct(shape, dtype) for shape, dtype in outs],
        in_specs=[VMEM] * len(inputs),
        out_specs=[VMEM] * len(outs),
        compiler_params=LIMIT,
        cost_estimate=cost,
    )(*inputs)


def h_numer(core, got_w, telemetry):
    per = H_WIDTH // (2 * H_OWN)
    piece = pl.BlockSpec((per, H_RED, 128), lambda n: (n, 0, 0))
    message = jax.ShapeDtypeStruct((PAIRS, H_RED, 128), BF16)
    return pl.pallas_call(
        h_numer_kernel,
        grid=(COLS // H_WIDTH,),
        out_shape=[message, message],
        in_specs=[
            pl.BlockSpec(memory_space=pltpu.SMEM),
            pl.BlockSpec(got_w.shape, lambda n: (0, 0, 0)),
            pl.BlockSpec((ROWS, H_WIDTH), lambda n: (0, n)),
        ],
        out_specs=[piece, piece],
        scratch_shapes=[
            pltpu.VMEM((K, ROWS), BF16),
            pltpu.VMEM((ROWS, K), F32),
            pltpu.VMEM((GRAM, 128), BF16),
        ],
        compiler_params=LIMIT,
        cost_estimate=PRODUCT,
    )(core, got_w, telemetry)


def exchange(x, axis):
    return lax.all_to_all(x, axis, 0, 0, tiled=True)


def body(telemetry, chip_factors, sample_factors):
    core = lax.axis_index("core").reshape(1)
    w, h = chip_factors.T, sample_factors.T
    (sent,) = call(start_kernel, (w,), [((SAMPLES, W_MSG, 128), BF16)])
    got_w = exchange(sent, "samples")
    for sweep in range(ITERS):
        keep, give = h_numer(core, got_w, telemetry)
        taken = lax.ppermute(give, "core", [(0, 1), (1, 0)])
        (sent,) = call(pair_kernel, (keep, taken), [((PAIRS, H_RED, 128), BF16)])
        got = exchange(sent, "pairs")
        h, sent = call(
            h_update_kernel, (got, h), [((H_OWN, K), F32), ((CHIPS, H_OWN, 128), BF16)]
        )
        got_h = exchange(sent, ("pairs", "core"))
        (sent,) = call(
            w_numer_kernel, (got_h, telemetry), [((SAMPLES, W_RED, 128), BF16)], PRODUCT
        )
        got = exchange(sent, "samples")
        rows = W_MSG if sweep < ITERS - 1 else W_HALF
        w, sent = call(
            w_update_kernel, (got, w), [((W_OWN, K), F32), ((SAMPLES, rows, 128), BF16)]
        )
        got_w = exchange(sent, "samples")
    (pair,) = call(
        error_kernel, (got_w, got_h, telemetry), [((SAMPLES, 8, 128), F32)], PRODUCT
    )
    pair = jnp.sum(exchange(pair, "samples"), axis=0)
    pair = exchange(jnp.broadcast_to(pair[None], (CHIPS, 8, 128)), ("pairs", "core"))
    pair = jnp.sum(pair, axis=0)
    return w.T, h.T, jnp.sqrt(pair[0, 0] / pair[0, K])


def solution(mesh):
    split_mesh = Mesh(mesh.devices.reshape(PAIRS, 2, SAMPLES), ("pairs", "core", "samples"))
    chips = ("pairs", "core")
    return jax.shard_map(
        body,
        mesh=split_mesh,
        in_specs=(
            P(chips, "samples"),
            P(None, (*chips, "samples")),
            P(None, ("samples", *chips)),
        ),
        out_specs=(P(None, (*chips, "samples")), P(None, ("samples", *chips)), P()),
        check_vma=False,
    )
```

```python
import jax
import jax.numpy as jnp
from jax import lax
from jax.experimental import pallas as pl
from jax.experimental.pallas import tpu as pltpu
from jax.sharding import Mesh
from jax.sharding import PartitionSpec as P

ITERS = 2

epsilon = 1e-09

F32 = jnp.float32
BF16 = jnp.bfloat16
HIGHEST = lax.Precision.HIGHEST

K = 64
CHIPS = 32
PAIRS = CHIPS // 2
SAMPLES = 16
ROWS = 2304
COLS = 1024
W_OWN = ROWS // SAMPLES
H_OWN = COLS // CHIPS
H_WIDTH = 256
GRAM = 32
W_HALF = 80
W_MSG = W_HALF + GRAM
H_RED = H_OWN + GRAM
W_RED = W_OWN + GRAM


def split(x):
    high = x.astype(BF16).astype(F32)
    return jnp.concatenate([high, x - high], axis=1).astype(BF16)


def join(x):
    return x[:, :K] + x[:, K:]


def squares():
    row = lax.broadcasted_iota(jnp.int32, (32, 32), 0)
    col = lax.broadcasted_iota(jnp.int32, (32, 32), 1)
    return row, col


def pack_parts(upper, block, lower_diag, row, col):
    high = upper.astype(BF16).astype(F32)
    low = upper - high
    block_high = block.astype(BF16).astype(F32)
    own = row == col
    return jnp.concatenate(
        [jnp.where(own, upper, high), block_high, jnp.where(own, lower_diag, low), block - block_high],
        axis=1,
    ).astype(BF16)


def pack_gram(gram):
    row, col = squares()
    first, block, last = gram[:32, :32], gram[:32, 32:], gram[32:, 32:]
    return pack_parts(jnp.where(row <= col, first, last), block, last, row, col)


def repack_gram(total):
    row, col = squares()
    own = row == col
    first, third = total[:, :32], total[:, 64:96]
    upper = jnp.where(own, first, first + third)
    return pack_parts(upper, total[:, 32:64] + total[:, 96:], third, row, col)


def unpack_gram(total):
    row, col = squares()
    first, third = total[:, :32], total[:, 64:96]
    mixed = first + third
    block = total[:, 32:64] + total[:, 96:]
    eye = (row == col).astype(F32)
    turned = lax.dot_general(
        eye,
        jnp.concatenate([mixed, block], axis=0),
        (((1,), (1,)), ((), ())),
        precision=HIGHEST,
        preferred_element_type=F32,
    )
    mixed_t, block_t = turned[:, :32], turned[:, 32:]
    one = jnp.where(row < col, mixed, jnp.where(row > col, mixed_t, first))
    two = jnp.where(row > col, mixed, jnp.where(row < col, mixed_t, third))
    return jnp.concatenate(
        [jnp.concatenate([one, block], axis=1), jnp.concatenate([block_t, two], axis=1)], axis=0
    )


def products(halves):
    return lax.dot_general(halves, halves, (((0,), (0,)), ((), ())), preferred_element_type=F32)


def quarters(four):
    two = four[:K] + four[K:]
    return two[:, :K] + two[:, K:]


def two_halves(w):
    tail = jnp.concatenate([w[W_HALF:], jnp.zeros((2 * W_HALF - W_OWN, K), F32)], axis=0)
    return jnp.concatenate([w[:W_HALF], tail], axis=1).astype(BF16)


def fill_w(w, out):
    rows = two_halves(w)
    gram = pack_gram(quarters(products(split(w))))
    for i in range(SAMPLES):
        out[i, :W_HALF, :] = rows
        out[i, W_HALF:, :] = gram


def own_rows(ref, i):
    both = ref[i, :W_HALF, :].astype(F32)
    return jnp.concatenate([both[:, :K], both[: W_OWN - W_HALF, K:]], axis=0)


def start_kernel(w, out):
    fill_w(w[...], out)


def h_numer_kernel(core, got, tel, keep, give, w_turned, w_all, gram):
    step = pl.program_id(0)

    @pl.when(step == 0)
    def _():
        total = jnp.zeros((GRAM, 128), F32)
        for i in range(SAMPLES):
            w_all[i * W_OWN : (i + 1) * W_OWN, :] = own_rows(got, i)
            total += got[i, W_HALF:, :].astype(F32)
        gram[...] = repack_gram(total)
        for j in range(ROWS // 128):
            w_turned[:, j * 128 : (j + 1) * 128] = w_all[j * 128 : (j + 1) * 128, :].T.astype(BF16)

    part = jnp.dot(w_turned[...], tel[...], preferred_element_type=F32).T
    first = core[0] == 0
    for q in range(H_WIDTH // (2 * H_OWN)):
        even = part[2 * q * H_OWN : (2 * q + 1) * H_OWN]
        odd = part[(2 * q + 1) * H_OWN : (2 * q + 2) * H_OWN]
        keep[q, :H_OWN, :] = split(jnp.where(first, even, odd))
        give[q, :H_OWN, :] = split(jnp.where(first, odd, even))
        keep[q, H_OWN:, :] = gram[...]
        give[q, H_OWN:, :] = gram[...]


def pair_kernel(keep, got, out):
    gram = repack_gram(keep[0, H_OWN:, :].astype(F32) + got[0, H_OWN:, :].astype(F32))
    for i in range(PAIRS):
        total = keep[i, :H_OWN, :].astype(F32) + got[i, :H_OWN, :].astype(F32)
        out[i, :H_OWN, :] = split(join(total))
        out[i, H_OWN:, :] = gram


def h_update_kernel(got, h, h_out, out):
    total = jnp.zeros((H_RED, 128), F32)
    for i in range(PAIRS):
        total += got[i].astype(F32)
    gram = unpack_gram(total[H_OWN:])
    old = h[...]
    below = jnp.dot(old, gram, precision=HIGHEST, preferred_element_type=F32) + epsilon
    new = old * join(total[:H_OWN]) / below
    h_out[...] = new
    halves = split(new)
    for i in range(CHIPS):
        out[i] = halves


def w_numer_kernel(got, tel, out):
    halves = got[...].reshape(COLS, 128)
    four = products(halves)
    gram = pack_gram(quarters(four))
    if out.shape[1] > W_RED:
        gram = jnp.concatenate([gram, pack_gram(four[:K, :K])], axis=0)
    high = halves[:, :K]
    per = 4
    block = per * W_OWN

    def step(b, carry):
        rows = pl.ds(pl.multiple_of(b * block, block), block)
        part = jnp.dot(tel[rows, :], high, preferred_element_type=F32)
        for q in range(per):
            out[b * per + q, :W_OWN, :] = split(part[q * W_OWN : (q + 1) * W_OWN])
            out[b * per + q, W_OWN:, :] = gram
        return carry

    lax.fori_loop(0, ROWS // block, step, 0)


def w_new(got, w):
    total = jnp.zeros(got.shape[1:], F32)
    for i in range(SAMPLES):
        total += got[i].astype(F32)
    numer = join(total[:W_OWN])
    gram = unpack_gram(total[W_OWN:W_RED])
    old = w[...]
    below = jnp.dot(old, gram, precision=HIGHEST, preferred_element_type=F32) + epsilon
    return old * numer / below, numer, total[W_RED:]


def w_update_kernel(got, w, w_out, out):
    new, _, _ = w_new(got, w)
    w_out[...] = new
    fill_w(new, out)


def tile_pair(left, right):
    lane = lax.broadcasted_iota(jnp.int32, (8, 128), 1)
    return jnp.where(lane < K, left, right)


def w_last_kernel(got, w, energy, w_out, out):
    new, numer, rest = w_new(got, w)
    w_out[...] = new
    rounded = new.astype(BF16).astype(F32)
    gram = unpack_gram(rest)
    fitted = jnp.dot(rounded, gram, precision=HIGHEST, preferred_element_type=F32)
    share = jnp.sum(rounded * (fitted - 2.0 * numer))
    pair = tile_pair(share, energy[...])
    for i in range(SAMPLES):
        out[i] = pair


def energy_kernel(tel, out):
    def step(i, energy):
        rows = pl.ds(pl.multiple_of(i * W_OWN, W_OWN), W_OWN)
        values = tel[rows, :].astype(F32)
        return energy + jnp.sum((values * values).reshape(W_OWN // 8, 8, COLS), axis=0)

    energy = lax.fori_loop(0, SAMPLES, step, jnp.zeros((8, COLS), F32))
    out[...] = jnp.full((8, 128), jnp.sum(energy), F32)


def last_rows_kernel(w, out):
    rows = two_halves(w[...])
    for i in range(SAMPLES):
        out[i] = rows


def error_kernel(got_w, got_h, tel, out):
    high = got_h[...].reshape(COLS, 128)[:, :K]

    def step(i, error):
        rows = pl.ds(pl.multiple_of(i * W_OWN, W_OWN), W_OWN)
        rebuilt = lax.dot_general(
            own_rows(got_w, i).astype(BF16),
            high,
            (((1,), (1,)), ((), ())),
            preferred_element_type=F32,
        )
        difference = tel[rows, :].astype(F32) - rebuilt
        return error + jnp.sum((difference * difference).reshape(W_OWN // 8, 8, COLS), axis=0)

    error = lax.fori_loop(0, SAMPLES, step, jnp.zeros((8, COLS), F32))
    share = jnp.full((8, 128), jnp.sum(error), F32)
    for i in range(SAMPLES):
        out[i] = share


VMEM = pl.BlockSpec(memory_space=pltpu.VMEM)
LIMIT = pltpu.CompilerParams(vmem_limit_bytes=32 * 1024 * 1024)
PRODUCT = pl.CostEstimate(
    flops=2 * K * ROWS * COLS, bytes_accessed=2 * ROWS * COLS, transcendentals=0
)


def call(kernel, inputs, outs, cost=None):
    return pl.pallas_call(
        kernel,
        out_shape=[jax.ShapeDtypeStruct(shape, dtype) for shape, dtype in outs],
        in_specs=[VMEM] * len(inputs),
        out_specs=[VMEM] * len(outs),
        compiler_params=LIMIT,
        cost_estimate=cost,
    )(*inputs)


def h_numer(core, got_w, telemetry):
    per = H_WIDTH // (2 * H_OWN)
    piece = pl.BlockSpec((per, H_RED, 128), lambda n: (n, 0, 0))
    message = jax.ShapeDtypeStruct((PAIRS, H_RED, 128), BF16)
    return pl.pallas_call(
        h_numer_kernel,
        grid=(COLS // H_WIDTH,),
        out_shape=[message, message],
        in_specs=[
            pl.BlockSpec(memory_space=pltpu.SMEM),
            pl.BlockSpec(got_w.shape, lambda n: (0, 0, 0)),
            pl.BlockSpec((ROWS, H_WIDTH), lambda n: (0, n)),
        ],
        out_specs=[piece, piece],
        scratch_shapes=[
            pltpu.VMEM((K, ROWS), BF16),
            pltpu.VMEM((ROWS, K), F32),
            pltpu.VMEM((GRAM, 128), BF16),
        ],
        compiler_params=LIMIT,
        cost_estimate=PRODUCT,
    )(core, got_w, telemetry)


def exchange(x, axis):
    return lax.all_to_all(x, axis, 0, 0, tiled=True)


def sum_everywhere(shares):
    part = jnp.sum(exchange(shares, "samples"), axis=0)
    part = exchange(jnp.broadcast_to(part[None], (CHIPS, 8, 128)), ("pairs", "core"))
    return jnp.sum(part, axis=0)


def body(telemetry, chip_factors, sample_factors):
    core = lax.axis_index("core").reshape(1)
    w, h = chip_factors.T, sample_factors.T
    (sent,) = call(start_kernel, (w,), [((SAMPLES, W_MSG, 128), BF16)])
    got_w = exchange(sent, "samples")
    (energy,) = call(
        energy_kernel,
        (telemetry,),
        [((8, 128), F32)],
        pl.CostEstimate(
            flops=2 * ROWS * COLS, bytes_accessed=2 * ROWS * COLS, transcendentals=0
        ),
    )
    for sweep in range(ITERS):
        last = sweep == ITERS - 1
        keep, give = h_numer(core, got_w, telemetry)
        taken = lax.ppermute(give, "core", [(0, 1), (1, 0)])
        (sent,) = call(pair_kernel, (keep, taken), [((PAIRS, H_RED, 128), BF16)])
        got = exchange(sent, "pairs")
        h, sent = call(
            h_update_kernel, (got, h), [((H_OWN, K), F32), ((CHIPS, H_OWN, 128), BF16)]
        )
        got_h = exchange(sent, ("pairs", "core"))
        rows = W_RED + GRAM if last else W_RED
        (sent,) = call(w_numer_kernel, (got_h, telemetry), [((SAMPLES, rows, 128), BF16)], PRODUCT)
        got = exchange(sent, "samples")
        if not last:
            w, sent = call(
                w_update_kernel, (got, w), [((W_OWN, K), F32), ((SAMPLES, W_MSG, 128), BF16)]
            )
            got_w = exchange(sent, "samples")
    w, shares = call(
        w_last_kernel, (got, w, energy), [((W_OWN, K), F32), ((SAMPLES, 8, 128), F32)]
    )
    sums = sum_everywhere(shares)
    total = sums[0, K]
    expanded = sums[0, 0] + total

    def direct(w, got_h, telemetry):
        (sent,) = call(last_rows_kernel, (w,), [((SAMPLES, W_HALF, 128), BF16)])
        (shares,) = call(
            error_kernel,
            (exchange(sent, "samples"), got_h, telemetry),
            [((SAMPLES, 8, 128), F32)],
            PRODUCT,
        )
        return sum_everywhere(shares)[0, 0]

    fit_error = lax.cond(
        expanded < 0.02 * total,
        direct,
        lambda *operands: expanded,
        w,
        got_h,
        telemetry,
    )
    return w.T, h.T, jnp.sqrt(fit_error / total)


def solution(mesh):
    split_mesh = Mesh(mesh.devices.reshape(PAIRS, 2, SAMPLES), ("pairs", "core", "samples"))
    chips = ("pairs", "core")
    return jax.shard_map(
        body,
        mesh=split_mesh,
        in_specs=(
            P(chips, "samples"),
            P(None, (*chips, "samples")),
            P(None, ("samples", *chips)),
        ),
        out_specs=(P(None, (*chips, "samples")), P(None, ("samples", *chips)), P()),
        check_vma=False,
    )
```

```python
import jax
import jax.numpy as jnp
from jax import lax
from jax.experimental import pallas as pl
from jax.experimental.pallas import tpu as pltpu
from jax.sharding import Mesh
from jax.sharding import PartitionSpec as P

ITERS = 2

epsilon = 1e-09

F32 = jnp.float32
BF16 = jnp.bfloat16
HIGHEST = lax.Precision.HIGHEST

K = 64
CHIPS = 32
PAIRS = CHIPS // 2
SAMPLES = 16
ROWS = 2304
COLS = 1024
W_OWN = ROWS // SAMPLES
H_OWN = COLS // CHIPS
H_WIDTH = 256
GRAM = 32
W_HALF = 80
W_MSG = W_HALF + GRAM
H_RED = H_OWN + GRAM


def split(x):
    high = x.astype(BF16).astype(F32)
    return jnp.concatenate([high, x - high], axis=1).astype(BF16)


def join(x):
    return x[:, :K] + x[:, K:]


def squares():
    row = lax.broadcasted_iota(jnp.int32, (32, 32), 0)
    col = lax.broadcasted_iota(jnp.int32, (32, 32), 1)
    return row, col


def pack_parts(upper, block, lower_diag, row, col):
    high = upper.astype(BF16).astype(F32)
    low = upper - high
    block_high = block.astype(BF16).astype(F32)
    own = row == col
    return jnp.concatenate(
        [jnp.where(own, upper, high), block_high, jnp.where(own, lower_diag, low), block - block_high],
        axis=1,
    ).astype(BF16)


def pack_gram(gram):
    row, col = squares()
    first, block, last = gram[:32, :32], gram[:32, 32:], gram[32:, 32:]
    return pack_parts(jnp.where(row <= col, first, last), block, last, row, col)


def repack_gram(total):
    row, col = squares()
    own = row == col
    first, third = total[:, :32], total[:, 64:96]
    upper = jnp.where(own, first, first + third)
    return pack_parts(upper, total[:, 32:64] + total[:, 96:], third, row, col)


def unpack_gram(total):
    row, col = squares()
    first, third = total[:, :32], total[:, 64:96]
    mixed = first + third
    block = total[:, 32:64] + total[:, 96:]
    eye = (row == col).astype(F32)
    turned = lax.dot_general(
        eye,
        jnp.concatenate([mixed, block], axis=0),
        (((1,), (1,)), ((), ())),
        precision=HIGHEST,
        preferred_element_type=F32,
    )
    mixed_t, block_t = turned[:, :32], turned[:, 32:]
    one = jnp.where(row < col, mixed, jnp.where(row > col, mixed_t, first))
    two = jnp.where(row > col, mixed, jnp.where(row < col, mixed_t, third))
    return jnp.concatenate(
        [jnp.concatenate([one, block], axis=1), jnp.concatenate([block_t, two], axis=1)], axis=0
    )


def products(halves):
    return lax.dot_general(halves, halves, (((0,), (0,)), ((), ())), preferred_element_type=F32)


def quarters(four):
    two = four[:K] + four[K:]
    return two[:, :K] + two[:, K:]


def two_halves(w):
    tail = jnp.concatenate([w[W_HALF:], jnp.zeros((2 * W_HALF - W_OWN, K), F32)], axis=0)
    return jnp.concatenate([w[:W_HALF], tail], axis=1)


def one_column(both):
    return jnp.concatenate([both[:, :K], both[: W_OWN - W_HALF, K:]], axis=0)


TOP = 14.0


def sender_factor(i):
    return 1.0 + i / 32.0


def eighth_power(x):
    x = x * x
    x = x * x
    return x * x


def eighth_root(x):
    return jnp.sqrt(jnp.sqrt(jnp.sqrt(x)))


def fill_w(w, out):
    rows = two_halves(w).astype(BF16)
    gram = pack_gram(quarters(products(split(w))))
    for i in range(SAMPLES):
        out[i, :W_HALF, :] = rows
        out[i, W_HALF:, :] = gram


def own_rows(ref, i):
    return one_column(ref[i, :W_HALF, :].astype(F32))


def start_kernel(w, out):
    fill_w(w[...], out)


def h_numer_kernel(core, got, tel, keep, give, w_turned, w_all, gram):
    step = pl.program_id(0)

    @pl.when(step == 0)
    def _():
        total = jnp.zeros((GRAM, 128), F32)
        for i in range(SAMPLES):
            w_all[i * W_OWN : (i + 1) * W_OWN, :] = own_rows(got, i)
            total += got[i, W_HALF:, :].astype(F32)
        gram[...] = repack_gram(total)
        for j in range(ROWS // 128):
            w_turned[:, j * 128 : (j + 1) * 128] = w_all[j * 128 : (j + 1) * 128, :].T.astype(BF16)

    part = jnp.dot(w_turned[...], tel[...], preferred_element_type=F32).T
    first = core[0] == 0
    for q in range(H_WIDTH // (2 * H_OWN)):
        even = part[2 * q * H_OWN : (2 * q + 1) * H_OWN]
        odd = part[(2 * q + 1) * H_OWN : (2 * q + 2) * H_OWN]
        keep[q, :H_OWN, :] = split(jnp.where(first, even, odd))
        give[q, :H_OWN, :] = split(jnp.where(first, odd, even))
        keep[q, H_OWN:, :] = gram[...]
        give[q, H_OWN:, :] = gram[...]


def pair_kernel(keep, got, out):
    gram = repack_gram(keep[0, H_OWN:, :].astype(F32) + got[0, H_OWN:, :].astype(F32))
    for i in range(PAIRS):
        total = keep[i, :H_OWN, :].astype(F32) + got[i, :H_OWN, :].astype(F32)
        out[i, :H_OWN, :] = split(join(total))
        out[i, H_OWN:, :] = gram


def h_update_kernel(got, h, h_out, out):
    total = jnp.zeros((H_RED, 128), F32)
    for i in range(PAIRS):
        total += got[i].astype(F32)
    gram = unpack_gram(total[H_OWN:])
    old = h[...]
    below = jnp.dot(old, gram, precision=HIGHEST, preferred_element_type=F32) + epsilon
    new = old * join(total[:H_OWN]) / below
    h_out[...] = new
    halves = split(new)
    for i in range(CHIPS):
        out[i] = halves


def w_numer_kernel(sender, got, tel, out, sums):
    halves = got[...].reshape(COLS, 128)
    four = products(halves)
    gram = pack_gram(quarters(four))
    if out.shape[1] > W_MSG:
        gram = jnp.concatenate([gram, pack_gram(four[:K, :K])], axis=0)
    high = halves[:, :K]
    block = 4 * W_OWN

    def multiply(b, largest):
        rows = pl.ds(pl.multiple_of(b * block, block), block)
        part = jnp.dot(tel[rows, :], high, preferred_element_type=F32)
        sums[rows, :] = part
        return jnp.maximum(largest, jnp.max(part.reshape(block // 8, 8, K), axis=0))

    largest = lax.fori_loop(0, ROWS // block, multiply, jnp.zeros((8, K), F32))
    largest = jnp.max(jnp.max(largest, axis=0, keepdims=True), axis=1, keepdims=True)
    power = jnp.floor(jnp.log2(jnp.maximum(largest, 1e-30)))
    scale = jnp.exp2(TOP - 1.0 - power) * sender_factor(sender[0].astype(F32))
    row = lax.broadcasted_iota(jnp.int32, (W_HALF, 128), 0)
    lane = lax.broadcasted_iota(jnp.int32, (W_HALF, 128), 1)
    free = (row >= W_OWN - W_HALF) & (lane >= K)

    def code(i, carry):
        rows = pl.ds(pl.multiple_of(i * W_OWN, W_OWN), W_OWN)
        coded = eighth_power(two_halves(sums[rows, :]) * scale)
        out[i, :W_HALF, :] = jnp.where(free, power, coded).astype(BF16)
        out[i, W_HALF:, :] = gram
        return carry

    lax.fori_loop(0, SAMPLES, code, 0)


def w_new(got, w):
    numer = jnp.zeros((W_HALF, 128), F32)
    rest = jnp.zeros((got.shape[1] - W_HALF, 128), F32)
    for i in range(SAMPLES):
        coded = got[i, :W_HALF, :].astype(F32)
        power = coded[W_HALF - 1 :, 127:]
        scale = jnp.exp2(power - (TOP - 1.0)) * (1.0 / sender_factor(i))
        numer += eighth_root(jnp.abs(coded)) * scale
        rest += got[i, W_HALF:, :].astype(F32)
    numer = one_column(numer)
    gram = unpack_gram(rest[:GRAM])
    old = w[...]
    below = jnp.dot(old, gram, precision=HIGHEST, preferred_element_type=F32) + epsilon
    return old * numer / below, numer, rest[GRAM:]


def w_update_kernel(got, w, w_out, out):
    new, _, _ = w_new(got, w)
    w_out[...] = new
    fill_w(new, out)


def w_last_kernel(got, w, energy, w_out, out):
    new, numer, rest = w_new(got, w)
    w_out[...] = new
    rounded = new.astype(BF16).astype(F32)
    gram = unpack_gram(rest)
    fitted = jnp.dot(rounded, gram, precision=HIGHEST, preferred_element_type=F32)
    share = jnp.sum(rounded * (fitted - 2.0 * numer))
    lane = lax.broadcasted_iota(jnp.int32, (1, 128), 1)
    pair = jnp.where(lane < K, share, energy[...])
    for i in range(SAMPLES):
        out[i] = pair


def energy_kernel(tel, out):
    def step(i, energy):
        rows = pl.ds(pl.multiple_of(i * W_OWN, W_OWN), W_OWN)
        values = tel[rows, :].astype(F32)
        return energy + jnp.sum((values * values).reshape(W_OWN // 8, 8, COLS), axis=0)

    energy = lax.fori_loop(0, SAMPLES, step, jnp.zeros((8, COLS), F32))
    out[...] = jnp.full((1, 128), jnp.sum(energy), F32)


def last_rows_kernel(w, out):
    rows = two_halves(w[...]).astype(BF16)
    for i in range(SAMPLES):
        out[i] = rows


def error_kernel(got_w, got_h, tel, out):
    high = got_h[...].reshape(COLS, 128)[:, :K]

    def step(i, error):
        rows = pl.ds(pl.multiple_of(i * W_OWN, W_OWN), W_OWN)
        rebuilt = lax.dot_general(
            own_rows(got_w, i).astype(BF16),
            high,
            (((1,), (1,)), ((), ())),
            preferred_element_type=F32,
        )
        difference = tel[rows, :].astype(F32) - rebuilt
        return error + jnp.sum((difference * difference).reshape(W_OWN // 8, 8, COLS), axis=0)

    error = lax.fori_loop(0, SAMPLES, step, jnp.zeros((8, COLS), F32))
    share = jnp.full((1, 128), jnp.sum(error), F32)
    for i in range(SAMPLES):
        out[i] = share


VMEM = pl.BlockSpec(memory_space=pltpu.VMEM)
LIMIT = pltpu.CompilerParams(vmem_limit_bytes=32 * 1024 * 1024)
PRODUCT = pl.CostEstimate(
    flops=2 * K * ROWS * COLS, bytes_accessed=2 * ROWS * COLS, transcendentals=0
)


def call(kernel, inputs, outs, cost=None):
    return pl.pallas_call(
        kernel,
        out_shape=[jax.ShapeDtypeStruct(shape, dtype) for shape, dtype in outs],
        in_specs=[VMEM] * len(inputs),
        out_specs=[VMEM] * len(outs),
        compiler_params=LIMIT,
        cost_estimate=cost,
    )(*inputs)


def h_numer(core, got_w, telemetry):
    per = H_WIDTH // (2 * H_OWN)
    piece = pl.BlockSpec((per, H_RED, 128), lambda n: (n, 0, 0))
    message = jax.ShapeDtypeStruct((PAIRS, H_RED, 128), BF16)
    return pl.pallas_call(
        h_numer_kernel,
        grid=(COLS // H_WIDTH,),
        out_shape=[message, message],
        in_specs=[
            pl.BlockSpec(memory_space=pltpu.SMEM),
            pl.BlockSpec(got_w.shape, lambda n: (0, 0, 0)),
            pl.BlockSpec((ROWS, H_WIDTH), lambda n: (0, n)),
        ],
        out_specs=[piece, piece],
        scratch_shapes=[
            pltpu.VMEM((K, ROWS), BF16),
            pltpu.VMEM((ROWS, K), F32),
            pltpu.VMEM((GRAM, 128), BF16),
        ],
        compiler_params=LIMIT,
        cost_estimate=PRODUCT,
    )(core, got_w, telemetry)


def w_numer(sender, got_h, telemetry, rows):
    return pl.pallas_call(
        w_numer_kernel,
        out_shape=jax.ShapeDtypeStruct((SAMPLES, rows, 128), BF16),
        in_specs=[pl.BlockSpec(memory_space=pltpu.SMEM), VMEM, VMEM],
        out_specs=VMEM,
        scratch_shapes=[pltpu.VMEM((ROWS, K), F32)],
        compiler_params=LIMIT,
        cost_estimate=PRODUCT,
    )(sender, got_h, telemetry)


def exchange(x, axis):
    return lax.all_to_all(x, axis, 0, 0, tiled=True)


def sum_everywhere(shares):
    part = jnp.sum(exchange(shares, "samples"), axis=0)
    part = exchange(jnp.broadcast_to(part[None], (CHIPS, 1, 128)), ("pairs", "core"))
    return jnp.sum(part, axis=0)


def body(telemetry, chip_factors, sample_factors):
    core = lax.axis_index("core").reshape(1)
    sender = lax.axis_index("samples").reshape(1)
    w, h = chip_factors.T, sample_factors.T
    (sent,) = call(start_kernel, (w,), [((SAMPLES, W_MSG, 128), BF16)])
    got_w = exchange(sent, "samples")
    (energy,) = call(
        energy_kernel,
        (telemetry,),
        [((1, 128), F32)],
        pl.CostEstimate(
            flops=2 * ROWS * COLS, bytes_accessed=2 * ROWS * COLS, transcendentals=0
        ),
    )
    for sweep in range(ITERS):
        last = sweep == ITERS - 1
        keep, give = h_numer(core, got_w, telemetry)
        taken = lax.ppermute(give, "core", [(0, 1), (1, 0)])
        (sent,) = call(pair_kernel, (keep, taken), [((PAIRS, H_RED, 128), BF16)])
        got = exchange(sent, "pairs")
        h, sent = call(
            h_update_kernel, (got, h), [((H_OWN, K), F32), ((CHIPS, H_OWN, 128), BF16)]
        )
        got_h = exchange(sent, ("pairs", "core"))
        sent = w_numer(sender, got_h, telemetry, W_MSG + GRAM if last else W_MSG)
        got = exchange(sent, "samples")
        if not last:
            w, sent = call(
                w_update_kernel, (got, w), [((W_OWN, K), F32), ((SAMPLES, W_MSG, 128), BF16)]
            )
            got_w = exchange(sent, "samples")
    w, shares = call(
        w_last_kernel, (got, w, energy), [((W_OWN, K), F32), ((SAMPLES, 1, 128), F32)]
    )
    sums = sum_everywhere(shares)
    total = sums[0, K]
    expanded = sums[0, 0] + total

    def direct(w, got_h, telemetry):
        (sent,) = call(last_rows_kernel, (w,), [((SAMPLES, W_HALF, 128), BF16)])
        (shares,) = call(
            error_kernel,
            (exchange(sent, "samples"), got_h, telemetry),
            [((SAMPLES, 1, 128), F32)],
            PRODUCT,
        )
        return sum_everywhere(shares)[0, 0]

    fit_error = lax.cond(
        expanded < 0.02 * total,
        direct,
        lambda *operands: expanded,
        w,
        got_h,
        telemetry,
    )
    return w.T, h.T, jnp.sqrt(fit_error / total)


def solution(mesh):
    split_mesh = Mesh(mesh.devices.reshape(PAIRS, 2, SAMPLES), ("pairs", "core", "samples"))
    chips = ("pairs", "core")
    return jax.shard_map(
        body,
        mesh=split_mesh,
        in_specs=(
            P(chips, "samples"),
            P(None, (*chips, "samples")),
            P(None, ("samples", *chips)),
        ),
        out_specs=(P(None, (*chips, "samples")), P(None, ("samples", *chips)), P()),
        check_vma=False,
    )
```

```python
import jax
import jax.numpy as jnp
from jax import lax
from jax.experimental import pallas as pl
from jax.experimental.pallas import tpu as pltpu
from jax.sharding import Mesh
from jax.sharding import PartitionSpec as P

ITERS = 2

epsilon = 1e-09

F32 = jnp.float32
BF16 = jnp.bfloat16
HIGHEST = lax.Precision.HIGHEST

K = 64
CHIPS = 32
PAIRS = CHIPS // 2
SAMPLES = 16
ROWS = 2304
COLS = 1024
W_OWN = ROWS // SAMPLES
H_OWN = COLS // CHIPS
H_WIDTH = 256
GRAM = 32
W_HALF = 80
W_MSG = W_HALF + GRAM
H_RED = H_OWN + GRAM


def split(x):
    high = x.astype(BF16).astype(F32)
    return jnp.concatenate([high, x - high], axis=1).astype(BF16)


def join(x):
    return x[:, :K] + x[:, K:]


def squares():
    row = lax.broadcasted_iota(jnp.int32, (32, 32), 0)
    col = lax.broadcasted_iota(jnp.int32, (32, 32), 1)
    return row, col


def pack_parts(upper, block, lower_diag, row, col):
    high = upper.astype(BF16).astype(F32)
    low = upper - high
    block_high = block.astype(BF16).astype(F32)
    own = row == col
    return jnp.concatenate(
        [jnp.where(own, upper, high), block_high, jnp.where(own, lower_diag, low), block - block_high],
        axis=1,
    ).astype(BF16)


def pack_gram(gram):
    row, col = squares()
    first, block, last = gram[:32, :32], gram[:32, 32:], gram[32:, 32:]
    return pack_parts(jnp.where(row <= col, first, last), block, last, row, col)


def repack_gram(total):
    row, col = squares()
    own = row == col
    first, third = total[:, :32], total[:, 64:96]
    upper = jnp.where(own, first, first + third)
    return pack_parts(upper, total[:, 32:64] + total[:, 96:], third, row, col)


def unpack_gram(total):
    row, col = squares()
    first, third = total[:, :32], total[:, 64:96]
    mixed = first + third
    block = total[:, 32:64] + total[:, 96:]
    eye = (row == col).astype(F32)
    turned = lax.dot_general(
        eye,
        jnp.concatenate([mixed, block], axis=0),
        (((1,), (1,)), ((), ())),
        precision=HIGHEST,
        preferred_element_type=F32,
    )
    mixed_t, block_t = turned[:, :32], turned[:, 32:]
    one = jnp.where(row < col, mixed, jnp.where(row > col, mixed_t, first))
    two = jnp.where(row > col, mixed, jnp.where(row < col, mixed_t, third))
    return jnp.concatenate(
        [jnp.concatenate([one, block], axis=1), jnp.concatenate([block_t, two], axis=1)], axis=0
    )


def products(halves):
    return lax.dot_general(halves, halves, (((0,), (0,)), ((), ())), preferred_element_type=F32)


def quarters(four):
    two = four[:K] + four[K:]
    return two[:, :K] + two[:, K:]


def two_halves(w):
    tail = jnp.concatenate([w[W_HALF:], jnp.zeros((2 * W_HALF - W_OWN, K), F32)], axis=0)
    return jnp.concatenate([w[:W_HALF], tail], axis=1)


def one_column(both):
    return jnp.concatenate([both[:, :K], both[: W_OWN - W_HALF, K:]], axis=0)


TOP = 6.0
BLOCK = 16
LEFT = W_HALF // BLOCK


def sender_factor(i):
    return 1.0 + i / 32.0


def encode(sums, factor):
    blocks = [sums[j * BLOCK : (j + 1) * BLOCK] for j in range(W_OWN // BLOCK)]
    largest = jnp.concatenate(
        [jnp.max(x, axis=0, keepdims=True) for x in blocks]
        + [jnp.zeros((BLOCK - len(blocks), K), F32)],
        axis=0,
    )
    largest = jnp.max(largest, axis=1, keepdims=True)
    power = jnp.floor(jnp.log2(jnp.maximum(largest, 1e-30)))
    scale = jnp.exp2(TOP - power) * factor
    coded = []
    for j, x in enumerate(blocks):
        x = x * scale[j : j + 1]
        x = x * x
        x = x * x
        x = x * x
        coded.append(x * x)
    coded.append(jnp.broadcast_to(power, (BLOCK, K)))
    return jnp.concatenate(
        [jnp.concatenate(coded[:LEFT], axis=0), jnp.concatenate(coded[LEFT:], axis=0)], axis=1
    ).astype(BF16)


def decode(message, factor):
    lane = lax.broadcasted_iota(jnp.int32, (BLOCK, 128), 1)
    message = message.astype(F32)
    scale = jnp.exp2(message[W_HALF - BLOCK :, 127:] - TOP) * (1.0 / factor)
    roots = jnp.sqrt(jnp.sqrt(jnp.sqrt(jnp.sqrt(jnp.abs(message)))))
    return [
        roots[j * BLOCK : (j + 1) * BLOCK]
        * jnp.where(lane < K, scale[j : j + 1], scale[LEFT + j : LEFT + j + 1])
        for j in range(LEFT)
    ]


def fill_w(w, out):
    rows = two_halves(w).astype(BF16)
    gram = pack_gram(quarters(products(split(w))))
    for i in range(SAMPLES):
        out[i, :W_HALF, :] = rows
        out[i, W_HALF:, :] = gram


def own_rows(ref, i):
    return one_column(ref[i, :W_HALF, :].astype(F32))


def start_kernel(w, out):
    fill_w(w[...], out)


def h_numer_kernel(core, got, tel, keep, give, w_turned, w_all, gram):
    step = pl.program_id(0)

    @pl.when(step == 0)
    def _():
        total = jnp.zeros((GRAM, 128), F32)
        for i in range(SAMPLES):
            w_all[i * W_OWN : (i + 1) * W_OWN, :] = own_rows(got, i)
            total += got[i, W_HALF:, :].astype(F32)
        gram[...] = repack_gram(total)
        for j in range(ROWS // 128):
            w_turned[:, j * 128 : (j + 1) * 128] = w_all[j * 128 : (j + 1) * 128, :].T.astype(BF16)

    part = jnp.dot(w_turned[...], tel[...], preferred_element_type=F32).T
    first = core[0] == 0
    for q in range(H_WIDTH // (2 * H_OWN)):
        even = part[2 * q * H_OWN : (2 * q + 1) * H_OWN]
        odd = part[(2 * q + 1) * H_OWN : (2 * q + 2) * H_OWN]
        keep[q, :H_OWN, :] = split(jnp.where(first, even, odd))
        give[q, :H_OWN, :] = split(jnp.where(first, odd, even))
        keep[q, H_OWN:, :] = gram[...]
        give[q, H_OWN:, :] = gram[...]


def pair_kernel(keep, got, out):
    gram = repack_gram(keep[0, H_OWN:, :].astype(F32) + got[0, H_OWN:, :].astype(F32))
    for i in range(PAIRS):
        total = keep[i, :H_OWN, :].astype(F32) + got[i, :H_OWN, :].astype(F32)
        out[i, :H_OWN, :] = split(join(total))
        out[i, H_OWN:, :] = gram


def h_update_kernel(got, h, h_out, out):
    total = jnp.zeros((H_RED, 128), F32)
    for i in range(PAIRS):
        total += got[i].astype(F32)
    gram = unpack_gram(total[H_OWN:])
    old = h[...]
    below = jnp.dot(old, gram, precision=HIGHEST, preferred_element_type=F32) + epsilon
    new = old * join(total[:H_OWN]) / below
    h_out[...] = new
    halves = split(new)
    for i in range(CHIPS):
        out[i] = halves


def w_numer_kernel(sender, got, tel, out):
    halves = got[...].reshape(COLS, 128)
    four = products(halves)
    gram = pack_gram(quarters(four))
    if out.shape[1] > W_MSG:
        gram = jnp.concatenate([gram, pack_gram(four[:K, :K])], axis=0)
    high = halves[:, :K]
    per = 4
    block = per * W_OWN
    factor = sender_factor(sender[0].astype(F32))

    def step(b, carry):
        rows = pl.ds(pl.multiple_of(b * block, block), block)
        part = jnp.dot(tel[rows, :], high, preferred_element_type=F32)
        for q in range(per):
            out[b * per + q, :W_HALF, :] = encode(part[q * W_OWN : (q + 1) * W_OWN], factor)
            out[b * per + q, W_HALF:, :] = gram
        return carry

    lax.fori_loop(0, ROWS // block, step, 0)


def w_new(got, w):
    blocks = [jnp.zeros((BLOCK, 128), F32)] * LEFT
    rest = jnp.zeros((got.shape[1] - W_HALF, 128), F32)
    for i in range(SAMPLES):
        terms = decode(got[i, :W_HALF, :], sender_factor(i))
        blocks = [total + term for total, term in zip(blocks, terms)]
        rest += got[i, W_HALF:, :].astype(F32)
    numer = one_column(jnp.concatenate(blocks, axis=0))
    gram = unpack_gram(rest[:GRAM])
    old = w[...]
    below = jnp.dot(old, gram, precision=HIGHEST, preferred_element_type=F32) + epsilon
    return old * numer / below, numer, rest[GRAM:]


def w_update_kernel(got, w, w_out, out):
    new, _, _ = w_new(got, w)
    w_out[...] = new
    fill_w(new, out)


def w_last_kernel(got, w, energy, w_out, out):
    new, numer, rest = w_new(got, w)
    w_out[...] = new
    rounded = new.astype(BF16).astype(F32)
    gram = unpack_gram(rest)
    fitted = jnp.dot(rounded, gram, precision=HIGHEST, preferred_element_type=F32)
    share = jnp.sum(rounded * (fitted - 2.0 * numer))
    lane = lax.broadcasted_iota(jnp.int32, (1, 128), 1)
    pair = jnp.where(lane < K, share, energy[...])
    for i in range(SAMPLES):
        out[i] = pair


def load_kernel(tel, tile, out):
    def step(i, energy):
        rows = pl.ds(pl.multiple_of(i * W_OWN, W_OWN), W_OWN)
        tile[rows, :] = tel[rows, :]
        values = tel[rows, :].astype(F32)
        return energy + jnp.sum((values * values).reshape(W_OWN // 8, 8, COLS), axis=0)

    energy = lax.fori_loop(0, SAMPLES, step, jnp.zeros((8, COLS), F32))
    out[...] = jnp.full((1, 128), jnp.sum(energy), F32)


def last_rows_kernel(w, out):
    rows = two_halves(w[...]).astype(BF16)
    for i in range(SAMPLES):
        out[i] = rows


def error_kernel(got_w, got_h, tel, out):
    high = got_h[...].reshape(COLS, 128)[:, :K]

    def step(i, error):
        rows = pl.ds(pl.multiple_of(i * W_OWN, W_OWN), W_OWN)
        rebuilt = lax.dot_general(
            own_rows(got_w, i).astype(BF16),
            high,
            (((1,), (1,)), ((), ())),
            preferred_element_type=F32,
        )
        difference = tel[rows, :].astype(F32) - rebuilt
        return error + jnp.sum((difference * difference).reshape(W_OWN // 8, 8, COLS), axis=0)

    error = lax.fori_loop(0, SAMPLES, step, jnp.zeros((8, COLS), F32))
    share = jnp.full((1, 128), jnp.sum(error), F32)
    for i in range(SAMPLES):
        out[i] = share


VMEM = pl.BlockSpec(memory_space=pltpu.VMEM)
LIMIT = pltpu.CompilerParams(vmem_limit_bytes=32 * 1024 * 1024)
PRODUCT = pl.CostEstimate(
    flops=2 * K * ROWS * COLS, bytes_accessed=2 * ROWS * COLS, transcendentals=0
)
LOAD = pl.CostEstimate(flops=2 * ROWS * COLS, bytes_accessed=4 * ROWS * COLS, transcendentals=0)


def call(kernel, inputs, outs, cost=None):
    return pl.pallas_call(
        kernel,
        out_shape=[jax.ShapeDtypeStruct(shape, dtype) for shape, dtype in outs],
        in_specs=[VMEM] * len(inputs),
        out_specs=[VMEM] * len(outs),
        compiler_params=LIMIT,
        cost_estimate=cost,
    )(*inputs)


def h_numer(core, got_w, telemetry):
    per = H_WIDTH // (2 * H_OWN)
    piece = pl.BlockSpec((per, H_RED, 128), lambda n: (n, 0, 0))
    message = jax.ShapeDtypeStruct((PAIRS, H_RED, 128), BF16)
    return pl.pallas_call(
        h_numer_kernel,
        grid=(COLS // H_WIDTH,),
        out_shape=[message, message],
        in_specs=[
            pl.BlockSpec(memory_space=pltpu.SMEM),
            pl.BlockSpec(got_w.shape, lambda n: (0, 0, 0)),
            pl.BlockSpec((ROWS, H_WIDTH), lambda n: (0, n)),
        ],
        out_specs=[piece, piece],
        scratch_shapes=[
            pltpu.VMEM((K, ROWS), BF16),
            pltpu.VMEM((ROWS, K), F32),
            pltpu.VMEM((GRAM, 128), BF16),
        ],
        compiler_params=LIMIT,
        cost_estimate=PRODUCT,
    )(core, got_w, telemetry)


def w_numer(sender, got_h, telemetry, rows):
    return pl.pallas_call(
        w_numer_kernel,
        out_shape=jax.ShapeDtypeStruct((SAMPLES, rows, 128), BF16),
        in_specs=[pl.BlockSpec(memory_space=pltpu.SMEM), VMEM, VMEM],
        out_specs=VMEM,
        compiler_params=LIMIT,
        cost_estimate=PRODUCT,
    )(sender, got_h, telemetry)


def exchange(x, axis):
    return lax.all_to_all(x, axis, 0, 0, tiled=True)


def sum_everywhere(shares):
    part = jnp.sum(exchange(shares, "samples"), axis=0)
    part = exchange(jnp.broadcast_to(part[None], (CHIPS, 1, 128)), ("pairs", "core"))
    return jnp.sum(part, axis=0)


def body(telemetry, chip_factors, sample_factors):
    core = lax.axis_index("core").reshape(1)
    sender = lax.axis_index("samples").reshape(1)
    w, h = chip_factors.T, sample_factors.T
    (sent,) = call(start_kernel, (w,), [((SAMPLES, W_MSG, 128), BF16)])
    got_w = exchange(sent, "samples")
    tile, energy = call(
        load_kernel, (telemetry,), [((ROWS, COLS), BF16), ((1, 128), F32)], LOAD
    )
    for sweep in range(ITERS):
        last = sweep == ITERS - 1
        keep, give = h_numer(core, got_w, tile)
        taken = lax.ppermute(give, "core", [(0, 1), (1, 0)])
        (sent,) = call(pair_kernel, (keep, taken), [((PAIRS, H_RED, 128), BF16)])
        got = exchange(sent, "pairs")
        h, sent = call(
            h_update_kernel, (got, h), [((H_OWN, K), F32), ((CHIPS, H_OWN, 128), BF16)]
        )
        got_h = exchange(sent, ("pairs", "core"))
        sent = w_numer(sender, got_h, tile, W_MSG + GRAM if last else W_MSG)
        got = exchange(sent, "samples")
        if not last:
            w, sent = call(
                w_update_kernel, (got, w), [((W_OWN, K), F32), ((SAMPLES, W_MSG, 128), BF16)]
            )
            got_w = exchange(sent, "samples")
    w, shares = call(
        w_last_kernel, (got, w, energy), [((W_OWN, K), F32), ((SAMPLES, 1, 128), F32)]
    )
    sums = sum_everywhere(shares)
    total = sums[0, K]
    expanded = sums[0, 0] + total

    def direct(w, got_h, tile):
        (sent,) = call(last_rows_kernel, (w,), [((SAMPLES, W_HALF, 128), BF16)])
        (shares,) = call(
            error_kernel,
            (exchange(sent, "samples"), got_h, tile),
            [((SAMPLES, 1, 128), F32)],
            PRODUCT,
        )
        return sum_everywhere(shares)[0, 0]

    fit_error = lax.cond(
        expanded < 0.02 * total,
        direct,
        lambda *operands: expanded,
        w,
        got_h,
        tile,
    )
    return w.T, h.T, jnp.sqrt(fit_error / total)


def solution(mesh):
    split_mesh = Mesh(mesh.devices.reshape(PAIRS, 2, SAMPLES), ("pairs", "core", "samples"))
    chips = ("pairs", "core")
    return jax.shard_map(
        body,
        mesh=split_mesh,
        in_specs=(
            P(chips, "samples"),
            P(None, (*chips, "samples")),
            P(None, ("samples", *chips)),
        ),
        out_specs=(P(None, (*chips, "samples")), P(None, ("samples", *chips)), P()),
        check_vma=False,
    )
```

```python
import jax
import jax.numpy as jnp
from jax import lax
from jax.experimental import pallas as pl
from jax.experimental.pallas import tpu as pltpu
from jax.sharding import PartitionSpec as P

ITERS = 2

epsilon = 1e-09

F32 = jnp.float32
BF16 = jnp.bfloat16
HIGHEST = lax.Precision.HIGHEST

K = 64
CHIPS = 32
SAMPLES = 16
ROWS = 2304
COLS = 1024
W_OWN = ROWS // SAMPLES
H_OWN = COLS // CHIPS
H_WIDTH = 256
W_STEP = 4
BLOCK = 16
W_HALF = 80
GRAM = 16
W_MSG = W_HALF + GRAM
PAIR = 32
H_MSG = BLOCK + GRAM + 8
LEFT = W_HALF // BLOCK
W_BLOCKS = W_OWN // BLOCK


def split(x):
    high = x.astype(BF16).astype(F32)
    return jnp.concatenate([high, x - high], axis=1).astype(BF16)


def join(x):
    return x[:, :K] + x[:, K:]


def squares():
    row = lax.broadcasted_iota(jnp.int32, (32, 32), 0)
    col = lax.broadcasted_iota(jnp.int32, (32, 32), 1)
    return row, col


TOP = 6.0


def peak(x):
    return jnp.max(jnp.max(x, axis=0, keepdims=True), axis=1, keepdims=True)


def power_of(largest):
    return jnp.floor(jnp.log2(jnp.maximum(largest, 1e-30)))


def code(x, power, factor):
    x = x * (jnp.exp2(TOP - power) * factor)
    x = x * x
    x = x * x
    x = x * x
    return x * x


def root(x):
    return jnp.sqrt(jnp.sqrt(jnp.sqrt(jnp.sqrt(jnp.abs(x)))))


def scale_of(power, factor):
    return jnp.exp2(power - TOP) * (1.0 / factor)


def sample_factor(i):
    return 1.0 + i / 32.0


def chip_factor(i):
    return 1.0 + i / 64.0


def gram_parts(gram):
    row, col = squares()
    first, block, last = gram[:32, :32], gram[:32, 32:], gram[32:, 32:]
    parts = jnp.concatenate([jnp.where(row <= col, first, last), block], axis=1)
    return parts, jnp.sum(jnp.where(row == col, last, 0.0), axis=0, keepdims=True)


def gram_whole(parts, diagonal):
    row, col = squares()
    mixed, block = parts[:, :32], parts[:, 32:]
    turned = lax.dot_general(
        (row == col).astype(F32),
        jnp.concatenate([mixed, block], axis=0),
        (((1,), (1,)), ((), ())),
        precision=HIGHEST,
        preferred_element_type=F32,
    )
    mixed_t, block_t = turned[:, :32], turned[:, 32:]
    one = jnp.where(row <= col, mixed, mixed_t)
    two = jnp.where(row > col, mixed, jnp.where(row < col, mixed_t, diagonal))
    return jnp.concatenate(
        [jnp.concatenate([one, block], axis=1), jnp.concatenate([block_t, two], axis=1)], axis=0
    )


def encode_gram(parts, diagonal, factor):
    power = power_of(jnp.maximum(peak(parts), peak(diagonal)))
    coded = code(parts, power, factor)
    return (
        jnp.concatenate([coded[:GRAM], coded[GRAM:]], axis=1),
        code(diagonal, power, factor),
        power,
    )


def one_above(x):
    return jnp.concatenate([x[:, :K], x[:, K:]], axis=0)


def pair_of(gram):
    row, col = squares()
    parts, diagonal = gram_parts(gram)
    high = parts.astype(BF16).astype(F32)
    low = parts - high
    own = row == col
    first = jnp.where(own, parts[:, :32], high[:, :32])
    third = jnp.where(own, diagonal, low[:, :32])
    return jnp.concatenate([first, high[:, 32:], third, low[:, 32:]], axis=1).astype(BF16)


def of_pair(total):
    row, col = squares()
    own = row == col
    first, third = total[:, :32], total[:, 64:96]
    mixed = jnp.where(own, first, first + third)
    diagonal = jnp.sum(jnp.where(own, third, 0.0), axis=0, keepdims=True)
    block = total[:, 32:64] + total[:, 96:]
    return gram_whole(jnp.concatenate([mixed, block], axis=1), diagonal)


def products(halves):
    return lax.dot_general(halves, halves, (((0,), (0,)), ((), ())), preferred_element_type=F32)


def quarters(four):
    two = four[:K] + four[K:]
    return two[:, :K] + two[:, K:]


def spare_rows(powers, diagonal, power):
    return jnp.concatenate(
        [
            jnp.broadcast_to(powers, (W_BLOCKS, K)),
            jnp.broadcast_to(power, (1, K)),
            jnp.concatenate([diagonal, jnp.zeros((1, K - 32), F32)], axis=1),
            jnp.zeros((BLOCK - W_BLOCKS - 2, K), F32),
        ],
        axis=0,
    )


def w_message(w, gram):
    coded, diagonal, power = gram
    right = jnp.concatenate(
        [w[W_HALF:], spare_rows(jnp.zeros((W_BLOCKS, 1), F32), diagonal, power)], axis=0
    )
    return jnp.concatenate(
        [jnp.concatenate([w[:W_HALF], right], axis=1), coded], axis=0
    ).astype(BF16)


def sums_message(sums, gram, factor):
    coded, diagonal, power = gram
    blocks = [sums[j * BLOCK : (j + 1) * BLOCK] for j in range(W_BLOCKS)]
    largest = jnp.concatenate([jnp.max(x, axis=0, keepdims=True) for x in blocks], axis=0)
    powers = power_of(jnp.max(largest, axis=1, keepdims=True))
    blocks = [code(x, powers[j : j + 1], factor) for j, x in enumerate(blocks)]
    left = jnp.concatenate(blocks[:LEFT], axis=0)
    right = jnp.concatenate(blocks[LEFT:] + [spare_rows(powers, diagonal, power)], axis=0)
    return jnp.concatenate(
        [jnp.concatenate([left, right], axis=1), coded], axis=0
    ).astype(BF16)


def read_gram(message, factor):
    roots = root(message)
    scale = scale_of(message[W_BLOCKS : W_BLOCKS + 1, 127:], factor)
    return roots[BLOCK:] * scale, roots[W_BLOCKS + 1 : W_BLOCKS + 2] * scale


def read_sums(message, factor):
    lane = lax.broadcasted_iota(jnp.int32, (BLOCK, 128), 1)
    scale = scale_of(message[W_HALF - BLOCK :, 127:], factor)
    roots = root(message)
    return [
        roots[j * BLOCK : (j + 1) * BLOCK]
        * jnp.where(lane < K, scale[j : j + 1], scale[LEFT + j : LEFT + j + 1])
        for j in range(LEFT)
    ]


def one_column(both):
    return jnp.concatenate([both[:, :K], both[: W_OWN - W_HALF, K:]], axis=0)


def fill_w(w, factor, out):
    gram = gram_parts(quarters(products(split(w))))
    message = w_message(w, encode_gram(*gram, factor))
    for i in range(SAMPLES):
        out[i] = message


def start_kernel(me, w, out):
    fill_w(w[...], sample_factor(me[1].astype(F32)), out)


def h_numer_kernel(me, got, tel, out, tile, w_turned, w_all, arrived):
    copy = pltpu.make_async_copy(tel, tile, arrived)
    copy.start()
    gram = jnp.zeros((GRAM, 128), F32)
    diagonal = jnp.zeros((1, 128), F32)
    for i in range(SAMPLES):
        message = got[i].astype(F32)
        w_all[i * W_OWN : (i + 1) * W_OWN, :] = one_column(message[:W_HALF])
        more, ends = read_gram(message[W_HALF - BLOCK :], sample_factor(i))
        gram += more
        diagonal += ends
    for j in range(ROWS // 128):
        w_turned[:, j * 128 : (j + 1) * 128] = w_all[j * 128 : (j + 1) * 128, :].T.astype(BF16)
    factor = chip_factor(me[0].astype(F32))
    coded, ends, power = encode_gram(one_above(gram), diagonal[:, K : K + 32], factor)
    ends = jnp.concatenate([ends, jnp.zeros((1, 96), F32)], axis=1)
    power = jnp.broadcast_to(power, (1, 128))
    copy.wait()
    per = H_WIDTH // H_OWN

    def step(n, carry):
        cols = pl.ds(pl.multiple_of(n * H_WIDTH, H_WIDTH), H_WIDTH)
        part = jnp.dot(w_turned[...], tile[:, cols], preferred_element_type=F32).T
        for q in range(per):
            halves = [part[q * H_OWN + r : q * H_OWN + r + BLOCK] for r in (0, BLOCK)]
            powers = [power_of(peak(x)) for x in halves]
            out[n * per + q] = jnp.concatenate(
                [
                    jnp.concatenate([code(x, p, factor) for x, p in zip(halves, powers)], axis=1),
                    coded,
                    ends,
                    power,
                    jnp.broadcast_to(powers[0], (1, 128)),
                    jnp.broadcast_to(powers[1], (1, 128)),
                    jnp.zeros((4, 128), F32),
                ],
                axis=0,
            ).astype(BF16)
        return carry

    lax.fori_loop(0, COLS // H_WIDTH, step, 0)


def h_update_kernel(got, h, h_out, out):
    lane = lax.broadcasted_iota(jnp.int32, (BLOCK, 128), 1)
    numer = jnp.zeros((BLOCK, 128), F32)
    gram = jnp.zeros((GRAM, 128), F32)
    diagonal = jnp.zeros((1, 128), F32)
    for i in range(CHIPS):
        message = got[i].astype(F32)
        roots = root(message)
        scales = scale_of(message[H_MSG - 8 :, 127:], chip_factor(i))
        numer += roots[:BLOCK] * jnp.where(lane < K, scales[2:3], scales[3:4])
        gram += roots[BLOCK : BLOCK + GRAM] * scales[1:2]
        diagonal += roots[H_MSG - 8 : H_MSG - 7] * scales[1:2]
    gram = gram_whole(one_above(gram), diagonal[:, :32])
    old = h[...]
    below = jnp.dot(old, gram, precision=HIGHEST, preferred_element_type=F32) + epsilon
    new = old * one_above(numer) / below
    h_out[...] = new
    halves = split(new)
    for i in range(CHIPS):
        out[i] = halves


def w_numer_kernel(me, got, tel, out, tile, arrived):
    block = W_STEP * W_OWN

    def copy(b):
        rows = pl.ds(pl.multiple_of(b * block, block), block)
        return pltpu.make_async_copy(tel.at[rows], tile.at[rows], arrived.at[b])

    for b in range(ROWS // block):
        copy(b).start()
    halves = got[...].reshape(COLS, 128)
    four = products(halves)
    factor = sample_factor(me[1].astype(F32))
    gram = encode_gram(*gram_parts(quarters(four)), factor)
    last = out.shape[1] > W_MSG
    if last:
        pair = pair_of(four[:K, :K])
    high = halves[:, :K]

    def step(b, carry):
        copy(b).wait()
        rows = pl.ds(pl.multiple_of(b * block, block), block)
        part = jnp.dot(tile[rows, :], high, preferred_element_type=F32)
        for q in range(W_STEP):
            message = sums_message(part[q * W_OWN : (q + 1) * W_OWN], gram, factor)
            if last:
                message = jnp.concatenate([message, pair], axis=0)
            out[b * W_STEP + q] = message
        return carry

    lax.fori_loop(0, ROWS // block, step, 0)


def w_new(got, w):
    blocks = [jnp.zeros((BLOCK, 128), F32)] * LEFT
    gram = jnp.zeros((GRAM, 128), F32)
    diagonal = jnp.zeros((1, 128), F32)
    rest = jnp.zeros((got.shape[1] - W_MSG, 128), F32) if got.shape[1] > W_MSG else None
    for i in range(SAMPLES):
        message = got[i].astype(F32)
        terms = read_sums(message[:W_HALF], sample_factor(i))
        blocks = [total + term for total, term in zip(blocks, terms)]
        more, ends = read_gram(message[W_HALF - BLOCK : W_MSG], sample_factor(i))
        gram += more
        diagonal += ends
        if rest is not None:
            rest += message[W_MSG:]
    numer = one_column(jnp.concatenate(blocks, axis=0))
    gram = gram_whole(one_above(gram), diagonal[:, K : K + 32])
    old = w[...]
    below = jnp.dot(old, gram, precision=HIGHEST, preferred_element_type=F32) + epsilon
    return old * numer / below, numer, rest


def w_update_kernel(me, got, w, w_out, out):
    new, _, _ = w_new(got, w)
    w_out[...] = new
    fill_w(new, sample_factor(me[1].astype(F32)), out)


def w_last_kernel(got, w, energy, w_out, out):
    new, numer, rest = w_new(got, w)
    w_out[...] = new
    rounded = new.astype(BF16).astype(F32)
    gram = of_pair(rest)
    fitted = jnp.dot(rounded, gram, precision=HIGHEST, preferred_element_type=F32)
    share = jnp.sum(rounded * (fitted - 2.0 * numer))
    lane = lax.broadcasted_iota(jnp.int32, (1, 128), 1)
    pair = jnp.where(lane < K, share, energy[...])
    for i in range(SAMPLES):
        out[i] = pair


def energy_kernel(tel, out):
    def step(i, energy):
        rows = pl.ds(pl.multiple_of(i * W_OWN, W_OWN), W_OWN)
        values = tel[rows, :].astype(F32)
        return energy + jnp.sum((values * values).reshape(W_OWN // 8, 8, COLS), axis=0)

    energy = lax.fori_loop(0, SAMPLES, step, jnp.zeros((8, COLS), F32))
    out[...] = jnp.full((1, 128), jnp.sum(energy), F32)


def last_rows_kernel(w, out):
    rows = w[...]
    right = jnp.concatenate([rows[W_HALF:], jnp.zeros((BLOCK, K), F32)], axis=0)
    message = jnp.concatenate([rows[:W_HALF], right], axis=1).astype(BF16)
    for i in range(SAMPLES):
        out[i] = message


def error_kernel(got_w, got_h, tel, out):
    high = got_h[...].reshape(COLS, 128)[:, :K]

    def step(i, error):
        rows = pl.ds(pl.multiple_of(i * W_OWN, W_OWN), W_OWN)
        rebuilt = lax.dot_general(
            one_column(got_w[i].astype(F32)).astype(BF16),
            high,
            (((1,), (1,)), ((), ())),
            preferred_element_type=F32,
        )
        difference = tel[rows, :].astype(F32) - rebuilt
        return error + jnp.sum((difference * difference).reshape(W_OWN // 8, 8, COLS), axis=0)

    error = lax.fori_loop(0, SAMPLES, step, jnp.zeros((8, COLS), F32))
    share = jnp.full((1, 128), jnp.sum(error), F32)
    for i in range(SAMPLES):
        out[i] = share


VMEM = pl.BlockSpec(memory_space=pltpu.VMEM)
SMEM = pl.BlockSpec(memory_space=pltpu.SMEM)
HBM = pl.BlockSpec(memory_space=pltpu.HBM)
LIMIT = pltpu.CompilerParams(vmem_limit_bytes=32 * 1024 * 1024)
PRODUCT = pl.CostEstimate(
    flops=2 * K * ROWS * COLS, bytes_accessed=2 * ROWS * COLS, transcendentals=0
)
ENERGY = pl.CostEstimate(flops=2 * ROWS * COLS, bytes_accessed=2 * ROWS * COLS, transcendentals=0)


def call(kernel, inputs, outs, cost=None, specs=None, scratch=()):
    return pl.pallas_call(
        kernel,
        out_shape=[jax.ShapeDtypeStruct(shape, dtype) for shape, dtype in outs],
        in_specs=[VMEM] * len(inputs) if specs is None else specs,
        out_specs=[VMEM] * len(outs),
        scratch_shapes=list(scratch),
        compiler_params=LIMIT,
        cost_estimate=cost,
    )(*inputs)


def exchange(x, axis):
    return lax.all_to_all(x, axis, 0, 0, tiled=True)


def sum_everywhere(shares):
    part = jnp.sum(exchange(shares, "samples"), axis=0)
    part = exchange(jnp.broadcast_to(part[None], (CHIPS, 1, 128)), "chips")
    return jnp.sum(part, axis=0)


def body(telemetry, chip_factors, sample_factors):
    me = jnp.stack([lax.axis_index("chips"), lax.axis_index("samples")])
    tile = pltpu.VMEM((ROWS, COLS), BF16)
    w, h = chip_factors.T, sample_factors.T
    w_sent = ((SAMPLES, W_MSG, 128), BF16)
    (sent,) = call(start_kernel, (me, w), [w_sent], None, [SMEM, VMEM])
    got_w = exchange(sent, "samples")
    (energy,) = call(energy_kernel, (telemetry,), [((1, 128), F32)], ENERGY)
    for sweep in range(ITERS):
        last = sweep == ITERS - 1
        (sent,) = call(
            h_numer_kernel,
            (me, got_w, telemetry),
            [((CHIPS, H_MSG, 128), BF16)],
            PRODUCT,
            [SMEM, VMEM, HBM],
            [
                tile,
                pltpu.VMEM((K, ROWS), BF16),
                pltpu.VMEM((ROWS, K), F32),
                pltpu.SemaphoreType.DMA,
            ],
        )
        got = exchange(sent, "chips")
        h, sent = call(
            h_update_kernel, (got, h), [((H_OWN, K), F32), ((CHIPS, H_OWN, 128), BF16)]
        )
        got_h = exchange(sent, "chips")
        (sent,) = call(
            w_numer_kernel,
            (me, got_h, telemetry),
            [((SAMPLES, W_MSG + PAIR if last else W_MSG, 128), BF16)],
            PRODUCT,
            [SMEM, VMEM, HBM],
            [tile, pltpu.SemaphoreType.DMA((SAMPLES // W_STEP,))],
        )
        got = exchange(sent, "samples")
        if not last:
            w, sent = call(
                w_update_kernel,
                (me, got, w),
                [((W_OWN, K), F32), w_sent],
                None,
                [SMEM, VMEM, VMEM],
            )
            got_w = exchange(sent, "samples")
    w, shares = call(
        w_last_kernel, (got, w, energy), [((W_OWN, K), F32), ((SAMPLES, 1, 128), F32)]
    )
    sums = sum_everywhere(shares)
    total = sums[0, K]
    expanded = sums[0, 0] + total

    def direct(w, got_h, telemetry):
        (sent,) = call(last_rows_kernel, (w,), [((SAMPLES, W_HALF, 128), BF16)])
        (shares,) = call(
            error_kernel,
            (exchange(sent, "samples"), got_h, telemetry),
            [((SAMPLES, 1, 128), F32)],
            PRODUCT,
        )
        return sum_everywhere(shares)[0, 0]

    fit_error = lax.cond(
        expanded < 0.02 * total,
        direct,
        lambda *operands: expanded,
        w,
        got_h,
        telemetry,
    )
    return w.T, h.T, jnp.sqrt(fit_error / total)


def solution(mesh):
    return jax.shard_map(
        body,
        mesh=mesh,
        in_specs=(
            P("chips", "samples"),
            P(None, ("chips", "samples")),
            P(None, ("samples", "chips")),
        ),
        out_specs=(P(None, ("chips", "samples")), P(None, ("samples", "chips")), P()),
        check_vma=False,
    )
```

```python
import jax
import jax.numpy as jnp
from jax import lax
from jax.experimental import pallas as pl
from jax.experimental.pallas import tpu as pltpu
from jax.sharding import PartitionSpec as P

ITERS = 2

epsilon = 1e-09

F32 = jnp.float32
BF16 = jnp.bfloat16
HIGHEST = lax.Precision.HIGHEST

K = 64
CHIPS = 32
SAMPLES = 16
ROWS = 2304
COLS = 1024
W_OWN = ROWS // SAMPLES
H_OWN = COLS // CHIPS
H_WIDTH = 256
W_STEP = 16
BLOCK = 16
W_HALF = 80
GRAM = 16
W_MSG = W_HALF + GRAM
PAIR = 32
H_MSG = BLOCK + GRAM + 8
LEFT = W_HALF // BLOCK
W_BLOCKS = W_OWN // BLOCK


def split(x):
    high = x.astype(BF16).astype(F32)
    return jnp.concatenate([high, x - high], axis=1).astype(BF16)


def join(x):
    return x[:, :K] + x[:, K:]


def squares():
    row = lax.broadcasted_iota(jnp.int32, (32, 32), 0)
    col = lax.broadcasted_iota(jnp.int32, (32, 32), 1)
    return row, col


TOP = 6.0


def peak(x):
    return jnp.max(jnp.max(x, axis=0, keepdims=True), axis=1, keepdims=True)


def power_of(largest):
    return jnp.floor(jnp.log2(jnp.maximum(largest, 1e-30)))


def sixteenth(x):
    x = x * x
    x = x * x
    x = x * x
    return x * x


def code(x, power, factor):
    return sixteenth(x * (jnp.exp2(TOP - power) * factor))


def root(x):
    return lax.rsqrt(lax.rsqrt(lax.rsqrt(lax.rsqrt(jnp.abs(x)))))


def scale_of(power, factor):
    return jnp.exp2(power - TOP) / factor


def copies(message, out):
    def step(i, carry):
        out[i] = message
        return carry

    lax.fori_loop(0, out.shape[0], step, 0, unroll=True)


def sample_factor(i):
    return 1.0 + jnp.full((1, 1), i, jnp.int32).astype(F32) * (1.0 / 32.0)


def chip_factor(i):
    return 1.0 + jnp.full((1, 1), i, jnp.int32).astype(F32) * (1.0 / 64.0)


def gram_parts(gram):
    row, col = squares()
    first, block, last = gram[:32, :32], gram[:32, 32:], gram[32:, 32:]
    parts = jnp.concatenate([jnp.where(row <= col, first, last), block], axis=1)
    return parts, jnp.sum(jnp.where(row == col, last, 0.0), axis=0, keepdims=True)


def gram_whole(parts, diagonal):
    row, col = squares()
    mixed, block = parts[:, :32], parts[:, 32:]
    turned = lax.dot_general(
        (row == col).astype(F32),
        jnp.concatenate([mixed, block], axis=0),
        (((1,), (1,)), ((), ())),
        precision=HIGHEST,
        preferred_element_type=F32,
    )
    mixed_t, block_t = turned[:, :32], turned[:, 32:]
    one = jnp.where(row <= col, mixed, mixed_t)
    two = jnp.where(row > col, mixed, jnp.where(row < col, mixed_t, diagonal))
    return jnp.concatenate(
        [jnp.concatenate([one, block], axis=1), jnp.concatenate([block_t, two], axis=1)], axis=0
    )


def encode_gram(parts, diagonal, factor):
    power = power_of(jnp.maximum(peak(parts), peak(diagonal)))
    coded = code(parts, power, factor)
    return (
        jnp.concatenate([coded[:GRAM], coded[GRAM:]], axis=1),
        code(diagonal, power, factor),
        power,
    )


def one_above(x):
    return jnp.concatenate([x[:, :K], x[:, K:]], axis=0)


def pair_of(gram):
    row, col = squares()
    parts, diagonal = gram_parts(gram)
    high = parts.astype(BF16).astype(F32)
    low = parts - high
    own = row == col
    first = jnp.where(own, parts[:, :32], high[:, :32])
    third = jnp.where(own, diagonal, low[:, :32])
    return jnp.concatenate([first, high[:, 32:], third, low[:, 32:]], axis=1).astype(BF16)


def of_pair(total):
    row, col = squares()
    own = row == col
    first, third = total[:, :32], total[:, 64:96]
    mixed = jnp.where(own, first, first + third)
    diagonal = jnp.sum(jnp.where(own, third, 0.0), axis=0, keepdims=True)
    block = total[:, 32:64] + total[:, 96:]
    return gram_whole(jnp.concatenate([mixed, block], axis=1), diagonal)


def products(halves):
    return lax.dot_general(halves, halves, (((0,), (0,)), ((), ())), preferred_element_type=F32)


def quarters(four):
    two = four[:K] + four[K:]
    return two[:, :K] + two[:, K:]


def spare_rows(left, right, diagonal, power):
    return jnp.concatenate(
        [
            jnp.broadcast_to(left, (LEFT, K)),
            jnp.broadcast_to(right, (LEFT - 1, K)),
            jnp.broadcast_to(power, (1, K)),
            jnp.concatenate([diagonal, jnp.zeros((1, K - 32), F32)], axis=1),
            jnp.zeros((BLOCK - W_BLOCKS - 2, K), F32),
        ],
        axis=0,
    )


def w_message(w, gram):
    coded, diagonal, power = gram
    none = jnp.zeros((LEFT, 1), F32)
    right = jnp.concatenate(
        [w[W_HALF:], spare_rows(none, none[1:], diagonal, power)], axis=0
    )
    return jnp.concatenate(
        [jnp.concatenate([w[:W_HALF], right], axis=1), coded], axis=0
    ).astype(BF16)


def sums_message(sums, gram, factor):
    coded, diagonal, power = gram
    both = jnp.concatenate(
        [sums[:W_HALF], jnp.concatenate([sums[W_HALF:], jnp.zeros((BLOCK, K), F32)], axis=0)],
        axis=1,
    )
    blocks = [both[j * BLOCK : (j + 1) * BLOCK] for j in range(LEFT)]
    largest = jnp.concatenate(
        [jnp.max(x, axis=0, keepdims=True) for x in blocks] + [jnp.zeros((8 - LEFT, 128), F32)],
        axis=0,
    )
    lane = lax.broadcasted_iota(jnp.int32, (8, 128), 1)
    left = power_of(jnp.max(jnp.where(lane < K, largest, 0.0), axis=1, keepdims=True))
    right = power_of(jnp.max(jnp.where(lane < K, 0.0, largest), axis=1, keepdims=True))
    powers = jnp.where(lane < K, left, right)
    scale = jnp.exp2(TOP - powers) * factor
    blocks = [sixteenth(x * scale[j : j + 1]) for j, x in enumerate(blocks)]
    free = jnp.concatenate(
        [blocks[-1][:, :K], spare_rows(left[:LEFT], right[: LEFT - 1], diagonal, power)], axis=1
    )
    return jnp.concatenate(blocks[:-1] + [free, coded], axis=0).astype(BF16)


def read_gram(message, factor):
    roots = root(message)
    scale = scale_of(message[W_BLOCKS : W_BLOCKS + 1, 127:], factor)
    return roots[BLOCK:] * scale, roots[W_BLOCKS + 1 : W_BLOCKS + 2] * scale


def read_sums(message, factor):
    lane = lax.broadcasted_iota(jnp.int32, (BLOCK, 128), 1)
    scale = scale_of(message[W_HALF - BLOCK :, 127:], factor)
    roots = root(message)
    return [
        roots[j * BLOCK : (j + 1) * BLOCK]
        * jnp.where(lane < K, scale[j : j + 1], scale[LEFT + j : LEFT + j + 1])
        for j in range(LEFT)
    ]


def one_column(both):
    return jnp.concatenate([both[:, :K], both[: W_OWN - W_HALF, K:]], axis=0)


def fill_w(w, factor, out):
    gram = gram_parts(quarters(products(split(w))))
    copies(w_message(w, encode_gram(*gram, factor)), out)


def start_kernel(me, w, w_out, out):
    wide = jnp.concatenate([w[...], jnp.zeros((K, 256 - W_OWN), F32)], axis=1)
    turned = wide.T[:W_OWN]
    w_out[...] = turned
    fill_w(turned, sample_factor(me[1]), out)


def h_numer_kernel(me, got, tel, out, tile, w_turned, w_all, arrived):
    copy = pltpu.make_async_copy(tel, tile, arrived)
    copy.start()

    def gather(i, carry):
        gram, diagonal = carry
        message = got[i].astype(F32)
        w_all[pl.ds(pl.multiple_of(i * W_OWN, BLOCK), W_OWN), :] = one_column(message[:W_HALF])
        more, ends = read_gram(message[W_HALF - BLOCK :], sample_factor(i))
        return gram + more, diagonal + ends

    zero = (jnp.zeros((GRAM, 128), F32), jnp.zeros((1, 128), F32))
    gram, diagonal = lax.fori_loop(0, SAMPLES, gather, zero, unroll=True)

    def turn(j, carry):
        at = pl.ds(pl.multiple_of(j * 128, 128), 128)
        w_turned[:, at] = w_all[at, :].T.astype(BF16)
        return carry

    lax.fori_loop(0, ROWS // 128, turn, 0, unroll=True)
    factor = chip_factor(me[0])
    coded, ends, power = encode_gram(one_above(gram), diagonal[:, K : K + 32], factor)
    ends = jnp.concatenate([ends, jnp.zeros((1, 96), F32)], axis=1)
    power = jnp.broadcast_to(power, (1, 128))
    copy.wait()
    per = H_WIDTH // H_OWN

    def step(n, carry):
        cols = pl.ds(pl.multiple_of(n * H_WIDTH, H_WIDTH), H_WIDTH)
        part = jnp.dot(w_turned[...], tile[:, cols], preferred_element_type=F32).T
        for q in range(per):
            halves = [part[q * H_OWN + r : q * H_OWN + r + BLOCK] for r in (0, BLOCK)]
            powers = [power_of(peak(x)) for x in halves]
            out[n * per + q] = jnp.concatenate(
                [
                    jnp.concatenate([code(x, p, factor) for x, p in zip(halves, powers)], axis=1),
                    coded,
                    ends,
                    power,
                    jnp.broadcast_to(powers[0], (1, 128)),
                    jnp.broadcast_to(powers[1], (1, 128)),
                    jnp.zeros((4, 128), F32),
                ],
                axis=0,
            ).astype(BF16)
        return carry

    lax.fori_loop(0, COLS // H_WIDTH, step, 0, unroll=True)


def h_update_kernel(got, h, h_out, out):
    lane = lax.broadcasted_iota(jnp.int32, (BLOCK, 128), 1)

    def add(i, carry):
        numer, gram, diagonal = carry
        message = got[i].astype(F32)
        roots = root(message)
        scales = scale_of(message[H_MSG - 8 :, 127:], chip_factor(i))
        numer += roots[:BLOCK] * jnp.where(lane < K, scales[2:3], scales[3:4])
        gram += roots[BLOCK : BLOCK + GRAM] * scales[1:2]
        diagonal += roots[H_MSG - 8 : H_MSG - 7] * scales[1:2]
        return numer, gram, diagonal

    zero = jnp.zeros((BLOCK, 128), F32)
    numer, gram, diagonal = lax.fori_loop(
        0, CHIPS, add, (zero, zero, jnp.zeros((1, 128), F32)), unroll=True
    )
    gram = gram_whole(one_above(gram), diagonal[:, :32])
    old = h[...]
    below = jnp.dot(old, gram, precision=HIGHEST, preferred_element_type=F32) + epsilon
    new = old * one_above(numer) / below
    h_out[...] = new
    copies(split(new), out)


def w_numer_kernel(me, got, tel, out, tile, arrived):
    block = W_STEP * W_OWN

    def copy(b):
        rows = pl.ds(pl.multiple_of(b * block, block), block)
        return pltpu.make_async_copy(tel.at[rows], tile.at[rows], arrived.at[b])

    for b in range(ROWS // block):
        copy(b).start()
    halves = got[...].reshape(COLS, 128)
    four = products(halves)
    factor = sample_factor(me[1])
    gram = encode_gram(*gram_parts(quarters(four)), factor)
    last = out.shape[1] > W_MSG
    if last:
        pair = pair_of(four[:K, :K])
    high = halves[:, :K]

    def step(b, carry):
        copy(b).wait()
        rows = pl.ds(pl.multiple_of(b * block, block), block)
        part = jnp.dot(tile[rows, :], high, preferred_element_type=F32)
        for q in range(W_STEP):
            message = sums_message(part[q * W_OWN : (q + 1) * W_OWN], gram, factor)
            if last:
                message = jnp.concatenate([message, pair], axis=0)
            out[b * W_STEP + q] = message
        return carry

    lax.fori_loop(0, ROWS // block, step, 0)


def w_new(got, w):
    last = got.shape[1] > W_MSG

    def add(i, carry):
        blocks, gram, diagonal, rest = carry
        message = got[i].astype(F32)
        terms = read_sums(message[:W_HALF], sample_factor(i))
        more, ends = read_gram(message[W_HALF - BLOCK : W_MSG], sample_factor(i))
        if last:
            rest += message[W_MSG:]
        blocks = tuple(total + term for total, term in zip(blocks, terms))
        return blocks, gram + more, diagonal + ends, rest

    zero = jnp.zeros((BLOCK, 128), F32)
    blocks, gram, diagonal, rest = lax.fori_loop(
        0,
        SAMPLES,
        add,
        ((zero,) * LEFT, zero, jnp.zeros((1, 128), F32), jnp.zeros((PAIR, 128), F32)),
        unroll=True,
    )
    numer = one_column(jnp.concatenate(blocks, axis=0))
    gram = gram_whole(one_above(gram), diagonal[:, K : K + 32])
    old = w[...]
    below = jnp.dot(old, gram, precision=HIGHEST, preferred_element_type=F32) + epsilon
    return old * numer / below, numer, rest


def w_update_kernel(me, got, w, w_out, out):
    new, _, _ = w_new(got, w)
    w_out[...] = new
    fill_w(new, sample_factor(me[1]), out)


def w_last_kernel(got, w, energy, w_out, out):
    new, numer, rest = w_new(got, w)
    w_out[...] = new
    rounded = new.astype(BF16).astype(F32)
    gram = of_pair(rest)
    fitted = jnp.dot(rounded, gram, precision=HIGHEST, preferred_element_type=F32)
    share = jnp.sum(rounded * (fitted - 2.0 * numer))
    lane = lax.broadcasted_iota(jnp.int32, (1, 128), 1)
    pair = jnp.where(lane < K, share, energy[...])
    copies(pair, out)


def energy_kernel(tel, out):
    def step(i, energy):
        rows = pl.ds(pl.multiple_of(i * W_OWN, W_OWN), W_OWN)
        values = tel[rows, :].astype(F32)
        return energy + jnp.sum((values * values).reshape(W_OWN // 8, 8, COLS), axis=0)

    energy = lax.fori_loop(0, SAMPLES, step, jnp.zeros((8, COLS), F32))
    out[...] = jnp.full((1, 128), jnp.sum(energy), F32)


def last_rows_kernel(w, out):
    rows = w[...]
    right = jnp.concatenate([rows[W_HALF:], jnp.zeros((BLOCK, K), F32)], axis=0)
    message = jnp.concatenate([rows[:W_HALF], right], axis=1).astype(BF16)
    copies(message, out)


def error_kernel(got_w, got_h, tel, out):
    high = got_h[...].reshape(COLS, 128)[:, :K]

    def step(i, error):
        rows = pl.ds(pl.multiple_of(i * W_OWN, W_OWN), W_OWN)
        rebuilt = lax.dot_general(
            one_column(got_w[i].astype(F32)).astype(BF16),
            high,
            (((1,), (1,)), ((), ())),
            preferred_element_type=F32,
        )
        difference = tel[rows, :].astype(F32) - rebuilt
        return error + jnp.sum((difference * difference).reshape(W_OWN // 8, 8, COLS), axis=0)

    error = lax.fori_loop(0, SAMPLES, step, jnp.zeros((8, COLS), F32))
    share = jnp.full((1, 128), jnp.sum(error), F32)
    copies(share, out)


VMEM = pl.BlockSpec(memory_space=pltpu.VMEM)
SMEM = pl.BlockSpec(memory_space=pltpu.SMEM)
HBM = pl.BlockSpec(memory_space=pltpu.HBM)
LIMIT = pltpu.CompilerParams(vmem_limit_bytes=32 * 1024 * 1024)
PRODUCT = pl.CostEstimate(
    flops=2 * K * ROWS * COLS, bytes_accessed=2 * ROWS * COLS, transcendentals=0
)
ENERGY = pl.CostEstimate(flops=2 * ROWS * COLS, bytes_accessed=2 * ROWS * COLS, transcendentals=0)


def call(kernel, inputs, outs, cost=None, specs=None, scratch=()):
    return pl.pallas_call(
        kernel,
        out_shape=[jax.ShapeDtypeStruct(shape, dtype) for shape, dtype in outs],
        in_specs=[VMEM] * len(inputs) if specs is None else specs,
        out_specs=[VMEM] * len(outs),
        scratch_shapes=list(scratch),
        compiler_params=LIMIT,
        cost_estimate=cost,
    )(*inputs)


def exchange(x, axis):
    return lax.all_to_all(x, axis, 0, 0, tiled=True)


def sum_everywhere(shares):
    part = jnp.sum(exchange(shares, "samples"), axis=0)
    part = exchange(jnp.broadcast_to(part[None], (CHIPS, 1, 128)), "chips")
    return jnp.sum(part, axis=0)


def body(telemetry, chip_factors, sample_factors):
    me = jnp.stack([lax.axis_index("chips"), lax.axis_index("samples")])
    tile = pltpu.VMEM((ROWS, COLS), BF16)
    h = sample_factors.T
    w_sent = [((W_OWN, K), F32), ((SAMPLES, W_MSG, 128), BF16)]
    w, sent = call(start_kernel, (me, chip_factors), w_sent, None, [SMEM, VMEM])
    got_w = exchange(sent, "samples")
    (energy,) = call(energy_kernel, (telemetry,), [((1, 128), F32)], ENERGY)
    for sweep in range(ITERS):
        last = sweep == ITERS - 1
        (sent,) = call(
            h_numer_kernel,
            (me, got_w, telemetry),
            [((CHIPS, H_MSG, 128), BF16)],
            PRODUCT,
            [SMEM, VMEM, HBM],
            [
                tile,
                pltpu.VMEM((K, ROWS), BF16),
                pltpu.VMEM((ROWS, K), F32),
                pltpu.SemaphoreType.DMA,
            ],
        )
        got = exchange(sent, "chips")
        h, sent = call(
            h_update_kernel, (got, h), [((H_OWN, K), F32), ((CHIPS, H_OWN, 128), BF16)]
        )
        got_h = exchange(sent, "chips")
        (sent,) = call(
            w_numer_kernel,
            (me, got_h, telemetry),
            [((SAMPLES, W_MSG + PAIR if last else W_MSG, 128), BF16)],
            PRODUCT,
            [SMEM, VMEM, HBM],
            [tile, pltpu.SemaphoreType.DMA((SAMPLES // W_STEP,))],
        )
        got = exchange(sent, "samples")
        if not last:
            w, sent = call(
                w_update_kernel,
                (me, got, w),
                w_sent,
                None,
                [SMEM, VMEM, VMEM],
            )
            got_w = exchange(sent, "samples")
    w, shares = call(
        w_last_kernel, (got, w, energy), [((W_OWN, K), F32), ((SAMPLES, 1, 128), F32)]
    )
    sums = sum_everywhere(shares)
    total = sums[0, K]
    expanded = sums[0, 0] + total

    def direct(w, got_h, telemetry):
        (sent,) = call(last_rows_kernel, (w,), [((SAMPLES, W_HALF, 128), BF16)])
        (shares,) = call(
            error_kernel,
            (exchange(sent, "samples"), got_h, telemetry),
            [((SAMPLES, 1, 128), F32)],
            PRODUCT,
        )
        return sum_everywhere(shares)[0, 0]

    fit_error = lax.cond(
        expanded < 0.02 * total,
        direct,
        lambda *operands: expanded,
        w,
        got_h,
        telemetry,
    )
    return w.T, h.T, jnp.sqrt(fit_error / total)


def solution(mesh):
    return jax.shard_map(
        body,
        mesh=mesh,
        in_specs=(
            P("chips", "samples"),
            P(None, ("chips", "samples")),
            P(None, ("samples", "chips")),
        ),
        out_specs=(P(None, ("chips", "samples")), P(None, ("samples", "chips")), P()),
        check_vma=False,
    )
```

```python
import jax
import jax.numpy as jnp
from jax import lax
from jax.experimental import pallas as pl
from jax.experimental.pallas import tpu as pltpu
from jax.sharding import PartitionSpec as P

ITERS = 2

epsilon = 1e-09

F32 = jnp.float32
BF16 = jnp.bfloat16
HIGHEST = lax.Precision.HIGHEST

K = 64
CHIPS = 32
SAMPLES = 16
ROWS = 2304
COLS = 1024
W_OWN = ROWS // SAMPLES
H_OWN = COLS // CHIPS
H_WIDTH = 256
PARTS = 2
TOUCH = 1152
BLOCK = 16
W_HALF = 80
GRAM = 16
W_MSG = W_HALF + GRAM
PAIR = 32
H_MSG = BLOCK + GRAM + 8
LEFT = W_HALF // BLOCK
W_BLOCKS = W_OWN // BLOCK


def split(x):
    high = x.astype(BF16).astype(F32)
    return jnp.concatenate([high, x - high], axis=1).astype(BF16)


def join(x):
    return x[:, :K] + x[:, K:]


def squares():
    row = lax.broadcasted_iota(jnp.int32, (32, 32), 0)
    col = lax.broadcasted_iota(jnp.int32, (32, 32), 1)
    return row, col


TOP = 6.0


def peak(x):
    return jnp.max(jnp.max(x, axis=0, keepdims=True), axis=1, keepdims=True)


def power_of(largest):
    return jnp.floor(jnp.log2(jnp.maximum(largest, 1e-30)))


def sixteenth(x):
    x = x * x
    x = x * x
    x = x * x
    return x * x


def code(x, power, factor):
    return sixteenth(x * (jnp.exp2(TOP - power) * factor))


def root(x):
    return lax.rsqrt(lax.rsqrt(lax.rsqrt(lax.rsqrt(jnp.abs(x)))))


def scale_of(power, factor):
    return jnp.exp2(power - TOP) / factor


def copies(message, out):
    def step(i, carry):
        out[i] = message
        return carry

    lax.fori_loop(0, out.shape[0], step, 0, unroll=True)


def sample_factor(i):
    return 1.0 + jnp.full((1, 1), i, jnp.int32).astype(F32) * (1.0 / 32.0)


def chip_factor(i):
    return 1.0 + jnp.full((1, 1), i, jnp.int32).astype(F32) * (1.0 / 64.0)


def gram_parts(gram):
    row, col = squares()
    first, block, last = gram[:32, :32], gram[:32, 32:], gram[32:, 32:]
    parts = jnp.concatenate([jnp.where(row <= col, first, last), block], axis=1)
    return parts, jnp.sum(jnp.where(row == col, last, 0.0), axis=0, keepdims=True)


def gram_whole(parts, diagonal):
    row, col = squares()
    mixed, block = parts[:, :32], parts[:, 32:]
    turned = lax.dot_general(
        (row == col).astype(F32),
        jnp.concatenate([mixed, block], axis=0),
        (((1,), (1,)), ((), ())),
        precision=HIGHEST,
        preferred_element_type=F32,
    )
    mixed_t, block_t = turned[:, :32], turned[:, 32:]
    one = jnp.where(row <= col, mixed, mixed_t)
    two = jnp.where(row > col, mixed, jnp.where(row < col, mixed_t, diagonal))
    return jnp.concatenate(
        [jnp.concatenate([one, block], axis=1), jnp.concatenate([block_t, two], axis=1)], axis=0
    )


def encode_gram(parts, diagonal, factor):
    power = power_of(jnp.maximum(peak(parts), peak(diagonal)))
    coded = code(parts, power, factor)
    return (
        jnp.concatenate([coded[:GRAM], coded[GRAM:]], axis=1),
        code(diagonal, power, factor),
        power,
    )


def one_above(x):
    return jnp.concatenate([x[:, :K], x[:, K:]], axis=0)


def pair_of(gram):
    row, col = squares()
    parts, diagonal = gram_parts(gram)
    high = parts.astype(BF16).astype(F32)
    low = parts - high
    own = row == col
    first = jnp.where(own, parts[:, :32], high[:, :32])
    third = jnp.where(own, diagonal, low[:, :32])
    return jnp.concatenate([first, high[:, 32:], third, low[:, 32:]], axis=1).astype(BF16)


def of_pair(total):
    row, col = squares()
    own = row == col
    first, third = total[:, :32], total[:, 64:96]
    mixed = jnp.where(own, first, first + third)
    diagonal = jnp.sum(jnp.where(own, third, 0.0), axis=0, keepdims=True)
    block = total[:, 32:64] + total[:, 96:]
    return gram_whole(jnp.concatenate([mixed, block], axis=1), diagonal)


def products(halves):
    return lax.dot_general(halves, halves, (((0,), (0,)), ((), ())), preferred_element_type=F32)


def quarters(four):
    two = four[:K] + four[K:]
    return two[:, :K] + two[:, K:]


def spare_rows(left, right, diagonal, power):
    return jnp.concatenate(
        [
            jnp.broadcast_to(left, (LEFT, K)),
            jnp.broadcast_to(right, (LEFT - 1, K)),
            jnp.broadcast_to(power, (1, K)),
            jnp.concatenate([diagonal, jnp.zeros((1, K - 32), F32)], axis=1),
            jnp.zeros((BLOCK - W_BLOCKS - 2, K), F32),
        ],
        axis=0,
    )


def w_message(w, gram):
    coded, diagonal, power = gram
    none = jnp.zeros((LEFT, 1), F32)
    right = jnp.concatenate(
        [w[W_HALF:], spare_rows(none, none[1:], diagonal, power)], axis=0
    )
    return jnp.concatenate(
        [jnp.concatenate([w[:W_HALF], right], axis=1), coded], axis=0
    ).astype(BF16)


def sums_message(sums, gram, factor):
    coded, diagonal, power = gram
    both = jnp.concatenate(
        [sums[:W_HALF], jnp.concatenate([sums[W_HALF:], jnp.zeros((BLOCK, K), F32)], axis=0)],
        axis=1,
    )
    blocks = [both[j * BLOCK : (j + 1) * BLOCK] for j in range(LEFT)]
    largest = jnp.concatenate(
        [jnp.max(x, axis=0, keepdims=True) for x in blocks] + [jnp.zeros((8 - LEFT, 128), F32)],
        axis=0,
    )
    lane = lax.broadcasted_iota(jnp.int32, (8, 128), 1)
    left = power_of(jnp.max(jnp.where(lane < K, largest, 0.0), axis=1, keepdims=True))
    right = power_of(jnp.max(jnp.where(lane < K, 0.0, largest), axis=1, keepdims=True))
    powers = jnp.where(lane < K, left, right)
    scale = jnp.exp2(TOP - powers) * factor
    blocks = [sixteenth(x * scale[j : j + 1]) for j, x in enumerate(blocks)]
    free = jnp.concatenate(
        [blocks[-1][:, :K], spare_rows(left[:LEFT], right[: LEFT - 1], diagonal, power)], axis=1
    )
    return jnp.concatenate(blocks[:-1] + [free, coded], axis=0).astype(BF16)


def read_gram(message, factor):
    roots = root(message)
    scale = scale_of(message[W_BLOCKS : W_BLOCKS + 1, 127:], factor)
    return roots[BLOCK:] * scale, roots[W_BLOCKS + 1 : W_BLOCKS + 2] * scale


def read_sums(message, factor):
    lane = lax.broadcasted_iota(jnp.int32, (BLOCK, 128), 1)
    scale = scale_of(message[W_HALF - BLOCK :, 127:], factor)
    roots = root(message)
    return [
        roots[j * BLOCK : (j + 1) * BLOCK]
        * jnp.where(lane < K, scale[j : j + 1], scale[LEFT + j : LEFT + j + 1])
        for j in range(LEFT)
    ]


def one_column(both):
    return jnp.concatenate([both[:, :K], both[: W_OWN - W_HALF, K:]], axis=0)


def fill_w(w, factor, out):
    gram = gram_parts(quarters(products(split(w))))
    copies(w_message(w, encode_gram(*gram, factor)), out)


def start_kernel(me, w, tel, w_out, out, touched, arrived, own, own_arrived):
    touches = [
        pltpu.make_async_copy(
            tel.at[pl.ds(j * TOUCH, BLOCK)], touched.at[pl.ds(j * BLOCK, BLOCK)], arrived.at[j]
        )
        for j in range(ROWS // TOUCH)
    ]
    own_copy = pltpu.make_async_copy(w, own, own_arrived)
    own_copy.start()
    for copy in touches:
        copy.start()
    own_copy.wait()
    wide = jnp.concatenate([own[...], jnp.zeros((K, 256 - W_OWN), F32)], axis=1)
    turned = wide.T[:W_OWN]
    w_out[...] = turned
    fill_w(turned, sample_factor(me[1]), out)
    for copy in touches:
        copy.wait()


def h_numer_kernel(me, got, tel, out, tile, w_turned, w_all, arrived):
    copy = pltpu.make_async_copy(tel, tile, arrived)
    copy.start()

    def gather(i, carry):
        gram, diagonal = carry
        message = got[i].astype(F32)
        w_all[pl.ds(pl.multiple_of(i * W_OWN, BLOCK), W_OWN), :] = one_column(message[:W_HALF])
        more, ends = read_gram(message[W_HALF - BLOCK :], sample_factor(i))
        return gram + more, diagonal + ends

    zero = (jnp.zeros((GRAM, 128), F32), jnp.zeros((1, 128), F32))
    gram, diagonal = lax.fori_loop(0, SAMPLES, gather, zero, unroll=True)

    def turn(j, carry):
        at = pl.ds(pl.multiple_of(j * 128, 128), 128)
        w_turned[:, at] = w_all[at, :].T.astype(BF16)
        return carry

    lax.fori_loop(0, ROWS // 128, turn, 0, unroll=True)
    factor = chip_factor(me[0])
    coded, ends, power = encode_gram(one_above(gram), diagonal[:, K : K + 32], factor)
    ends = jnp.concatenate([ends, jnp.zeros((1, 96), F32)], axis=1)
    power = jnp.broadcast_to(power, (1, 128))
    copy.wait()
    per = H_WIDTH // H_OWN

    def step(n, carry):
        cols = pl.ds(pl.multiple_of(n * H_WIDTH, H_WIDTH), H_WIDTH)
        part = jnp.dot(w_turned[...], tile[:, cols], preferred_element_type=F32).T
        for q in range(per):
            halves = [part[q * H_OWN + r : q * H_OWN + r + BLOCK] for r in (0, BLOCK)]
            powers = [power_of(peak(x)) for x in halves]
            out[n * per + q] = jnp.concatenate(
                [
                    jnp.concatenate([code(x, p, factor) for x, p in zip(halves, powers)], axis=1),
                    coded,
                    ends,
                    power,
                    jnp.broadcast_to(powers[0], (1, 128)),
                    jnp.broadcast_to(powers[1], (1, 128)),
                    jnp.zeros((4, 128), F32),
                ],
                axis=0,
            ).astype(BF16)
        return carry

    lax.fori_loop(0, COLS // H_WIDTH, step, 0, unroll=True)


def h_update_kernel(got, h, h_out, out):
    lane = lax.broadcasted_iota(jnp.int32, (BLOCK, 128), 1)

    def add(i, carry):
        numer, gram, diagonal = carry
        message = got[i].astype(F32)
        roots = root(message)
        scales = scale_of(message[H_MSG - 8 :, 127:], chip_factor(i))
        numer += roots[:BLOCK] * jnp.where(lane < K, scales[2:3], scales[3:4])
        gram += roots[BLOCK : BLOCK + GRAM] * scales[1:2]
        diagonal += roots[H_MSG - 8 : H_MSG - 7] * scales[1:2]
        return numer, gram, diagonal

    zero = jnp.zeros((BLOCK, 128), F32)
    numer, gram, diagonal = lax.fori_loop(
        0, CHIPS, add, (zero, zero, jnp.zeros((1, 128), F32)), unroll=True
    )
    gram = gram_whole(one_above(gram), diagonal[:, :32])
    old = h[...]
    below = jnp.dot(old, gram, precision=HIGHEST, preferred_element_type=F32) + epsilon
    new = old * one_above(numer) / below
    h_out[...] = new
    copies(split(new), out)


def w_numer(me, got, tel, out, tile, arrived, energy=None):
    parts = arrived.shape[0]
    block = ROWS // parts
    copies_in = [
        pltpu.make_async_copy(
            tel.at[pl.ds(b * block, block)], tile.at[pl.ds(b * block, block)], arrived.at[b]
        )
        for b in range(parts)
    ]
    for copy in copies_in:
        copy.start()
    halves = got[...].reshape(COLS, 128)
    four = products(halves)
    factor = sample_factor(me[1])
    gram = encode_gram(*gram_parts(quarters(four)), factor)
    last = out.shape[1] > W_MSG
    if last:
        pair = pair_of(four[:K, :K])
    squares_sum = jnp.zeros((8, COLS), F32)
    for b, copy in enumerate(copies_in):
        copy.wait()
        if energy is not None:

            def add(i, total):
                rows = pl.ds(pl.multiple_of(b * block + i * W_OWN, W_OWN), W_OWN)
                values = tile[rows, :].astype(F32)
                return total + jnp.sum((values * values).reshape(W_OWN // 8, 8, COLS), axis=0)

            squares_sum = lax.fori_loop(0, block // W_OWN, add, squares_sum)
    if energy is not None:
        energy[...] = jnp.full((1, 128), jnp.sum(squares_sum), F32)
    sums = jnp.dot(tile[...], halves[:, :K], preferred_element_type=F32)
    for q in range(SAMPLES):
        message = sums_message(sums[q * W_OWN : (q + 1) * W_OWN], gram, factor)
        if last:
            message = jnp.concatenate([message, pair], axis=0)
        out[q] = message


def w_numer_kernel(me, got, tel, out, tile, arrived):
    w_numer(me, got, tel, out, tile, arrived)


def w_numer_energy_kernel(me, got, tel, out, energy, tile, arrived):
    w_numer(me, got, tel, out, tile, arrived, energy)


def w_new(got, w):
    last = got.shape[1] > W_MSG

    def add(i, carry):
        blocks, gram, diagonal, rest = carry
        message = got[i].astype(F32)
        terms = read_sums(message[:W_HALF], sample_factor(i))
        more, ends = read_gram(message[W_HALF - BLOCK : W_MSG], sample_factor(i))
        if last:
            rest += message[W_MSG:]
        blocks = tuple(total + term for total, term in zip(blocks, terms))
        return blocks, gram + more, diagonal + ends, rest

    zero = jnp.zeros((BLOCK, 128), F32)
    blocks, gram, diagonal, rest = lax.fori_loop(
        0,
        SAMPLES,
        add,
        ((zero,) * LEFT, zero, jnp.zeros((1, 128), F32), jnp.zeros((PAIR, 128), F32)),
        unroll=True,
    )
    numer = one_column(jnp.concatenate(blocks, axis=0))
    gram = gram_whole(one_above(gram), diagonal[:, K : K + 32])
    old = w[...]
    below = jnp.dot(old, gram, precision=HIGHEST, preferred_element_type=F32) + epsilon
    return old * numer / below, numer, rest


def w_update_kernel(me, got, w, w_out, out):
    new, _, _ = w_new(got, w)
    w_out[...] = new
    fill_w(new, sample_factor(me[1]), out)


def w_last_kernel(got, w, energy, w_out, out):
    new, numer, rest = w_new(got, w)
    w_out[...] = new
    rounded = new.astype(BF16).astype(F32)
    gram = of_pair(rest)
    fitted = jnp.dot(rounded, gram, precision=HIGHEST, preferred_element_type=F32)
    share = jnp.sum(rounded * (fitted - 2.0 * numer))
    lane = lax.broadcasted_iota(jnp.int32, (1, 128), 1)
    pair = jnp.where(lane < K, share, energy[...])
    copies(pair, out)


def share_kernel(got, out):
    copies(jnp.sum(got[...], axis=0), out)


def ratio_kernel(got, ratio, close, total_out):
    sums = jnp.sum(got[...], axis=0)
    total = sums[:, K : K + 1]
    expanded = sums[:, :1] + total
    ratio[0, 0] = jnp.sum(jnp.sqrt(jnp.maximum(expanded, 0.0) / total))
    close[0, 0] = jnp.sum((expanded < 0.02 * total).astype(F32)).astype(jnp.int32)
    total_out[0, 0] = jnp.sum(total)


def last_rows_kernel(w, out):
    rows = w[...]
    right = jnp.concatenate([rows[W_HALF:], jnp.zeros((BLOCK, K), F32)], axis=0)
    message = jnp.concatenate([rows[:W_HALF], right], axis=1).astype(BF16)
    copies(message, out)


def error_kernel(got_w, got_h, tel, out):
    high = got_h[...].reshape(COLS, 128)[:, :K]

    def step(i, error):
        rows = pl.ds(pl.multiple_of(i * W_OWN, W_OWN), W_OWN)
        rebuilt = lax.dot_general(
            one_column(got_w[i].astype(F32)).astype(BF16),
            high,
            (((1,), (1,)), ((), ())),
            preferred_element_type=F32,
        )
        difference = tel[rows, :].astype(F32) - rebuilt
        return error + jnp.sum((difference * difference).reshape(W_OWN // 8, 8, COLS), axis=0)

    error = lax.fori_loop(0, SAMPLES, step, jnp.zeros((8, COLS), F32))
    share = jnp.full((1, 128), jnp.sum(error), F32)
    copies(share, out)


VMEM = pl.BlockSpec(memory_space=pltpu.VMEM)
SMEM = pl.BlockSpec(memory_space=pltpu.SMEM)
HBM = pl.BlockSpec(memory_space=pltpu.HBM)
LIMIT = pltpu.CompilerParams(vmem_limit_bytes=32 * 1024 * 1024)
PRODUCT = pl.CostEstimate(
    flops=2 * K * ROWS * COLS, bytes_accessed=2 * ROWS * COLS, transcendentals=0
)


def call(kernel, inputs, outs, cost=None, specs=None, scratch=(), out_spec=VMEM):
    return pl.pallas_call(
        kernel,
        out_shape=[jax.ShapeDtypeStruct(shape, dtype) for shape, dtype in outs],
        in_specs=[VMEM] * len(inputs) if specs is None else specs,
        out_specs=[out_spec] * len(outs),
        scratch_shapes=list(scratch),
        compiler_params=LIMIT,
        cost_estimate=cost,
    )(*inputs)


def exchange(x, axis):
    return lax.all_to_all(x, axis, 0, 0, tiled=True)


def sum_everywhere(shares):
    part = jnp.sum(exchange(shares, "samples"), axis=0)
    part = exchange(jnp.broadcast_to(part[None], (CHIPS, 1, 128)), "chips")
    return jnp.sum(part, axis=0)


def body(telemetry, chip_factors, sample_factors):
    me = jnp.stack([lax.axis_index("chips"), lax.axis_index("samples")])
    tile = pltpu.VMEM((ROWS, COLS), BF16)
    h = sample_factors.T
    w_sent = [((W_OWN, K), F32), ((SAMPLES, W_MSG, 128), BF16)]
    touches = ROWS // TOUCH
    w, sent = call(
        start_kernel,
        (me, chip_factors, telemetry),
        w_sent,
        None,
        [SMEM, HBM, HBM],
        [
            pltpu.VMEM((touches * BLOCK, COLS), BF16),
            pltpu.SemaphoreType.DMA((touches,)),
            pltpu.VMEM((K, W_OWN), F32),
            pltpu.SemaphoreType.DMA,
        ],
    )
    got_w = exchange(sent, "samples")
    for sweep in range(ITERS):
        last = sweep == ITERS - 1
        (sent,) = call(
            h_numer_kernel,
            (me, got_w, telemetry),
            [((CHIPS, H_MSG, 128), BF16)],
            PRODUCT,
            [SMEM, VMEM, HBM],
            [
                tile,
                pltpu.VMEM((K, ROWS), BF16),
                pltpu.VMEM((ROWS, K), F32),
                pltpu.SemaphoreType.DMA,
            ],
        )
        got = exchange(sent, "chips")
        h, sent = call(
            h_update_kernel, (got, h), [((H_OWN, K), F32), ((CHIPS, H_OWN, 128), BF16)]
        )
        got_h = exchange(sent, "chips")
        w_sums = [((SAMPLES, W_MSG + PAIR if last else W_MSG, 128), BF16)]
        specs, scratch = [SMEM, VMEM, HBM], [tile, pltpu.SemaphoreType.DMA((PARTS,))]
        if sweep == 0:
            sent, energy = call(
                w_numer_energy_kernel,
                (me, got_h, telemetry),
                [*w_sums, ((1, 128), F32)],
                PRODUCT,
                specs,
                scratch,
            )
        else:
            (sent,) = call(
                w_numer_kernel, (me, got_h, telemetry), w_sums, PRODUCT, specs, scratch
            )
        got = exchange(sent, "samples")
        if not last:
            w, sent = call(
                w_update_kernel,
                (me, got, w),
                w_sent,
                None,
                [SMEM, VMEM, VMEM],
            )
            got_w = exchange(sent, "samples")
    w, shares = call(
        w_last_kernel, (got, w, energy), [((W_OWN, K), F32), ((SAMPLES, 1, 128), F32)]
    )
    (shares,) = call(
        share_kernel, (exchange(shares, "samples"),), [((CHIPS, 1, 128), F32)]
    )
    ratio, close, total = call(
        ratio_kernel,
        (exchange(shares, "chips"),),
        [((1, 1), F32), ((1, 1), jnp.int32), ((1, 1), F32)],
        out_spec=SMEM,
    )

    def direct(ratio, total, w, got_h, telemetry):
        (sent,) = call(last_rows_kernel, (w,), [((SAMPLES, W_HALF, 128), BF16)])
        (shares,) = call(
            error_kernel,
            (exchange(sent, "samples"), got_h, telemetry),
            [((SAMPLES, 1, 128), F32)],
            PRODUCT,
        )
        return jnp.sqrt(sum_everywhere(shares)[:1, :1] / total)

    ratio = lax.cond(
        close[0, 0] > 0,
        direct,
        lambda ratio, *operands: ratio,
        ratio,
        total,
        w,
        got_h,
        telemetry,
    )
    return w.T, h.T, ratio[0, 0]


def solution(mesh):
    return jax.shard_map(
        body,
        mesh=mesh,
        in_specs=(
            P("chips", "samples"),
            P(None, ("chips", "samples")),
            P(None, ("samples", "chips")),
        ),
        out_specs=(P(None, ("chips", "samples")), P(None, ("samples", "chips")), P()),
        check_vma=False,
    )
```

```python
import jax
import jax.numpy as jnp
from jax import lax
from jax.experimental import pallas as pl
from jax.experimental.pallas import tpu as pltpu
from jax.sharding import PartitionSpec as P

ITERS = 2

epsilon = 1e-09

F32 = jnp.float32
BF16 = jnp.bfloat16
HIGHEST = lax.Precision.HIGHEST

K = 64
CHIPS = 32
SAMPLES = 16
ROWS = 2304
COLS = 1024
W_OWN = ROWS // SAMPLES
H_OWN = COLS // CHIPS
H_WIDTH = 256
BLOCK = 16
W_HALF = 80
GRAM = 16
W_MSG = W_HALF + GRAM
PAIR = 32
H_MSG = BLOCK + GRAM + 8
LEFT = W_HALF // BLOCK
W_BLOCKS = W_OWN // BLOCK


def split(x):
    high = x.astype(BF16).astype(F32)
    return jnp.concatenate([high, x - high], axis=1).astype(BF16)


def join(x):
    return x[:, :K] + x[:, K:]


def squares():
    row = lax.broadcasted_iota(jnp.int32, (32, 32), 0)
    col = lax.broadcasted_iota(jnp.int32, (32, 32), 1)
    return row, col


TOP = 6.0


def peak(x):
    return jnp.max(jnp.max(x, axis=0, keepdims=True), axis=1, keepdims=True)


def power_of(largest):
    return jnp.floor(jnp.log2(jnp.maximum(largest, 1e-30)))


def sixteenth(x):
    x = x * x
    x = x * x
    x = x * x
    return x * x


def code(x, power, factor):
    return sixteenth(x * (jnp.exp2(TOP - power) * factor))


def root(x):
    return lax.rsqrt(lax.rsqrt(lax.rsqrt(lax.rsqrt(jnp.abs(x)))))


def scale_of(power, factor):
    return jnp.exp2(power - TOP) / factor


def copies(message, out):
    def step(i, carry):
        out[i] = message
        return carry

    lax.fori_loop(0, out.shape[0], step, 0, unroll=True)


def sample_factor(i):
    return 1.0 + jnp.full((1, 1), i, jnp.int32).astype(F32) * (1.0 / 32.0)


def chip_factor(i):
    return 1.0 + jnp.full((1, 1), i, jnp.int32).astype(F32) * (1.0 / 64.0)


def gram_parts(gram):
    row, col = squares()
    first, block, last = gram[:32, :32], gram[:32, 32:], gram[32:, 32:]
    parts = jnp.concatenate([jnp.where(row <= col, first, last), block], axis=1)
    return parts, jnp.sum(jnp.where(row == col, last, 0.0), axis=0, keepdims=True)


def gram_whole(parts, diagonal):
    row, col = squares()
    mixed, block = parts[:, :32], parts[:, 32:]
    turned = lax.dot_general(
        (row == col).astype(F32),
        jnp.concatenate([mixed, block], axis=0),
        (((1,), (1,)), ((), ())),
        precision=HIGHEST,
        preferred_element_type=F32,
    )
    mixed_t, block_t = turned[:, :32], turned[:, 32:]
    one = jnp.where(row <= col, mixed, mixed_t)
    two = jnp.where(row > col, mixed, jnp.where(row < col, mixed_t, diagonal))
    return jnp.concatenate(
        [jnp.concatenate([one, block], axis=1), jnp.concatenate([block_t, two], axis=1)], axis=0
    )


def encode_gram(parts, diagonal, factor):
    power = power_of(jnp.maximum(peak(parts), peak(diagonal)))
    coded = code(parts, power, factor)
    return (
        jnp.concatenate([coded[:GRAM], coded[GRAM:]], axis=1),
        code(diagonal, power, factor),
        power,
    )


def one_above(x):
    return jnp.concatenate([x[:, :K], x[:, K:]], axis=0)


def pair_of(gram):
    row, col = squares()
    parts, diagonal = gram_parts(gram)
    high = parts.astype(BF16).astype(F32)
    low = parts - high
    own = row == col
    first = jnp.where(own, parts[:, :32], high[:, :32])
    third = jnp.where(own, diagonal, low[:, :32])
    return jnp.concatenate([first, high[:, 32:], third, low[:, 32:]], axis=1).astype(BF16)


def of_pair(total):
    row, col = squares()
    own = row == col
    first, third = total[:, :32], total[:, 64:96]
    mixed = jnp.where(own, first, first + third)
    diagonal = jnp.sum(jnp.where(own, third, 0.0), axis=0, keepdims=True)
    block = total[:, 32:64] + total[:, 96:]
    return gram_whole(jnp.concatenate([mixed, block], axis=1), diagonal)


def products(halves):
    return lax.dot_general(halves, halves, (((0,), (0,)), ((), ())), preferred_element_type=F32)


def quarters(four):
    two = four[:K] + four[K:]
    return two[:, :K] + two[:, K:]


def spare_rows(left, right, diagonal, power):
    return jnp.concatenate(
        [
            jnp.broadcast_to(left, (LEFT, K)),
            jnp.broadcast_to(right, (LEFT - 1, K)),
            jnp.broadcast_to(power, (1, K)),
            jnp.concatenate([diagonal, jnp.zeros((1, K - 32), F32)], axis=1),
            jnp.zeros((BLOCK - W_BLOCKS - 2, K), F32),
        ],
        axis=0,
    )


def w_message(w, gram):
    coded, diagonal, power = gram
    none = jnp.zeros((LEFT, 1), F32)
    right = jnp.concatenate(
        [w[W_HALF:], spare_rows(none, none[1:], diagonal, power)], axis=0
    )
    return jnp.concatenate(
        [jnp.concatenate([w[:W_HALF], right], axis=1), coded], axis=0
    ).astype(BF16)


def sums_message(sums, gram, factor):
    coded, diagonal, power = gram
    both = jnp.concatenate(
        [sums[:W_HALF], jnp.concatenate([sums[W_HALF:], jnp.zeros((BLOCK, K), F32)], axis=0)],
        axis=1,
    )
    blocks = [both[j * BLOCK : (j + 1) * BLOCK] for j in range(LEFT)]
    largest = jnp.concatenate(
        [jnp.max(x, axis=0, keepdims=True) for x in blocks] + [jnp.zeros((8 - LEFT, 128), F32)],
        axis=0,
    )
    lane = lax.broadcasted_iota(jnp.int32, (8, 128), 1)
    left = power_of(jnp.max(jnp.where(lane < K, largest, 0.0), axis=1, keepdims=True))
    right = power_of(jnp.max(jnp.where(lane < K, 0.0, largest), axis=1, keepdims=True))
    powers = jnp.where(lane < K, left, right)
    scale = jnp.exp2(TOP - powers) * factor
    blocks = [sixteenth(x * scale[j : j + 1]) for j, x in enumerate(blocks)]
    free = jnp.concatenate(
        [blocks[-1][:, :K], spare_rows(left[:LEFT], right[: LEFT - 1], diagonal, power)], axis=1
    )
    return jnp.concatenate(blocks[:-1] + [free, coded], axis=0).astype(BF16)


def read_gram(message, factor):
    roots = root(message)
    scale = scale_of(message[W_BLOCKS : W_BLOCKS + 1, 127:], factor)
    return roots[BLOCK:] * scale, roots[W_BLOCKS + 1 : W_BLOCKS + 2] * scale


def read_sums(message, factor):
    lane = lax.broadcasted_iota(jnp.int32, (BLOCK, 128), 1)
    scale = scale_of(message[W_HALF - BLOCK :, 127:], factor)
    roots = root(message)
    return [
        roots[j * BLOCK : (j + 1) * BLOCK]
        * jnp.where(lane < K, scale[j : j + 1], scale[LEFT + j : LEFT + j + 1])
        for j in range(LEFT)
    ]


def one_column(both):
    return jnp.concatenate([both[:, :K], both[: W_OWN - W_HALF, K:]], axis=0)


def fill_w(w, factor, out):
    gram = gram_parts(quarters(products(split(w))))
    copies(w_message(w, encode_gram(*gram, factor)), out)


def start_kernel(me, w, tel, w_out, out):
    del tel
    wide = jnp.concatenate([w[...], jnp.zeros((K, 256 - W_OWN), F32)], axis=1)
    turned = wide.T[:W_OWN]
    w_out[...] = turned
    fill_w(turned, sample_factor(me[1]), out)


def h_numer_kernel(me, got, tile, out, w_turned, w_all):

    def gather(i, carry):
        gram, diagonal = carry
        message = got[i].astype(F32)
        w_all[pl.ds(pl.multiple_of(i * W_OWN, BLOCK), W_OWN), :] = one_column(message[:W_HALF])
        more, ends = read_gram(message[W_HALF - BLOCK :], sample_factor(i))
        return gram + more, diagonal + ends

    zero = (jnp.zeros((GRAM, 128), F32), jnp.zeros((1, 128), F32))
    gram, diagonal = lax.fori_loop(0, SAMPLES, gather, zero, unroll=True)

    def turn(j, carry):
        at = pl.ds(pl.multiple_of(j * 128, 128), 128)
        w_turned[:, at] = w_all[at, :].T.astype(BF16)
        return carry

    lax.fori_loop(0, ROWS // 128, turn, 0, unroll=True)
    factor = chip_factor(me[0])
    coded, ends, power = encode_gram(one_above(gram), diagonal[:, K : K + 32], factor)
    ends = jnp.concatenate([ends, jnp.zeros((1, 96), F32)], axis=1)
    power = jnp.broadcast_to(power, (1, 128))
    per = H_WIDTH // H_OWN

    def step(n, carry):
        cols = pl.ds(pl.multiple_of(n * H_WIDTH, H_WIDTH), H_WIDTH)
        part = jnp.dot(w_turned[...], tile[:, cols], preferred_element_type=F32).T
        for q in range(per):
            halves = [part[q * H_OWN + r : q * H_OWN + r + BLOCK] for r in (0, BLOCK)]
            powers = [power_of(peak(x)) for x in halves]
            out[n * per + q] = jnp.concatenate(
                [
                    jnp.concatenate([code(x, p, factor) for x, p in zip(halves, powers)], axis=1),
                    coded,
                    ends,
                    power,
                    jnp.broadcast_to(powers[0], (1, 128)),
                    jnp.broadcast_to(powers[1], (1, 128)),
                    jnp.zeros((4, 128), F32),
                ],
                axis=0,
            ).astype(BF16)
        return carry

    lax.fori_loop(0, COLS // H_WIDTH, step, 0, unroll=True)


def h_update_kernel(got, h, h_out, out):
    lane = lax.broadcasted_iota(jnp.int32, (BLOCK, 128), 1)

    def add(i, carry):
        numer, gram, diagonal = carry
        message = got[i].astype(F32)
        roots = root(message)
        scales = scale_of(message[H_MSG - 8 :, 127:], chip_factor(i))
        numer += roots[:BLOCK] * jnp.where(lane < K, scales[2:3], scales[3:4])
        gram += roots[BLOCK : BLOCK + GRAM] * scales[1:2]
        diagonal += roots[H_MSG - 8 : H_MSG - 7] * scales[1:2]
        return numer, gram, diagonal

    zero = jnp.zeros((BLOCK, 128), F32)
    numer, gram, diagonal = lax.fori_loop(
        0, CHIPS, add, (zero, zero, jnp.zeros((1, 128), F32)), unroll=True
    )
    gram = gram_whole(one_above(gram), diagonal[:, :32])
    old = h[...]
    below = jnp.dot(old, gram, precision=HIGHEST, preferred_element_type=F32) + epsilon
    new = old * one_above(numer) / below
    h_out[...] = new
    copies(split(new), out)


def w_numer(me, got, tile, out, energy=None):
    halves = got[...].reshape(COLS, 128)
    four = products(halves)
    factor = sample_factor(me[1])
    gram = encode_gram(*gram_parts(quarters(four)), factor)
    last = out.shape[1] > W_MSG
    if last:
        pair = pair_of(four[:K, :K])
    if energy is not None:

        def add(i, total):
            rows = pl.ds(pl.multiple_of(i * W_OWN, W_OWN), W_OWN)
            values = tile[rows, :].astype(F32)
            return total + jnp.sum((values * values).reshape(W_OWN // 8, 8, COLS), axis=0)

        squares_sum = lax.fori_loop(0, SAMPLES, add, jnp.zeros((8, COLS), F32))
        energy[...] = jnp.full((1, 128), jnp.sum(squares_sum), F32)
    sums = jnp.dot(tile[...], halves[:, :K], preferred_element_type=F32)
    for q in range(SAMPLES):
        message = sums_message(sums[q * W_OWN : (q + 1) * W_OWN], gram, factor)
        if last:
            message = jnp.concatenate([message, pair], axis=0)
        out[q] = message


def w_numer_kernel(me, got, tile, out):
    w_numer(me, got, tile, out)


def w_numer_energy_kernel(me, got, tile, out, energy):
    w_numer(me, got, tile, out, energy)


def w_new(got, w):
    last = got.shape[1] > W_MSG

    def add(i, carry):
        blocks, gram, diagonal, rest = carry
        message = got[i].astype(F32)
        terms = read_sums(message[:W_HALF], sample_factor(i))
        more, ends = read_gram(message[W_HALF - BLOCK : W_MSG], sample_factor(i))
        if last:
            rest += message[W_MSG:]
        blocks = tuple(total + term for total, term in zip(blocks, terms))
        return blocks, gram + more, diagonal + ends, rest

    zero = jnp.zeros((BLOCK, 128), F32)
    blocks, gram, diagonal, rest = lax.fori_loop(
        0,
        SAMPLES,
        add,
        ((zero,) * LEFT, zero, jnp.zeros((1, 128), F32), jnp.zeros((PAIR, 128), F32)),
        unroll=True,
    )
    numer = one_column(jnp.concatenate(blocks, axis=0))
    gram = gram_whole(one_above(gram), diagonal[:, K : K + 32])
    old = w[...]
    below = jnp.dot(old, gram, precision=HIGHEST, preferred_element_type=F32) + epsilon
    return old * numer / below, numer, rest


def w_update_kernel(me, got, w, w_out, out):
    new, _, _ = w_new(got, w)
    w_out[...] = new
    fill_w(new, sample_factor(me[1]), out)


def w_last_kernel(got, w, energy, w_out, out):
    new, numer, rest = w_new(got, w)
    w_out[...] = new
    rounded = new.astype(BF16).astype(F32)
    gram = of_pair(rest)
    fitted = jnp.dot(rounded, gram, precision=HIGHEST, preferred_element_type=F32)
    share = jnp.sum(rounded * (fitted - 2.0 * numer))
    lane = lax.broadcasted_iota(jnp.int32, (1, 128), 1)
    pair = jnp.where(lane < K, share, energy[...])
    copies(pair, out)


def share_kernel(got, out):
    copies(jnp.sum(got[...], axis=0), out)


def ratio_kernel(got, ratio, close, total_out):
    sums = jnp.sum(got[...], axis=0)
    total = sums[:, K : K + 1]
    expanded = sums[:, :1] + total
    ratio[0, 0] = jnp.sum(jnp.sqrt(jnp.maximum(expanded, 0.0) / total))
    close[0, 0] = jnp.sum((expanded < 0.02 * total).astype(F32)).astype(jnp.int32)
    total_out[0, 0] = jnp.sum(total)


def last_rows_kernel(w, out):
    rows = w[...]
    right = jnp.concatenate([rows[W_HALF:], jnp.zeros((BLOCK, K), F32)], axis=0)
    message = jnp.concatenate([rows[:W_HALF], right], axis=1).astype(BF16)
    copies(message, out)


def error_kernel(got_w, got_h, tel, out):
    high = got_h[...].reshape(COLS, 128)[:, :K]

    def step(i, error):
        rows = pl.ds(pl.multiple_of(i * W_OWN, W_OWN), W_OWN)
        rebuilt = lax.dot_general(
            one_column(got_w[i].astype(F32)).astype(BF16),
            high,
            (((1,), (1,)), ((), ())),
            preferred_element_type=F32,
        )
        difference = tel[rows, :].astype(F32) - rebuilt
        return error + jnp.sum((difference * difference).reshape(W_OWN // 8, 8, COLS), axis=0)

    error = lax.fori_loop(0, SAMPLES, step, jnp.zeros((8, COLS), F32))
    share = jnp.full((1, 128), jnp.sum(error), F32)
    copies(share, out)


VMEM = pl.BlockSpec(memory_space=pltpu.VMEM)
SMEM = pl.BlockSpec(memory_space=pltpu.SMEM)
HBM = pl.BlockSpec(memory_space=pltpu.HBM)
LIMIT = pltpu.CompilerParams(vmem_limit_bytes=32 * 1024 * 1024)
PRODUCT = pl.CostEstimate(
    flops=2 * K * ROWS * COLS, bytes_accessed=2 * ROWS * COLS, transcendentals=0
)


def call(kernel, inputs, outs, cost=None, specs=None, scratch=(), out_spec=VMEM):
    return pl.pallas_call(
        kernel,
        out_shape=[jax.ShapeDtypeStruct(shape, dtype) for shape, dtype in outs],
        in_specs=[VMEM] * len(inputs) if specs is None else specs,
        out_specs=[out_spec] * len(outs),
        scratch_shapes=list(scratch),
        compiler_params=LIMIT,
        cost_estimate=cost,
    )(*inputs)


def exchange(x, axis):
    return lax.all_to_all(x, axis, 0, 0, tiled=True)


def sum_everywhere(shares):
    part = jnp.sum(exchange(shares, "samples"), axis=0)
    part = exchange(jnp.broadcast_to(part[None], (CHIPS, 1, 128)), "chips")
    return jnp.sum(part, axis=0)


def body(telemetry, chip_factors, sample_factors):
    me = jnp.stack([lax.axis_index("chips"), lax.axis_index("samples")])
    specs = [SMEM, VMEM, VMEM]
    h = sample_factors.T
    w_sent = [((W_OWN, K), F32), ((SAMPLES, W_MSG, 128), BF16)]
    w, sent = call(
        start_kernel, (me, chip_factors, telemetry), w_sent, None, [SMEM, VMEM, HBM]
    )
    got_w = exchange(sent, "samples")
    for sweep in range(ITERS):
        last = sweep == ITERS - 1
        (sent,) = call(
            h_numer_kernel,
            (me, got_w, telemetry),
            [((CHIPS, H_MSG, 128), BF16)],
            PRODUCT,
            specs,
            [pltpu.VMEM((K, ROWS), BF16), pltpu.VMEM((ROWS, K), F32)],
        )
        got = exchange(sent, "chips")
        h, sent = call(
            h_update_kernel, (got, h), [((H_OWN, K), F32), ((CHIPS, H_OWN, 128), BF16)]
        )
        got_h = exchange(sent, "chips")
        w_sums = [((SAMPLES, W_MSG + PAIR if last else W_MSG, 128), BF16)]
        if sweep == 0:
            sent, energy = call(
                w_numer_energy_kernel,
                (me, got_h, telemetry),
                [*w_sums, ((1, 128), F32)],
                PRODUCT,
                specs,
            )
        else:
            (sent,) = call(
                w_numer_kernel, (me, got_h, telemetry), w_sums, PRODUCT, specs
            )
        got = exchange(sent, "samples")
        if not last:
            w, sent = call(
                w_update_kernel,
                (me, got, w),
                w_sent,
                None,
                [SMEM, VMEM, VMEM],
            )
            got_w = exchange(sent, "samples")
    w, shares = call(
        w_last_kernel, (got, w, energy), [((W_OWN, K), F32), ((SAMPLES, 1, 128), F32)]
    )
    (shares,) = call(
        share_kernel, (exchange(shares, "samples"),), [((CHIPS, 1, 128), F32)]
    )
    ratio, close, total = call(
        ratio_kernel,
        (exchange(shares, "chips"),),
        [((1, 1), F32), ((1, 1), jnp.int32), ((1, 1), F32)],
        out_spec=SMEM,
    )

    def direct(ratio, total, w, got_h, telemetry):
        (sent,) = call(last_rows_kernel, (w,), [((SAMPLES, W_HALF, 128), BF16)])
        (shares,) = call(
            error_kernel,
            (exchange(sent, "samples"), got_h, telemetry),
            [((SAMPLES, 1, 128), F32)],
            PRODUCT,
        )
        return jnp.sqrt(sum_everywhere(shares)[:1, :1] / total)

    ratio = lax.cond(
        close[0, 0] > 0,
        direct,
        lambda ratio, *operands: ratio,
        ratio,
        total,
        w,
        got_h,
        telemetry,
    )
    return w.T, h.T, ratio[0, 0]


def solution(mesh):
    return jax.shard_map(
        body,
        mesh=mesh,
        in_specs=(
            P("chips", "samples"),
            P(None, ("chips", "samples")),
            P(None, ("samples", "chips")),
        ),
        out_specs=(P(None, ("chips", "samples")), P(None, ("samples", "chips")), P()),
        check_vma=False,
    )
```

```python
import jax
import jax.numpy as jnp
from jax import lax
from jax.experimental import pallas as pl
from jax.experimental.pallas import tpu as pltpu
from jax.sharding import PartitionSpec as P

ITERS = 2

epsilon = 1e-09

F32 = jnp.float32
BF16 = jnp.bfloat16
HIGHEST = lax.Precision.HIGHEST

K = 64
CHIPS = 32
SAMPLES = 16
ROWS = 2304
COLS = 1024
W_OWN = ROWS // SAMPLES
H_OWN = COLS // CHIPS
H_WIDTH = 256
BLOCK = 16
W_HALF = 80
GRAM = 16
W_MSG = W_HALF + GRAM
H_MSG = BLOCK + GRAM + 8
LEFT = W_HALF // BLOCK
W_BLOCKS = W_OWN // BLOCK


def split(x):
    high = x.astype(BF16).astype(F32)
    return jnp.concatenate([high, x - high], axis=1).astype(BF16)


def join(x):
    return x[:, :K] + x[:, K:]


def squares():
    row = lax.broadcasted_iota(jnp.int32, (32, 32), 0)
    col = lax.broadcasted_iota(jnp.int32, (32, 32), 1)
    return row, col


TOP = 6.0


def peak(x):
    return jnp.max(jnp.max(x, axis=0, keepdims=True), axis=1, keepdims=True)


def power_of(largest):
    return jnp.floor(jnp.log2(jnp.maximum(largest, 1e-30)))


def sixteenth(x):
    x = x * x
    x = x * x
    x = x * x
    return x * x


def code(x, power, factor):
    return sixteenth(x * (jnp.exp2(TOP - power) * factor))


def root(x):
    return lax.rsqrt(lax.rsqrt(lax.rsqrt(lax.rsqrt(jnp.abs(x)))))


def scale_of(power, factor):
    return jnp.exp2(power - TOP) / factor


def copies(message, out):
    def step(i, carry):
        out[i] = message
        return carry

    lax.fori_loop(0, out.shape[0], step, 0, unroll=True)


def sample_factor(i):
    return 1.0 + jnp.full((1, 1), i, jnp.int32).astype(F32) * (1.0 / 32.0)


def chip_factor(i):
    return 1.0 + jnp.full((1, 1), i, jnp.int32).astype(F32) * (1.0 / 64.0)


def gram_parts(gram):
    row, col = squares()
    first, block, last = gram[:32, :32], gram[:32, 32:], gram[32:, 32:]
    parts = jnp.concatenate([jnp.where(row <= col, first, last), block], axis=1)
    return parts, jnp.sum(jnp.where(row == col, last, 0.0), axis=0, keepdims=True)


def gram_whole(parts, diagonal):
    row, col = squares()
    mixed, block = parts[:, :32], parts[:, 32:]
    turned = lax.dot_general(
        (row == col).astype(F32),
        jnp.concatenate([mixed, block], axis=0),
        (((1,), (1,)), ((), ())),
        precision=HIGHEST,
        preferred_element_type=F32,
    )
    mixed_t, block_t = turned[:, :32], turned[:, 32:]
    one = jnp.where(row <= col, mixed, mixed_t)
    two = jnp.where(row > col, mixed, jnp.where(row < col, mixed_t, diagonal))
    return jnp.concatenate(
        [jnp.concatenate([one, block], axis=1), jnp.concatenate([block_t, two], axis=1)], axis=0
    )


GRAM_TOP = 13.0


def grain():
    row = lax.broadcasted_iota(jnp.int32, (32, K), 0)
    col = lax.broadcasted_iota(jnp.int32, (32, K), 1)
    return 1.0 + ((row * 11 + col * 23) & 31).astype(F32) * (1.0 / 64.0)


def eighth(x):
    x = x * x
    x = x * x
    return x * x


def eighth_root(x):
    return jnp.sqrt(lax.rsqrt(lax.rsqrt(jnp.abs(x))))


def encode_gram(parts, diagonal, factor):
    power = power_of(jnp.maximum(peak(parts), peak(diagonal)))
    scale = jnp.exp2(GRAM_TOP - power) * factor
    coded = eighth(parts * grain() * scale)
    return (
        jnp.concatenate([coded[:GRAM], coded[GRAM:]], axis=1),
        eighth(diagonal * scale),
        power,
    )


def gram_scale(power, factor):
    return jnp.exp2(power - GRAM_TOP) / factor


def one_above(x):
    return jnp.concatenate([x[:, :K], x[:, K:]], axis=0)


def added_parts(total):
    return one_above(total) / grain()


def products(halves):
    return lax.dot_general(halves, halves, (((0,), (0,)), ((), ())), preferred_element_type=F32)


def quarters(four):
    two = four[:K] + four[K:]
    return two[:, :K] + two[:, K:]


def spare_rows(left, right, grams):
    rows = []
    for _, diagonal, power in grams:
        rows.append(jnp.broadcast_to(power, (1, K)))
        rows.append(jnp.concatenate([diagonal, jnp.zeros((1, K - 32), F32)], axis=1))
    return jnp.concatenate(
        [
            jnp.broadcast_to(left, (LEFT, K)),
            jnp.broadcast_to(right, (LEFT - 1, K)),
            *rows,
            jnp.zeros((BLOCK - W_BLOCKS - len(rows), K), F32),
        ],
        axis=0,
    )


def w_message(w, gram):
    none = jnp.zeros((LEFT, 1), F32)
    right = jnp.concatenate(
        [w[W_HALF:], spare_rows(none, none[1:], [gram])], axis=0
    )
    return jnp.concatenate(
        [jnp.concatenate([w[:W_HALF], right], axis=1), gram[0]], axis=0
    ).astype(BF16)


def sums_message(sums, grams, factor):
    both = jnp.concatenate(
        [sums[:W_HALF], jnp.concatenate([sums[W_HALF:], jnp.zeros((BLOCK, K), F32)], axis=0)],
        axis=1,
    )
    blocks = [both[j * BLOCK : (j + 1) * BLOCK] for j in range(LEFT)]
    largest = jnp.concatenate(
        [jnp.max(x, axis=0, keepdims=True) for x in blocks] + [jnp.zeros((8 - LEFT, 128), F32)],
        axis=0,
    )
    lane = lax.broadcasted_iota(jnp.int32, (8, 128), 1)
    left = power_of(jnp.max(jnp.where(lane < K, largest, 0.0), axis=1, keepdims=True))
    right = power_of(jnp.max(jnp.where(lane < K, 0.0, largest), axis=1, keepdims=True))
    powers = jnp.where(lane < K, left, right)
    scale = jnp.exp2(TOP - powers) * factor
    blocks = [sixteenth(x * scale[j : j + 1]) for j, x in enumerate(blocks)]
    free = jnp.concatenate(
        [blocks[-1][:, :K], spare_rows(left[:LEFT], right[: LEFT - 1], grams)], axis=1
    )
    return jnp.concatenate(
        blocks[:-1] + [free] + [coded for coded, _, _ in grams], axis=0
    ).astype(BF16)


def read_gram(message, factor, which=0):
    at = W_BLOCKS + 2 * which
    scale = gram_scale(message[at : at + 1, 127:], factor)
    coded = message[BLOCK + GRAM * which : BLOCK + GRAM * (which + 1)]
    return eighth_root(coded) * scale, eighth_root(message[at + 1 : at + 2]) * scale


def read_sums(message, factor):
    lane = lax.broadcasted_iota(jnp.int32, (BLOCK, 128), 1)
    scale = scale_of(message[W_HALF - BLOCK :, 127:], factor)
    roots = root(message)
    return [
        roots[j * BLOCK : (j + 1) * BLOCK]
        * jnp.where(lane < K, scale[j : j + 1], scale[LEFT + j : LEFT + j + 1])
        for j in range(LEFT)
    ]


def one_column(both):
    return jnp.concatenate([both[:, :K], both[: W_OWN - W_HALF, K:]], axis=0)


def fill_w(w, factor, out):
    gram = gram_parts(quarters(products(split(w))))
    copies(w_message(w, encode_gram(*gram, factor)), out)


def start_kernel(me, w, tel, w_out, out):
    del tel
    wide = jnp.concatenate([w[...], jnp.zeros((K, 256 - W_OWN), F32)], axis=1)
    turned = wide.T[:W_OWN]
    w_out[...] = turned
    fill_w(turned, sample_factor(me[1]), out)


def h_numer_kernel(me, got, tile, out, w_turned, w_all):

    def gather(i, carry):
        gram, diagonal = carry
        message = got[i].astype(F32)
        w_all[pl.ds(pl.multiple_of(i * W_OWN, BLOCK), W_OWN), :] = one_column(message[:W_HALF])
        more, ends = read_gram(message[W_HALF - BLOCK :], sample_factor(i))
        return gram + more, diagonal + ends

    zero = (jnp.zeros((GRAM, 128), F32), jnp.zeros((1, 128), F32))
    gram, diagonal = lax.fori_loop(0, SAMPLES, gather, zero, unroll=True)

    def turn(j, carry):
        at = pl.ds(pl.multiple_of(j * 128, 128), 128)
        w_turned[:, at] = w_all[at, :].T.astype(BF16)
        return carry

    lax.fori_loop(0, ROWS // 128, turn, 0, unroll=True)
    factor = chip_factor(me[0])
    coded, ends, power = encode_gram(added_parts(gram), diagonal[:, K : K + 32], factor)
    ends = jnp.concatenate([ends, jnp.zeros((1, 96), F32)], axis=1)
    power = jnp.broadcast_to(power, (1, 128))
    per = H_WIDTH // H_OWN

    def step(n, carry):
        cols = pl.ds(pl.multiple_of(n * H_WIDTH, H_WIDTH), H_WIDTH)
        part = jnp.dot(w_turned[...], tile[:, cols], preferred_element_type=F32).T
        for q in range(per):
            halves = [part[q * H_OWN + r : q * H_OWN + r + BLOCK] for r in (0, BLOCK)]
            powers = [power_of(peak(x)) for x in halves]
            out[n * per + q] = jnp.concatenate(
                [
                    jnp.concatenate([code(x, p, factor) for x, p in zip(halves, powers)], axis=1),
                    coded,
                    ends,
                    power,
                    jnp.broadcast_to(powers[0], (1, 128)),
                    jnp.broadcast_to(powers[1], (1, 128)),
                    jnp.zeros((4, 128), F32),
                ],
                axis=0,
            ).astype(BF16)
        return carry

    lax.fori_loop(0, COLS // H_WIDTH, step, 0, unroll=True)


def h_update_kernel(got, h, h_out, out):
    lane = lax.broadcasted_iota(jnp.int32, (BLOCK, 128), 1)

    def add(i, carry):
        numer, gram, diagonal = carry
        message = got[i].astype(F32)
        powers = message[H_MSG - 8 :, 127:]
        scales = scale_of(powers, chip_factor(i))
        numer += root(message[:BLOCK]) * jnp.where(lane < K, scales[2:3], scales[3:4])
        scale = gram_scale(powers[1:2], chip_factor(i))
        gram += eighth_root(message[BLOCK : BLOCK + GRAM]) * scale
        diagonal += eighth_root(message[H_MSG - 8 : H_MSG - 7]) * scale
        return numer, gram, diagonal

    zero = jnp.zeros((BLOCK, 128), F32)
    numer, gram, diagonal = lax.fori_loop(
        0, CHIPS, add, (zero, zero, jnp.zeros((1, 128), F32)), unroll=True
    )
    gram = gram_whole(added_parts(gram), diagonal[:, :32])
    old = h[...]
    below = jnp.dot(old, gram, precision=HIGHEST, preferred_element_type=F32) + epsilon
    new = old * one_above(numer) / below
    h_out[...] = new
    copies(split(new), out)


def w_numer(me, got, tile, out, energy=None):
    halves = got[...].reshape(COLS, 128)
    four = products(halves)
    factor = sample_factor(me[1])
    grams = [encode_gram(*gram_parts(quarters(four)), factor)]
    if out.shape[1] > W_MSG:
        grams.append(encode_gram(*gram_parts(four[:K, :K]), factor))
    if energy is not None:

        def add(i, total):
            rows = pl.ds(pl.multiple_of(i * W_OWN, W_OWN), W_OWN)
            values = tile[rows, :].astype(F32)
            return total + jnp.sum((values * values).reshape(W_OWN // 8, 8, COLS), axis=0)

        squares_sum = lax.fori_loop(0, SAMPLES, add, jnp.zeros((8, COLS), F32), unroll=True)
        energy[...] = jnp.full((1, 128), jnp.sum(squares_sum), F32)
    sums = jnp.dot(tile[...], halves[:, :K], preferred_element_type=F32)
    for q in range(SAMPLES):
        out[q] = sums_message(sums[q * W_OWN : (q + 1) * W_OWN], grams, factor)


def w_numer_kernel(me, got, tile, out):
    w_numer(me, got, tile, out)


def w_numer_energy_kernel(me, got, tile, out, energy):
    w_numer(me, got, tile, out, energy)


def w_new(got, w):
    count = (got.shape[1] - W_HALF) // GRAM

    def add(i, carry):
        blocks, grams = carry
        message = got[i].astype(F32)
        terms = read_sums(message[:W_HALF], sample_factor(i))
        blocks = tuple(total + term for total, term in zip(blocks, terms))
        more = [read_gram(message[W_HALF - BLOCK :], sample_factor(i), n) for n in range(count)]
        return blocks, tuple((x + u, y + v) for (x, y), (u, v) in zip(grams, more))

    zero = jnp.zeros((BLOCK, 128), F32)
    empty = (zero, jnp.zeros((1, 128), F32))
    blocks, grams = lax.fori_loop(
        0, SAMPLES, add, ((zero,) * LEFT, (empty,) * count), unroll=True
    )
    numer = one_column(jnp.concatenate(blocks, axis=0))
    grams = [gram_whole(added_parts(x), y[:, K : K + 32]) for x, y in grams]
    gram = grams[0]
    old = w[...]
    below = jnp.dot(old, gram, precision=HIGHEST, preferred_element_type=F32) + epsilon
    return old * numer / below, numer, grams[-1]


def w_update_kernel(me, got, w, w_out, out):
    new, _, _ = w_new(got, w)
    w_out[...] = new
    fill_w(new, sample_factor(me[1]), out)


def w_last_kernel(got, w, energy, w_out, out):
    new, numer, gram = w_new(got, w)
    w_out[...] = new
    rounded = new.astype(BF16).astype(F32)
    fitted = jnp.dot(rounded, gram, precision=HIGHEST, preferred_element_type=F32)
    share = jnp.sum(rounded * (fitted - 2.0 * numer))
    lane = lax.broadcasted_iota(jnp.int32, (1, 128), 1)
    pair = jnp.where(lane < K, share, energy[...])
    copies(pair, out)


def share_kernel(got, out):
    copies(jnp.sum(got[...], axis=0), out)


def ratio_kernel(got, ratio, close, total_out):
    sums = jnp.sum(got[...], axis=0)
    total = sums[:, K : K + 1]
    expanded = sums[:, :1] + total
    ratio[0, 0] = jnp.sum(jnp.sqrt(jnp.maximum(expanded, 0.0) / total))
    close[0, 0] = jnp.sum((expanded < 0.02 * total).astype(F32)).astype(jnp.int32)
    total_out[0, 0] = jnp.sum(total)


def last_rows_kernel(w, out):
    rows = w[...]
    right = jnp.concatenate([rows[W_HALF:], jnp.zeros((BLOCK, K), F32)], axis=0)
    message = jnp.concatenate([rows[:W_HALF], right], axis=1).astype(BF16)
    copies(message, out)


def error_kernel(got_w, got_h, tel, out):
    high = got_h[...].reshape(COLS, 128)[:, :K]

    def step(i, error):
        rows = pl.ds(pl.multiple_of(i * W_OWN, W_OWN), W_OWN)
        rebuilt = lax.dot_general(
            one_column(got_w[i].astype(F32)).astype(BF16),
            high,
            (((1,), (1,)), ((), ())),
            preferred_element_type=F32,
        )
        difference = tel[rows, :].astype(F32) - rebuilt
        return error + jnp.sum((difference * difference).reshape(W_OWN // 8, 8, COLS), axis=0)

    error = lax.fori_loop(0, SAMPLES, step, jnp.zeros((8, COLS), F32))
    share = jnp.full((1, 128), jnp.sum(error), F32)
    copies(share, out)


VMEM = pl.BlockSpec(memory_space=pltpu.VMEM)
SMEM = pl.BlockSpec(memory_space=pltpu.SMEM)
HBM = pl.BlockSpec(memory_space=pltpu.HBM)
LIMIT = pltpu.CompilerParams(vmem_limit_bytes=32 * 1024 * 1024)
PRODUCT = pl.CostEstimate(
    flops=2 * K * ROWS * COLS, bytes_accessed=2 * ROWS * COLS, transcendentals=0
)


def call(kernel, inputs, outs, cost=None, specs=None, scratch=(), out_spec=VMEM):
    return pl.pallas_call(
        kernel,
        out_shape=[jax.ShapeDtypeStruct(shape, dtype) for shape, dtype in outs],
        in_specs=[VMEM] * len(inputs) if specs is None else specs,
        out_specs=[out_spec] * len(outs),
        scratch_shapes=list(scratch),
        compiler_params=LIMIT,
        cost_estimate=cost,
    )(*inputs)


def exchange(x, axis):
    return lax.all_to_all(x, axis, 0, 0, tiled=True)


def sum_everywhere(shares):
    part = jnp.sum(exchange(shares, "samples"), axis=0)
    part = exchange(jnp.broadcast_to(part[None], (CHIPS, 1, 128)), "chips")
    return jnp.sum(part, axis=0)


def body(telemetry, chip_factors, sample_factors):
    me = jnp.stack([lax.axis_index("chips"), lax.axis_index("samples")])
    specs = [SMEM, VMEM, VMEM]
    h = sample_factors.T
    w_sent = [((W_OWN, K), F32), ((SAMPLES, W_MSG, 128), BF16)]
    w, sent = call(
        start_kernel, (me, chip_factors, telemetry), w_sent, None, [SMEM, VMEM, HBM]
    )
    got_w = exchange(sent, "samples")
    for sweep in range(ITERS):
        last = sweep == ITERS - 1
        (sent,) = call(
            h_numer_kernel,
            (me, got_w, telemetry),
            [((CHIPS, H_MSG, 128), BF16)],
            PRODUCT,
            specs,
            [pltpu.VMEM((K, ROWS), BF16), pltpu.VMEM((ROWS, K), F32)],
        )
        got = exchange(sent, "chips")
        h, sent = call(
            h_update_kernel, (got, h), [((H_OWN, K), F32), ((CHIPS, H_OWN, 128), BF16)]
        )
        got_h = exchange(sent, "chips")
        w_sums = [((SAMPLES, W_MSG + GRAM if last else W_MSG, 128), BF16)]
        if sweep == 0:
            sent, energy = call(
                w_numer_energy_kernel,
                (me, got_h, telemetry),
                [*w_sums, ((1, 128), F32)],
                PRODUCT,
                specs,
            )
        else:
            (sent,) = call(
                w_numer_kernel, (me, got_h, telemetry), w_sums, PRODUCT, specs
            )
        got = exchange(sent, "samples")
        if not last:
            w, sent = call(
                w_update_kernel,
                (me, got, w),
                w_sent,
                None,
                [SMEM, VMEM, VMEM],
            )
            got_w = exchange(sent, "samples")
    w, shares = call(
        w_last_kernel, (got, w, energy), [((W_OWN, K), F32), ((SAMPLES, 1, 128), F32)]
    )
    (shares,) = call(
        share_kernel, (exchange(shares, "samples"),), [((CHIPS, 1, 128), F32)]
    )
    ratio, close, total = call(
        ratio_kernel,
        (exchange(shares, "chips"),),
        [((1, 1), F32), ((1, 1), jnp.int32), ((1, 1), F32)],
        out_spec=SMEM,
    )

    def direct(ratio, total, w, got_h, telemetry):
        (sent,) = call(last_rows_kernel, (w,), [((SAMPLES, W_HALF, 128), BF16)])
        (shares,) = call(
            error_kernel,
            (exchange(sent, "samples"), got_h, telemetry),
            [((SAMPLES, 1, 128), F32)],
            PRODUCT,
        )
        return jnp.sqrt(sum_everywhere(shares)[:1, :1] / total)

    ratio = lax.cond(
        close[0, 0] > 0,
        direct,
        lambda ratio, *operands: ratio,
        ratio,
        total,
        w,
        got_h,
        telemetry,
    )
    return w.T, h.T, ratio[0, 0]


def solution(mesh):
    return jax.shard_map(
        body,
        mesh=mesh,
        in_specs=(
            P("chips", "samples"),
            P(None, ("chips", "samples")),
            P(None, ("samples", "chips")),
        ),
        out_specs=(P(None, ("chips", "samples")), P(None, ("samples", "chips")), P()),
        check_vma=False,
    )
```

```python
import jax
import jax.numpy as jnp
from jax import lax
from jax.experimental import pallas as pl
from jax.experimental.pallas import tpu as pltpu
from jax.sharding import PartitionSpec as P

ITERS = 2

epsilon = 1e-09

F32 = jnp.float32
BF16 = jnp.bfloat16
HIGHEST = lax.Precision.HIGHEST

K = 64
CHIPS = 32
SAMPLES = 16
ROWS = 2304
COLS = 1024
W_OWN = ROWS // SAMPLES
H_OWN = COLS // CHIPS
H_WIDTH = 256
BLOCK = 16
W_HALF = 80
GRAM = 16
W_MSG = W_HALF + GRAM
H_MSG = BLOCK + GRAM + 8
LEFT = W_HALF // BLOCK
W_BLOCKS = W_OWN // BLOCK


def split(x):
    high = x.astype(BF16).astype(F32)
    return jnp.concatenate([high, x - high], axis=1).astype(BF16)


def join(x):
    return x[:, :K] + x[:, K:]


def squares():
    row = lax.broadcasted_iota(jnp.int32, (32, 32), 0)
    col = lax.broadcasted_iota(jnp.int32, (32, 32), 1)
    return row, col


TOP = 6.0


def peak(x):
    return jnp.max(jnp.max(x, axis=0, keepdims=True), axis=1, keepdims=True)


def power_of(largest):
    return jnp.floor(jnp.log2(jnp.maximum(largest, 1e-30)))


def sixteenth(x):
    x = x * x
    x = x * x
    x = x * x
    return x * x


def code(x, power, factor):
    return sixteenth(x * (jnp.exp2(TOP - power) * factor))


def root(x):
    return lax.rsqrt(lax.rsqrt(lax.rsqrt(lax.rsqrt(jnp.abs(x)))))


def scale_of(power, factor):
    return jnp.exp2(power - TOP) / factor


def copies(message, out):
    def step(i, carry):
        out[i] = message
        return carry

    lax.fori_loop(0, out.shape[0], step, 0, unroll=True)


def sample_factor(i):
    return 1.0 + jnp.full((1, 1), i, jnp.int32).astype(F32) * (1.0 / 32.0)


def chip_factor(i):
    return 1.0 + jnp.full((1, 1), i, jnp.int32).astype(F32) * (1.0 / 64.0)


def gram_parts(gram):
    row, col = squares()
    first, block, last = gram[:32, :32], gram[:32, 32:], gram[32:, 32:]
    parts = jnp.concatenate([jnp.where(row <= col, first, last), block], axis=1)
    return parts, jnp.sum(jnp.where(row == col, last, 0.0), axis=0, keepdims=True)


def gram_whole(parts, diagonal):
    row, col = squares()
    mixed, block = parts[:, :32], parts[:, 32:]
    turned = lax.dot_general(
        (row == col).astype(F32),
        jnp.concatenate([mixed, block], axis=0),
        (((1,), (1,)), ((), ())),
        precision=HIGHEST,
        preferred_element_type=F32,
    )
    mixed_t, block_t = turned[:, :32], turned[:, 32:]
    one = jnp.where(row <= col, mixed, mixed_t)
    two = jnp.where(row > col, mixed, jnp.where(row < col, mixed_t, diagonal))
    return jnp.concatenate(
        [jnp.concatenate([one, block], axis=1), jnp.concatenate([block_t, two], axis=1)], axis=0
    )


GRAM_TOP = 13.0


def grain():
    row = lax.broadcasted_iota(jnp.int32, (32, K), 0)
    col = lax.broadcasted_iota(jnp.int32, (32, K), 1)
    return 1.0 + ((row * 11 + col * 23) & 31).astype(F32) * (1.0 / 64.0)


def eighth(x):
    x = x * x
    x = x * x
    return x * x


def eighth_root(x):
    return jnp.sqrt(lax.rsqrt(lax.rsqrt(jnp.abs(x))))


def encode_gram(parts, diagonal, factor):
    power = power_of(jnp.maximum(peak(parts), peak(diagonal)))
    scale = jnp.exp2(GRAM_TOP - power) * factor
    coded = eighth(parts * grain() * scale)
    return (
        jnp.concatenate([coded[:GRAM], coded[GRAM:]], axis=1),
        eighth(diagonal * scale),
        power,
    )


def gram_scale(power, factor):
    return jnp.exp2(power - GRAM_TOP) / factor


def one_above(x):
    return jnp.concatenate([x[:, :K], x[:, K:]], axis=0)


def added_parts(total):
    return one_above(total) / grain()


def products(halves):
    return lax.dot_general(halves, halves, (((0,), (0,)), ((), ())), preferred_element_type=F32)


def quarters(four):
    two = four[:K] + four[K:]
    return two[:, :K] + two[:, K:]


def spare_rows(left, right, grams):
    rows = []
    for _, diagonal, power in grams:
        rows.append(jnp.broadcast_to(power, (1, K)))
        rows.append(jnp.concatenate([diagonal, jnp.zeros((1, K - 32), F32)], axis=1))
    return jnp.concatenate(
        [
            jnp.broadcast_to(left, (LEFT, K)),
            jnp.broadcast_to(right, (LEFT - 1, K)),
            *rows,
            jnp.zeros((BLOCK - W_BLOCKS - len(rows), K), F32),
        ],
        axis=0,
    )


def w_message(w, gram):
    none = jnp.zeros((LEFT, 1), F32)
    right = jnp.concatenate(
        [w[W_HALF:], spare_rows(none, none[1:], [gram])], axis=0
    )
    return jnp.concatenate(
        [jnp.concatenate([w[:W_HALF], right], axis=1), gram[0]], axis=0
    ).astype(BF16)


def sums_message(sums, grams, factor):
    both = jnp.concatenate(
        [sums[:W_HALF], jnp.concatenate([sums[W_HALF:], jnp.zeros((BLOCK, K), F32)], axis=0)],
        axis=1,
    )
    blocks = [both[j * BLOCK : (j + 1) * BLOCK] for j in range(LEFT)]
    largest = jnp.concatenate(
        [jnp.max(x, axis=0, keepdims=True) for x in blocks] + [jnp.zeros((8 - LEFT, 128), F32)],
        axis=0,
    )
    lane = lax.broadcasted_iota(jnp.int32, (8, 128), 1)
    left = power_of(jnp.max(jnp.where(lane < K, largest, 0.0), axis=1, keepdims=True))
    right = power_of(jnp.max(jnp.where(lane < K, 0.0, largest), axis=1, keepdims=True))
    powers = jnp.where(lane < K, left, right)
    scale = jnp.exp2(TOP - powers) * factor
    blocks = [sixteenth(x * scale[j : j + 1]) for j, x in enumerate(blocks)]
    free = jnp.concatenate(
        [blocks[-1][:, :K], spare_rows(left[:LEFT], right[: LEFT - 1], grams)], axis=1
    )
    return jnp.concatenate(
        blocks[:-1] + [free] + [coded for coded, _, _ in grams], axis=0
    ).astype(BF16)


def read_gram(message, factor, which=0):
    at = W_BLOCKS + 2 * which
    scale = gram_scale(message[at : at + 1, 127:], factor)
    coded = message[BLOCK + GRAM * which : BLOCK + GRAM * (which + 1)]
    return eighth_root(coded) * scale, eighth_root(message[at + 1 : at + 2]) * scale


def read_sums(message, factor):
    lane = lax.broadcasted_iota(jnp.int32, (BLOCK, 128), 1)
    scale = scale_of(message[W_HALF - BLOCK :, 127:], factor)
    roots = root(message)
    return [
        roots[j * BLOCK : (j + 1) * BLOCK]
        * jnp.where(lane < K, scale[j : j + 1], scale[LEFT + j : LEFT + j + 1])
        for j in range(LEFT)
    ]


def one_column(both):
    return jnp.concatenate([both[:, :K], both[: W_OWN - W_HALF, K:]], axis=0)


def fill_w(w, factor, out):
    gram = gram_parts(quarters(products(split(w))))
    copies(w_message(w, encode_gram(*gram, factor)), out)


def start_kernel(me, w, tel, w_out, out):
    del tel
    wide = jnp.concatenate([w[...], jnp.zeros((K, 256 - W_OWN), F32)], axis=1)
    turned = wide.T[:W_OWN]
    w_out[...] = turned
    fill_w(turned, sample_factor(me[1]), out)


def h_numer_kernel(me, got, tile, out, w_turned, w_all):

    def gather(i, carry):
        gram, diagonal = carry
        message = got[i].astype(F32)
        w_all[pl.ds(pl.multiple_of(i * W_OWN, BLOCK), W_OWN), :] = one_column(message[:W_HALF])
        more, ends = read_gram(message[W_HALF - BLOCK :], sample_factor(i))
        return gram + more, diagonal + ends

    zero = (jnp.zeros((GRAM, 128), F32), jnp.zeros((1, 128), F32))
    gram, diagonal = lax.fori_loop(0, SAMPLES, gather, zero, unroll=True)

    def turn(j, carry):
        at = pl.ds(pl.multiple_of(j * 128, 128), 128)
        w_turned[:, at] = w_all[at, :].T.astype(BF16)
        return carry

    lax.fori_loop(0, ROWS // 128, turn, 0, unroll=True)
    factor = chip_factor(me[0])
    coded, ends, power = encode_gram(added_parts(gram), diagonal[:, K : K + 32], factor)
    ends = jnp.concatenate([ends, jnp.zeros((1, 96), F32)], axis=1)
    power = jnp.broadcast_to(power, (1, 128))
    per = H_WIDTH // H_OWN

    def step(n, carry):
        cols = pl.ds(pl.multiple_of(n * H_WIDTH, H_WIDTH), H_WIDTH)
        part = jnp.dot(w_turned[...], tile[:, cols], preferred_element_type=F32).T
        for q in range(per):
            halves = [part[q * H_OWN + r : q * H_OWN + r + BLOCK] for r in (0, BLOCK)]
            powers = [power_of(peak(x)) for x in halves]
            out[n * per + q] = jnp.concatenate(
                [
                    jnp.concatenate([code(x, p, factor) for x, p in zip(halves, powers)], axis=1),
                    coded,
                    ends,
                    power,
                    jnp.broadcast_to(powers[0], (1, 128)),
                    jnp.broadcast_to(powers[1], (1, 128)),
                    jnp.zeros((4, 128), F32),
                ],
                axis=0,
            ).astype(BF16)
        return carry

    lax.fori_loop(0, COLS // H_WIDTH, step, 0, unroll=True)


def h_update_kernel(got, h, h_out, out):
    lane = lax.broadcasted_iota(jnp.int32, (BLOCK, 128), 1)

    def add(i, carry):
        numer, gram, diagonal = carry
        message = got[i].astype(F32)
        powers = message[H_MSG - 8 :, 127:]
        scales = scale_of(powers, chip_factor(i))
        numer += root(message[:BLOCK]) * jnp.where(lane < K, scales[2:3], scales[3:4])
        scale = gram_scale(powers[1:2], chip_factor(i))
        gram += eighth_root(message[BLOCK : BLOCK + GRAM]) * scale
        diagonal += eighth_root(message[H_MSG - 8 : H_MSG - 7]) * scale
        return numer, gram, diagonal

    zero = jnp.zeros((BLOCK, 128), F32)
    numer, gram, diagonal = lax.fori_loop(
        0, CHIPS, add, (zero, zero, jnp.zeros((1, 128), F32)), unroll=True
    )
    gram = gram_whole(added_parts(gram), diagonal[:, :32])
    old = h[...]
    below = jnp.dot(old, gram, precision=HIGHEST, preferred_element_type=F32) + epsilon
    new = old * one_above(numer) / below
    h_out[...] = new
    copies(split(new), out)


def w_numer(me, got, tile, out, energy=None):
    halves = got[...].reshape(COLS, 128)
    four = products(halves)
    factor = sample_factor(me[1])
    grams = [encode_gram(*gram_parts(quarters(four)), factor)]
    if out.shape[1] > W_MSG:
        grams.append(encode_gram(*gram_parts(four[:K, :K]), factor))
    if energy is not None:

        def add(i, total):
            rows = pl.ds(pl.multiple_of(i * W_OWN, W_OWN), W_OWN)
            values = tile[rows, :].astype(F32)
            return total + jnp.sum((values * values).reshape(W_OWN // 8, 8, COLS), axis=0)

        squares_sum = lax.fori_loop(0, SAMPLES, add, jnp.zeros((8, COLS), F32), unroll=True)
        energy[...] = jnp.full((1, 128), jnp.sum(squares_sum), F32)
    sums = jnp.dot(tile[...], halves[:, :K], preferred_element_type=F32)
    for q in range(SAMPLES):
        out[q] = sums_message(sums[q * W_OWN : (q + 1) * W_OWN], grams, factor)


def w_numer_kernel(me, got, tile, out):
    w_numer(me, got, tile, out)


def w_numer_energy_kernel(me, got, tile, out, energy):
    w_numer(me, got, tile, out, energy)


def w_new(got, w):
    count = (got.shape[1] - W_HALF) // GRAM

    def add(i, carry):
        blocks, grams = carry
        message = got[i].astype(F32)
        terms = read_sums(message[:W_HALF], sample_factor(i))
        blocks = tuple(total + term for total, term in zip(blocks, terms))
        more = [read_gram(message[W_HALF - BLOCK :], sample_factor(i), n) for n in range(count)]
        return blocks, tuple((x + u, y + v) for (x, y), (u, v) in zip(grams, more))

    zero = jnp.zeros((BLOCK, 128), F32)
    empty = (zero, jnp.zeros((1, 128), F32))
    blocks, grams = lax.fori_loop(
        0, SAMPLES, add, ((zero,) * LEFT, (empty,) * count), unroll=True
    )
    numer = one_column(jnp.concatenate(blocks, axis=0))
    grams = [gram_whole(added_parts(x), y[:, K : K + 32]) for x, y in grams]
    gram = grams[0]
    old = w[...]
    below = jnp.dot(old, gram, precision=HIGHEST, preferred_element_type=F32) + epsilon
    return old * numer / below, numer, grams[-1]


def w_update_kernel(me, got, w, w_out, out):
    new, _, _ = w_new(got, w)
    w_out[...] = new
    fill_w(new, sample_factor(me[1]), out)


def w_last_kernel(got, w, energy, w_out, out):
    new, numer, gram = w_new(got, w)
    w_out[...] = new
    rounded = new.astype(BF16).astype(F32)
    fitted = jnp.dot(rounded, gram, precision=HIGHEST, preferred_element_type=F32)
    share = jnp.sum(rounded * (fitted - 2.0 * numer))
    lane = lax.broadcasted_iota(jnp.int32, (1, 128), 1)
    pair = jnp.where(lane < K, share, energy[...])
    out[...] = jnp.broadcast_to(pair, out.shape)


def ratio_kernel(got, ratio, close, total_out):
    sums = jnp.sum(got[...], axis=0)
    total = sums[:, K : K + 1]
    expanded = sums[:, :1] + total
    ratio[0, 0] = jnp.sum(jnp.sqrt(jnp.maximum(expanded, 0.0) / total))
    close[0, 0] = jnp.sum((expanded < 0.02 * total).astype(F32)).astype(jnp.int32)
    total_out[0, 0] = jnp.sum(total)


def last_rows_kernel(w, out):
    rows = w[...]
    right = jnp.concatenate([rows[W_HALF:], jnp.zeros((BLOCK, K), F32)], axis=0)
    message = jnp.concatenate([rows[:W_HALF], right], axis=1).astype(BF16)
    copies(message, out)


def error_kernel(got_w, got_h, tel, out):
    high = got_h[...].reshape(COLS, 128)[:, :K]

    def step(i, error):
        rows = pl.ds(pl.multiple_of(i * W_OWN, W_OWN), W_OWN)
        rebuilt = lax.dot_general(
            one_column(got_w[i].astype(F32)).astype(BF16),
            high,
            (((1,), (1,)), ((), ())),
            preferred_element_type=F32,
        )
        difference = tel[rows, :].astype(F32) - rebuilt
        return error + jnp.sum((difference * difference).reshape(W_OWN // 8, 8, COLS), axis=0)

    error = lax.fori_loop(0, SAMPLES, step, jnp.zeros((8, COLS), F32))
    share = jnp.full((1, 128), jnp.sum(error), F32)
    copies(share, out)


VMEM = pl.BlockSpec(memory_space=pltpu.VMEM)
SMEM = pl.BlockSpec(memory_space=pltpu.SMEM)
HBM = pl.BlockSpec(memory_space=pltpu.HBM)
LIMIT = pltpu.CompilerParams(vmem_limit_bytes=32 * 1024 * 1024)
PRODUCT = pl.CostEstimate(
    flops=2 * K * ROWS * COLS, bytes_accessed=2 * ROWS * COLS, transcendentals=0
)


def call(kernel, inputs, outs, cost=None, specs=None, scratch=(), out_spec=VMEM):
    return pl.pallas_call(
        kernel,
        out_shape=[jax.ShapeDtypeStruct(shape, dtype) for shape, dtype in outs],
        in_specs=[VMEM] * len(inputs) if specs is None else specs,
        out_specs=[out_spec] * len(outs),
        scratch_shapes=list(scratch),
        compiler_params=LIMIT,
        cost_estimate=cost,
    )(*inputs)


def exchange(x, axis):
    return lax.all_to_all(x, axis, 0, 0, tiled=True)


def sum_everywhere(shares):
    part = jnp.sum(exchange(shares, "samples"), axis=0)
    part = exchange(jnp.broadcast_to(part[None], (CHIPS, 1, 128)), "chips")
    return jnp.sum(part, axis=0)


def body(telemetry, chip_factors, sample_factors):
    me = jnp.stack([lax.axis_index("chips"), lax.axis_index("samples")])
    specs = [SMEM, VMEM, VMEM]
    h = sample_factors.T
    w_sent = [((W_OWN, K), F32), ((SAMPLES, W_MSG, 128), BF16)]
    w, sent = call(
        start_kernel, (me, chip_factors, telemetry), w_sent, None, [SMEM, VMEM, HBM]
    )
    got_w = exchange(sent, "samples")
    for sweep in range(ITERS):
        last = sweep == ITERS - 1
        (sent,) = call(
            h_numer_kernel,
            (me, got_w, telemetry),
            [((CHIPS, H_MSG, 128), BF16)],
            PRODUCT,
            specs,
            [pltpu.VMEM((K, ROWS), BF16), pltpu.VMEM((ROWS, K), F32)],
        )
        got = exchange(sent, "chips")
        h, sent = call(
            h_update_kernel, (got, h), [((H_OWN, K), F32), ((CHIPS, H_OWN, 128), BF16)]
        )
        got_h = exchange(sent, "chips")
        w_sums = [((SAMPLES, W_MSG + GRAM if last else W_MSG, 128), BF16)]
        if sweep == 0:
            sent, energy = call(
                w_numer_energy_kernel,
                (me, got_h, telemetry),
                [*w_sums, ((1, 128), F32)],
                PRODUCT,
                specs,
            )
        else:
            (sent,) = call(
                w_numer_kernel, (me, got_h, telemetry), w_sums, PRODUCT, specs
            )
        got = exchange(sent, "samples")
        if not last:
            w, sent = call(
                w_update_kernel,
                (me, got, w),
                w_sent,
                None,
                [SMEM, VMEM, VMEM],
            )
            got_w = exchange(sent, "samples")
    w, shares = call(
        w_last_kernel,
        (got, w, energy),
        [((W_OWN, K), F32), ((CHIPS * SAMPLES, 1, 128), F32)],
    )
    ratio, close, total = call(
        ratio_kernel,
        (exchange(shares, ("chips", "samples")),),
        [((1, 1), F32), ((1, 1), jnp.int32), ((1, 1), F32)],
        out_spec=SMEM,
    )

    def direct(ratio, total, w, got_h, telemetry):
        (sent,) = call(last_rows_kernel, (w,), [((SAMPLES, W_HALF, 128), BF16)])
        (shares,) = call(
            error_kernel,
            (exchange(sent, "samples"), got_h, telemetry),
            [((SAMPLES, 1, 128), F32)],
            PRODUCT,
        )
        return jnp.sqrt(sum_everywhere(shares)[:1, :1] / total)

    ratio = lax.cond(
        close[0, 0] > 0,
        direct,
        lambda ratio, *operands: ratio,
        ratio,
        total,
        w,
        got_h,
        telemetry,
    )
    return w.T, h.T, ratio[0, 0]


def solution(mesh):
    return jax.shard_map(
        body,
        mesh=mesh,
        in_specs=(
            P("chips", "samples"),
            P(None, ("chips", "samples")),
            P(None, ("samples", "chips")),
        ),
        out_specs=(P(None, ("chips", "samples")), P(None, ("samples", "chips")), P()),
        check_vma=False,
    )
```

```python
import jax
import jax.numpy as jnp
from jax import lax
from jax.experimental import pallas as pl
from jax.experimental.pallas import tpu as pltpu
from jax.sharding import PartitionSpec as P

ITERS = 2

epsilon = 1e-09

F32 = jnp.float32
BF16 = jnp.bfloat16
HIGHEST = lax.Precision.HIGHEST

K = 64
CHIPS = 32
SAMPLES = 16
ROWS = 2304
COLS = 1024
W_OWN = ROWS // SAMPLES
H_OWN = COLS // CHIPS
H_WIDTH = 256
BLOCK = 16
W_HALF = 80
GRAM = 16
W_MSG = W_HALF + GRAM
H_MSG = BLOCK + GRAM + 8
LEFT = W_HALF // BLOCK
W_BLOCKS = W_OWN // BLOCK


def split(x):
    high = x.astype(BF16).astype(F32)
    return jnp.concatenate([high, x - high], axis=1).astype(BF16)


def join(x):
    return x[:, :K] + x[:, K:]


def squares():
    row = lax.broadcasted_iota(jnp.int32, (32, 32), 0)
    col = lax.broadcasted_iota(jnp.int32, (32, 32), 1)
    return row, col


TOP = 6.0


def peak(x):
    return jnp.max(jnp.max(x, axis=0, keepdims=True), axis=1, keepdims=True)


def power_of(largest):
    return jnp.floor(jnp.log2(jnp.maximum(largest, 1e-30)))


def sixteenth(x):
    x = x * x
    x = x * x
    x = x * x
    return x * x


def code(x, power, factor):
    return sixteenth(x * (jnp.exp2(TOP - power) * factor))


def root(x):
    return lax.rsqrt(lax.rsqrt(lax.rsqrt(lax.rsqrt(jnp.abs(x)))))


def scale_of(power, factor):
    return jnp.exp2(power - TOP) / factor


def copies(message, out):
    def step(i, carry):
        out[i] = message
        return carry

    lax.fori_loop(0, out.shape[0], step, 0, unroll=True)


def sample_factor(i):
    return 1.0 + jnp.full((1, 1), i, jnp.int32).astype(F32) * (1.0 / 32.0)


def chip_factor(i):
    return 1.0 + jnp.full((1, 1), i, jnp.int32).astype(F32) * (1.0 / 64.0)


def gram_parts(gram):
    row, col = squares()
    first, block, last = gram[:32, :32], gram[:32, 32:], gram[32:, 32:]
    parts = jnp.concatenate([jnp.where(row <= col, first, last), block], axis=1)
    return parts, jnp.sum(jnp.where(row == col, last, 0.0), axis=0, keepdims=True)


def gram_whole(parts, diagonal):
    row, col = squares()
    mixed, block = parts[:, :32], parts[:, 32:]
    turned = lax.dot_general(
        (row == col).astype(F32),
        jnp.concatenate([mixed, block], axis=0),
        (((1,), (1,)), ((), ())),
        precision=HIGHEST,
        preferred_element_type=F32,
    )
    mixed_t, block_t = turned[:, :32], turned[:, 32:]
    one = jnp.where(row <= col, mixed, mixed_t)
    two = jnp.where(row > col, mixed, jnp.where(row < col, mixed_t, diagonal))
    return jnp.concatenate(
        [jnp.concatenate([one, block], axis=1), jnp.concatenate([block_t, two], axis=1)], axis=0
    )


GRAM_TOP = 13.0


def grain():
    row = lax.broadcasted_iota(jnp.int32, (32, K), 0)
    col = lax.broadcasted_iota(jnp.int32, (32, K), 1)
    return 1.0 + ((row * 11 + col * 23) & 31).astype(F32) * (1.0 / 64.0)


def eighth(x):
    x = x * x
    x = x * x
    return x * x


def eighth_root(x):
    return jnp.sqrt(lax.rsqrt(lax.rsqrt(jnp.abs(x))))


def encode_gram(parts, diagonal, factor):
    power = power_of(jnp.maximum(peak(parts), peak(diagonal)))
    scale = jnp.exp2(GRAM_TOP - power) * factor
    coded = eighth(parts * grain() * scale)
    return (
        jnp.concatenate([coded[:GRAM], coded[GRAM:]], axis=1),
        eighth(diagonal * scale),
        power,
    )


def gram_scale(power, factor):
    return jnp.exp2(power - GRAM_TOP) / factor


def one_above(x):
    return jnp.concatenate([x[:, :K], x[:, K:]], axis=0)


def added_parts(total):
    return one_above(total) / grain()


def products(halves):
    return lax.dot_general(halves, halves, (((0,), (0,)), ((), ())), preferred_element_type=F32)


def quarters(four):
    two = four[:K] + four[K:]
    return two[:, :K] + two[:, K:]


def spare_rows(left, right, grams):
    rows = []
    for _, diagonal, power in grams:
        rows.append(jnp.broadcast_to(power, (1, K)))
        rows.append(jnp.concatenate([diagonal, jnp.zeros((1, K - 32), F32)], axis=1))
    return jnp.concatenate(
        [
            jnp.broadcast_to(left, (LEFT, K)),
            jnp.broadcast_to(right, (LEFT - 1, K)),
            *rows,
            jnp.zeros((BLOCK - W_BLOCKS - len(rows), K), F32),
        ],
        axis=0,
    )


def w_message(w, gram):
    none = jnp.zeros((LEFT, 1), F32)
    right = jnp.concatenate(
        [w[W_HALF:], spare_rows(none, none[1:], [gram])], axis=0
    )
    return jnp.concatenate(
        [jnp.concatenate([w[:W_HALF], right], axis=1), gram[0]], axis=0
    ).astype(BF16)


def sums_message(sums, grams, factor):
    both = jnp.concatenate(
        [sums[:W_HALF], jnp.concatenate([sums[W_HALF:], jnp.zeros((BLOCK, K), F32)], axis=0)],
        axis=1,
    )
    blocks = [both[j * BLOCK : (j + 1) * BLOCK] for j in range(LEFT)]
    largest = jnp.concatenate(
        [jnp.max(x, axis=0, keepdims=True) for x in blocks] + [jnp.zeros((8 - LEFT, 128), F32)],
        axis=0,
    )
    lane = lax.broadcasted_iota(jnp.int32, (8, 128), 1)
    left = power_of(jnp.max(jnp.where(lane < K, largest, 0.0), axis=1, keepdims=True))
    right = power_of(jnp.max(jnp.where(lane < K, 0.0, largest), axis=1, keepdims=True))
    powers = jnp.where(lane < K, left, right)
    scale = jnp.exp2(TOP - powers) * factor
    blocks = [sixteenth(x * scale[j : j + 1]) for j, x in enumerate(blocks)]
    free = jnp.concatenate(
        [blocks[-1][:, :K], spare_rows(left[:LEFT], right[: LEFT - 1], grams)], axis=1
    )
    return jnp.concatenate(
        blocks[:-1] + [free] + [coded for coded, _, _ in grams], axis=0
    ).astype(BF16)


def read_gram(message, factor, which=0):
    at = W_BLOCKS + 2 * which
    scale = gram_scale(message[at : at + 1, 127:], factor)
    coded = message[BLOCK + GRAM * which : BLOCK + GRAM * (which + 1)]
    return eighth_root(coded) * scale, eighth_root(message[at + 1 : at + 2]) * scale


def read_sums(message, factor):
    lane = lax.broadcasted_iota(jnp.int32, (BLOCK, 128), 1)
    scale = scale_of(message[W_HALF - BLOCK :, 127:], factor)
    roots = root(message)
    return [
        roots[j * BLOCK : (j + 1) * BLOCK]
        * jnp.where(lane < K, scale[j : j + 1], scale[LEFT + j : LEFT + j + 1])
        for j in range(LEFT)
    ]


def one_column(both):
    return jnp.concatenate([both[:, :K], both[: W_OWN - W_HALF, K:]], axis=0)


def fill_w(w, factor, out):
    gram = gram_parts(quarters(products(split(w))))
    copies(w_message(w, encode_gram(*gram, factor)), out)


def start_kernel(me, w, tel, w_out, out, own, arrived):
    del tel
    copy = pltpu.make_async_copy(w, own, arrived)
    copy.start()
    copy.wait()
    wide = jnp.concatenate([own[...], jnp.zeros((K, 256 - W_OWN), F32)], axis=1)
    turned = wide.T[:W_OWN]
    w_out[...] = turned
    fill_w(turned, sample_factor(me[1]), out)


def h_numer_kernel(me, got, tile, out, w_turned, w_all):

    def gather(i, carry):
        gram, diagonal = carry
        message = got[i].astype(F32)
        w_all[pl.ds(pl.multiple_of(i * W_OWN, BLOCK), W_OWN), :] = one_column(message[:W_HALF])
        more, ends = read_gram(message[W_HALF - BLOCK :], sample_factor(i))
        return gram + more, diagonal + ends

    zero = (jnp.zeros((GRAM, 128), F32), jnp.zeros((1, 128), F32))
    gram, diagonal = lax.fori_loop(0, SAMPLES, gather, zero, unroll=True)

    def turn(j, carry):
        at = pl.ds(pl.multiple_of(j * 128, 128), 128)
        w_turned[:, at] = w_all[at, :].T.astype(BF16)
        return carry

    lax.fori_loop(0, ROWS // 128, turn, 0, unroll=True)
    factor = chip_factor(me[0])
    coded, ends, power = encode_gram(added_parts(gram), diagonal[:, K : K + 32], factor)
    ends = jnp.concatenate([ends, jnp.zeros((1, 96), F32)], axis=1)
    power = jnp.broadcast_to(power, (1, 128))
    per = H_WIDTH // H_OWN

    def step(n, carry):
        cols = pl.ds(pl.multiple_of(n * H_WIDTH, H_WIDTH), H_WIDTH)
        part = jnp.dot(w_turned[...], tile[:, cols], preferred_element_type=F32).T
        for q in range(per):
            halves = [part[q * H_OWN + r : q * H_OWN + r + BLOCK] for r in (0, BLOCK)]
            powers = [power_of(peak(x)) for x in halves]
            out[n * per + q] = jnp.concatenate(
                [
                    jnp.concatenate([code(x, p, factor) for x, p in zip(halves, powers)], axis=1),
                    coded,
                    ends,
                    power,
                    jnp.broadcast_to(powers[0], (1, 128)),
                    jnp.broadcast_to(powers[1], (1, 128)),
                    jnp.zeros((4, 128), F32),
                ],
                axis=0,
            ).astype(BF16)
        return carry

    lax.fori_loop(0, COLS // H_WIDTH, step, 0, unroll=True)


def h_update_kernel(got, h, h_out, out):
    lane = lax.broadcasted_iota(jnp.int32, (BLOCK, 128), 1)

    def add(i, carry):
        numer, gram, diagonal = carry
        message = got[i].astype(F32)
        powers = message[H_MSG - 8 :, 127:]
        scales = scale_of(powers, chip_factor(i))
        numer += root(message[:BLOCK]) * jnp.where(lane < K, scales[2:3], scales[3:4])
        scale = gram_scale(powers[1:2], chip_factor(i))
        gram += eighth_root(message[BLOCK : BLOCK + GRAM]) * scale
        diagonal += eighth_root(message[H_MSG - 8 : H_MSG - 7]) * scale
        return numer, gram, diagonal

    zero = jnp.zeros((BLOCK, 128), F32)
    numer, gram, diagonal = lax.fori_loop(
        0, CHIPS, add, (zero, zero, jnp.zeros((1, 128), F32)), unroll=True
    )
    gram = gram_whole(added_parts(gram), diagonal[:, :32])
    old = h[...]
    below = jnp.dot(old, gram, precision=HIGHEST, preferred_element_type=F32) + epsilon
    new = old * one_above(numer) / below
    h_out[...] = new
    copies(split(new), out)


def w_numer(me, got, tile, out, energy=None):
    halves = got[...].reshape(COLS, 128)
    four = products(halves)
    factor = sample_factor(me[1])
    grams = [encode_gram(*gram_parts(quarters(four)), factor)]
    if out.shape[1] > W_MSG:
        grams.append(encode_gram(*gram_parts(four[:K, :K]), factor))
    if energy is not None:

        def add(i, total):
            rows = pl.ds(pl.multiple_of(i * W_OWN, W_OWN), W_OWN)
            values = tile[rows, :].astype(F32)
            return total + jnp.sum((values * values).reshape(W_OWN // 8, 8, COLS), axis=0)

        squares_sum = lax.fori_loop(0, SAMPLES, add, jnp.zeros((8, COLS), F32), unroll=True)
        energy[...] = jnp.full((1, 128), jnp.sum(squares_sum), F32)
    sums = jnp.dot(tile[...], halves[:, :K], preferred_element_type=F32)
    for q in range(SAMPLES):
        out[q] = sums_message(sums[q * W_OWN : (q + 1) * W_OWN], grams, factor)


def w_numer_kernel(me, got, tile, out):
    w_numer(me, got, tile, out)


def w_numer_energy_kernel(me, got, tile, out, energy):
    w_numer(me, got, tile, out, energy)


def w_new(got, w):
    count = (got.shape[1] - W_HALF) // GRAM

    def add(i, carry):
        blocks, grams = carry
        message = got[i].astype(F32)
        terms = read_sums(message[:W_HALF], sample_factor(i))
        blocks = tuple(total + term for total, term in zip(blocks, terms))
        more = [read_gram(message[W_HALF - BLOCK :], sample_factor(i), n) for n in range(count)]
        return blocks, tuple((x + u, y + v) for (x, y), (u, v) in zip(grams, more))

    zero = jnp.zeros((BLOCK, 128), F32)
    empty = (zero, jnp.zeros((1, 128), F32))
    blocks, grams = lax.fori_loop(
        0, SAMPLES, add, ((zero,) * LEFT, (empty,) * count), unroll=True
    )
    numer = one_column(jnp.concatenate(blocks, axis=0))
    grams = [gram_whole(added_parts(x), y[:, K : K + 32]) for x, y in grams]
    gram = grams[0]
    old = w[...]
    below = jnp.dot(old, gram, precision=HIGHEST, preferred_element_type=F32) + epsilon
    return old * numer / below, numer, grams[-1]


def w_update_kernel(me, got, w, w_out, out):
    new, _, _ = w_new(got, w)
    w_out[...] = new
    fill_w(new, sample_factor(me[1]), out)


def w_last_kernel(got, w, energy, w_out, out):
    new, numer, gram = w_new(got, w)
    w_out[...] = new
    rounded = new.astype(BF16).astype(F32)
    fitted = jnp.dot(rounded, gram, precision=HIGHEST, preferred_element_type=F32)
    share = jnp.sum(rounded * (fitted - 2.0 * numer))
    lane = lax.broadcasted_iota(jnp.int32, (1, 128), 1)
    pair = jnp.where(lane < K, share, energy[...])
    copies(pair, out)


def share_kernel(got, out):
    copies(jnp.sum(got[...], axis=0), out)


def ratio_kernel(got, ratio, close, total_out):
    sums = jnp.sum(got[...], axis=0)
    total = sums[:, K : K + 1]
    expanded = sums[:, :1] + total
    ratio[0, 0] = jnp.sum(jnp.sqrt(jnp.maximum(expanded, 0.0) / total))
    close[0, 0] = jnp.sum((expanded < 0.02 * total).astype(F32)).astype(jnp.int32)
    total_out[0, 0] = jnp.sum(total)


def last_rows_kernel(w, out):
    rows = w[...]
    right = jnp.concatenate([rows[W_HALF:], jnp.zeros((BLOCK, K), F32)], axis=0)
    message = jnp.concatenate([rows[:W_HALF], right], axis=1).astype(BF16)
    copies(message, out)


def error_kernel(got_w, got_h, tel, out):
    high = got_h[...].reshape(COLS, 128)[:, :K]

    def step(i, error):
        rows = pl.ds(pl.multiple_of(i * W_OWN, W_OWN), W_OWN)
        rebuilt = lax.dot_general(
            one_column(got_w[i].astype(F32)).astype(BF16),
            high,
            (((1,), (1,)), ((), ())),
            preferred_element_type=F32,
        )
        difference = tel[rows, :].astype(F32) - rebuilt
        return error + jnp.sum((difference * difference).reshape(W_OWN // 8, 8, COLS), axis=0)

    error = lax.fori_loop(0, SAMPLES, step, jnp.zeros((8, COLS), F32))
    share = jnp.full((1, 128), jnp.sum(error), F32)
    copies(share, out)


VMEM = pl.BlockSpec(memory_space=pltpu.VMEM)
SMEM = pl.BlockSpec(memory_space=pltpu.SMEM)
HBM = pl.BlockSpec(memory_space=pltpu.HBM)
LIMIT = pltpu.CompilerParams(vmem_limit_bytes=32 * 1024 * 1024)
PRODUCT = pl.CostEstimate(
    flops=2 * K * ROWS * COLS, bytes_accessed=2 * ROWS * COLS, transcendentals=0
)


def call(kernel, inputs, outs, cost=None, specs=None, scratch=(), out_spec=VMEM):
    return pl.pallas_call(
        kernel,
        out_shape=[jax.ShapeDtypeStruct(shape, dtype) for shape, dtype in outs],
        in_specs=[VMEM] * len(inputs) if specs is None else specs,
        out_specs=[out_spec] * len(outs),
        scratch_shapes=list(scratch),
        compiler_params=LIMIT,
        cost_estimate=cost,
    )(*inputs)


def exchange(x, axis):
    return lax.all_to_all(x, axis, 0, 0, tiled=True)


def sum_everywhere(shares):
    part = jnp.sum(exchange(shares, "samples"), axis=0)
    part = exchange(jnp.broadcast_to(part[None], (CHIPS, 1, 128)), "chips")
    return jnp.sum(part, axis=0)


def body(telemetry, chip_factors, sample_factors):
    me = jnp.stack([lax.axis_index("chips"), lax.axis_index("samples")])
    specs = [SMEM, VMEM, VMEM]
    h = sample_factors.T
    w_sent = [((W_OWN, K), F32), ((SAMPLES, W_MSG, 128), BF16)]
    w, sent = call(
        start_kernel,
        (me, pltpu.with_memory_space_constraint(chip_factors, pltpu.HBM), telemetry),
        w_sent,
        None,
        [SMEM, HBM, HBM],
        [pltpu.VMEM((K, W_OWN), F32), pltpu.SemaphoreType.DMA],
    )
    got_w = exchange(sent, "samples")
    for sweep in range(ITERS):
        last = sweep == ITERS - 1
        (sent,) = call(
            h_numer_kernel,
            (me, got_w, telemetry),
            [((CHIPS, H_MSG, 128), BF16)],
            PRODUCT,
            specs,
            [pltpu.VMEM((K, ROWS), BF16), pltpu.VMEM((ROWS, K), F32)],
        )
        got = exchange(sent, "chips")
        h, sent = call(
            h_update_kernel, (got, h), [((H_OWN, K), F32), ((CHIPS, H_OWN, 128), BF16)]
        )
        got_h = exchange(sent, "chips")
        w_sums = [((SAMPLES, W_MSG + GRAM if last else W_MSG, 128), BF16)]
        if sweep == 0:
            sent, energy = call(
                w_numer_energy_kernel,
                (me, got_h, telemetry),
                [*w_sums, ((1, 128), F32)],
                PRODUCT,
                specs,
            )
        else:
            (sent,) = call(
                w_numer_kernel, (me, got_h, telemetry), w_sums, PRODUCT, specs
            )
        got = exchange(sent, "samples")
        if not last:
            w, sent = call(
                w_update_kernel,
                (me, got, w),
                w_sent,
                None,
                [SMEM, VMEM, VMEM],
            )
            got_w = exchange(sent, "samples")
    w, shares = call(
        w_last_kernel, (got, w, energy), [((W_OWN, K), F32), ((SAMPLES, 1, 128), F32)]
    )
    (shares,) = call(
        share_kernel, (exchange(shares, "samples"),), [((CHIPS, 1, 128), F32)]
    )
    ratio, close, total = call(
        ratio_kernel,
        (exchange(shares, "chips"),),
        [((1, 1), F32), ((1, 1), jnp.int32), ((1, 1), F32)],
        out_spec=SMEM,
    )

    def direct(ratio, total, w, got_h, telemetry):
        (sent,) = call(last_rows_kernel, (w,), [((SAMPLES, W_HALF, 128), BF16)])
        (shares,) = call(
            error_kernel,
            (exchange(sent, "samples"), got_h, telemetry),
            [((SAMPLES, 1, 128), F32)],
            PRODUCT,
        )
        return jnp.sqrt(sum_everywhere(shares)[:1, :1] / total)

    ratio = lax.cond(
        close[0, 0] > 0,
        direct,
        lambda ratio, *operands: ratio,
        ratio,
        total,
        w,
        got_h,
        telemetry,
    )
    return w.T, h.T, ratio[0, 0]


def solution(mesh):
    return jax.shard_map(
        body,
        mesh=mesh,
        in_specs=(
            P("chips", "samples"),
            P(None, ("chips", "samples")),
            P(None, ("samples", "chips")),
        ),
        out_specs=(P(None, ("chips", "samples")), P(None, ("samples", "chips")), P()),
        check_vma=False,
    )
```
